32 devices in a mesh: slot: 8 (over y, x, core), seq: 4 (over z).
Axes of the slice: x: 2, y: 2, z: 4, core: 2. Of those that a mesh axis runs over, the one named last changes fastest.
Arguments:
- patches: bfloat16 [8, 1536, 768], P('slot', 'seq'), may hold values from -6 to 6
- segments: int32 [8, 1536], P('slot'), may hold values from 0 to 2, as said below
- code_bits: int32 [8, 1536, 18], P('slot', 'seq'), may hold values from 0 to 1
- norm_gain: bfloat16 [2, 2, 768], P(None, None, ('slot', 'seq')), may hold values from 0.5 to 1.5
- norm_shift: bfloat16 [2, 2, 768], P(None, None, ('slot', 'seq')), may hold values from -1.1953125 to 1.1953125
- project_weight: bfloat16 [2, 768, 2304], P(None, ('slot', 'seq')), may hold values from -0.3125 to 0.3125
- query_value_bias: bfloat16 [2, 2, 768], P(None, None, ('slot', 'seq')), may hold values from -1.1953125 to 1.1953125
- output_weight: bfloat16 [2, 768, 768], P(None, ('slot', 'seq')), may hold values from -0.625 to 0.625
- output_bias: bfloat16 [2, 768], P(None, ('slot', 'seq')), may hold values from -1.1953125 to 1.1953125
- expand_weight: bfloat16 [2, 768, 3072], P(None, ('slot', 'seq')), may hold values from -0.21875 to 0.21875
- expand_bias: bfloat16 [2, 3072], P(None, ('slot', 'seq')), may hold values from -1.1953125 to 1.1953125
- shrink_weight: bfloat16 [2, 3072, 768], P(None, ('slot', 'seq')), may hold values from -0.109375 to 0.109375
- shrink_bias: bfloat16 [2, 768], P(None, ('slot', 'seq')), may hold values from -1.1953125 to 1.1953125
- encode_weight: bfloat16 [768, 18], P(('slot', 'seq')), may hold values from -0.21875 to 0.21875
- decode_weight: bfloat16 [18, 768], P(None, ('slot', 'seq')), may hold values from -6 to 6
- decode_bias: bfloat16 [768], P(('slot', 'seq')), may hold values from -1.1953125 to 1.1953125
- cotangent: bfloat16 [8, 1536, 768], P('slot', 'seq'), may hold values from -6 to 6
Outputs:
- decoded: bfloat16 [8, 1536, 768], P('slot', 'seq')
- input_grad: float32 [8, 1536, 768], P('slot', 'seq')
- norm_gain_grad: float32 [2, 2, 768], P(None, None, ('slot', 'seq'))
- norm_shift_grad: float32 [2, 2, 768], P(None, None, ('slot', 'seq'))
- project_grad: float32 [2, 768, 2304], P(None, ('slot', 'seq'))
- query_value_grad: float32 [2, 2, 768], P(None, None, ('slot', 'seq'))
- output_weight_grad: float32 [2, 768, 768], P(None, ('slot', 'seq'))
- output_bias_grad: float32 [2, 768], P(None, ('slot', 'seq'))
- expand_weight_grad: float32 [2, 768, 3072], P(None, ('slot', 'seq'))
- expand_bias_grad: float32 [2, 3072], P(None, ('slot', 'seq'))
- shrink_weight_grad: float32 [2, 3072, 768], P(None, ('slot', 'seq'))
- shrink_bias_grad: float32 [2, 768], P(None, ('slot', 'seq'))
- encode_grad: float32 [768, 18], P(('slot', 'seq'))
- decode_grad: float32 [18, 768], P(None, ('slot', 'seq'))
- decode_bias_grad: float32 [768], P(('slot', 'seq'))
The draws below stay inside these ranges and needn't reach their ends.
Inputs may be any that keep to these rules, and one draw needn't show every extreme that they name: `segments`: each slot holds three items numbered 0, 1, 2 in order of position; item 1 is 1024 patches long, begins within the first quarter of the slot and ends within the last quarter; items 0 and 2 are not empty.
All inputs are finite; a program needn't handle non-finite values.
Results may differ from the reference program's by a relative error of at most 0.02.
Values may be sent and summed in bfloat16 or wider, within the bound.
A program may use at most 256 MiB of HBM per device.

```python
import jax
import jax.numpy as jnp
from jax import lax

D = 768
H = 12
HD = 64
FF = 3072
CODE = 18
SLOT_LEN = 1536
SLOTS = 8
LONG = 1024


def draw_segments(key, part):
    key = jax.random.fold_in(key, 7)
    lowest = 3 * SLOT_LEN // 4 - LONG + 1
    first = jax.random.randint(key, (SLOTS, 1), lowest, SLOT_LEN // 4).astype(jnp.int32)
    position = jnp.arange(SLOT_LEN, dtype=jnp.int32)[None, :]
    return (position >= first).astype(jnp.int32) + (position >= first + LONG).astype(jnp.int32)


def set_ends(result, rng, smallest, high):
    shape = result.shape
    place = [jax.random.randint(jax.random.fold_in(rng, axis), (), 0, shape[axis]) for axis in range(len(shape))]
    result = result.at[tuple(place)].set(smallest)
    longest = shape.index(max(shape))
    place[longest] = (place[longest] + 1) % shape[longest]
    return result.at[tuple(place)].set(high)


def steps_of(stream_key, shape, cuts, smallest, high):
    def one(dim, parts):
        draws = jax.random.uniform(jax.random.fold_in(jax.random.fold_in(stream_key, 6), dim), (parts,), jnp.float32, smallest / len(cuts), high / len(cuts))
        return jnp.repeat(jnp.exp(draws), shape[dim] // parts).reshape((-1,) + (1,) * (len(shape) - dim - 1))

    gain = one(*cuts[0])
    for cut in cuts[1:]:
        gain = gain * one(*cut)
    return gain


def gaussian(stream_key, shape, width, bound, pieces=(), held_as=jnp.bfloat16):
    values = jax.random.normal(stream_key, shape, jnp.float32) * width
    if len(pieces) > 0:
        values = steps_of(stream_key, shape, pieces, -0.22, 0.18) * values
    return jnp.clip(values, min=-bound, max=bound).astype(held_as)


def setup_inputs(seed: int = 0) -> dict:
    key_of = jax.random.split(jax.random.key(seed), 18)
    return {
        "patches": gaussian(key_of[0], (SLOTS, SLOT_LEN, D), 1.0, 6.0, ((0, 8), (1, 4))),
        "segments": draw_segments(jax.random.fold_in(key_of[17], 71), 0),
        "code_bits": set_ends(jax.random.randint(key_of[2], (SLOTS, SLOT_LEN, CODE), 0, 2), jax.random.fold_in(key_of[2], 1), 0, 1).astype(jnp.int32),
        "norm_gain": jnp.clip(1.0 + 0.1 * jax.random.normal(key_of[3], (2, 2, D), jnp.float32), 0.5, 1.5).astype(jnp.bfloat16),
        "norm_shift": gaussian(key_of[4], (2, 2, D), 0.2, 1.1953125, ((2, 32),)),
        "project_weight": gaussian(key_of[5], (2, D, 3 * D), (D // 2) ** -0.5, 0.3125, ((1, 32),)),
        "query_value_bias": gaussian(key_of[6], (2, 2, D), 0.2, 1.1953125, ((2, 32),)),
        "output_weight": gaussian(key_of[7], (2, D, D), (D // 8) ** -0.5, 0.625, ((1, 32),)),
        "output_bias": gaussian(key_of[8], (2, D), 0.2, 1.1953125, ((1, 32),)),
        "expand_weight": gaussian(key_of[9], (2, D, FF), D ** -0.5, 0.21875, ((1, 32),)),
        "expand_bias": gaussian(key_of[10], (2, FF), 0.2, 1.1953125, ((1, 32),)),
        "shrink_weight": gaussian(key_of[11], (2, FF, D), FF ** -0.5, 0.109375, ((1, 32),)),
        "shrink_bias": gaussian(key_of[12], (2, D), 0.2, 1.1953125, ((1, 32),)),
        "encode_weight": gaussian(key_of[13], (D, CODE), D ** -0.5, 0.21875, ((0, 32),)),
        "decode_weight": gaussian(key_of[14], (CODE, D), 1.0, 6.0, ((1, 32),)),
        "decode_bias": gaussian(key_of[15], (D,), 0.2, 1.1953125, ((0, 32),)),
        "cotangent": gaussian(key_of[16], (SLOTS, SLOT_LEN, D), 1.0, 6.0, ((0, 8), (1, 4))),
    }


@jax.custom_vjp
def low(v):
    return lax.optimization_barrier(v.astype(jnp.bfloat16)).astype(jnp.float32)

@jax.custom_vjp
def low_back(v):
    return v

def low_keep(v):
    return (low(v), None)

def low_pass(kept, grad):
    return (grad,)

def back_keep(v):
    return (v, None)

def back_low(kept, grad):
    return (low(grad),)
low.defvjp(low_keep, low_pass)
low_back.defvjp(back_keep, back_low)

def multiply(left, right):
    return jnp.dot(left, right, precision=lax.Precision.HIGHEST)

def layer_norm(stream, gains, shifts):
    centre = stream - lax.optimization_barrier(jnp.mean(stream, axis=-1, keepdims=True))
    spread = lax.optimization_barrier(jnp.mean(centre * centre, axis=-1, keepdims=True))
    return centre * lax.rsqrt(spread + 1e-06) * gains + shifts

def attention(projected, segment_row):
    length = projected.shape[0]
    queries = projected[:, :D].reshape(length, H, HD)
    key_rows = projected[:, D:2 * D].reshape(length, H, HD)
    values = projected[:, 2 * D:].reshape(length, H, HD)
    scores = jnp.einsum('qhd,khd->hqk', queries, key_rows, precision=lax.Precision.HIGHEST)
    scores = low_back(scores * HD ** (-0.5))
    same_item = segment_row[:, None] == segment_row[None, :]
    scores = jnp.where(same_item[None], scores, -1000000000.0)
    probability = low(jax.nn.softmax(scores, axis=-1))
    mixed_rows = jnp.einsum('hqk,khd->qhd', probability, values, precision=lax.Precision.HIGHEST)
    return low(low_back(mixed_rows.reshape(length, D)))

def block(stream, layer, segment_row):
    gains, shifts, project, query_value, output, output_shift, expand, expand_shift, shrink, shrink_shift = layer
    normed = low(layer_norm(stream, gains[0], shifts[0]))
    bias_row = jnp.concatenate([query_value[0], jnp.zeros_like(query_value[0]), query_value[1]])
    projected = low(low_back(multiply(normed, project) + bias_row))
    middle = stream + low_back(multiply(attention(projected, segment_row), output) + output_shift)
    normed_mid = low(layer_norm(middle, gains[1], shifts[1]))
    hidden = low_back(multiply(normed_mid, expand) + expand_shift)
    active = low(jax.nn.gelu(hidden, approximate=False))
    return middle + low_back(multiply(active, shrink) + shrink_shift)

def reference(patches, segments, code_bits, norm_gain, norm_shift, project_weight, query_value_bias, output_weight, output_bias, expand_weight, expand_bias, shrink_weight, shrink_bias, encode_weight, decode_weight, decode_bias, cotangent):
    stacked = tuple((array.astype(jnp.float32) for array in (norm_gain, norm_shift, project_weight, query_value_bias, output_weight, output_bias, expand_weight, expand_bias, shrink_weight, shrink_bias)))
    encoder = tuple((array[0] for array in stacked))
    decoder = tuple((array[1] for array in stacked))
    signs = (2 * code_bits - 1).astype(jnp.float32) * CODE ** (-0.5)

    def section_one(layer, encode_full, stream):

        def per_slot(slot_pair):
            encoded = block(slot_pair[0], layer, slot_pair[1])
            coded = low_back(multiply(low(encoded), encode_full))
            return coded / jnp.sqrt(lax.optimization_barrier(jnp.sum(coded * coded, axis=-1, keepdims=True)) + 1e-06)
        return lax.map(jax.checkpoint(per_slot), (stream, segments))

    def section_two(layer, decode_full, decode_shift, sign_rows):

        def per_slot(slot_pair):
            start = low_back(multiply(low(slot_pair[0]), decode_full) + decode_shift)
            return block(start, layer, slot_pair[1])
        return lax.map(jax.checkpoint(per_slot), (sign_rows, segments))
    decoded, back_two = jax.vjp(section_two, decoder, decode_weight.astype(jnp.float32), decode_bias.astype(jnp.float32), signs)
    decoder_grads, decode_grad, decode_bias_grad, sign_grad = back_two(cotangent.astype(jnp.float32))
    unit, back_one = jax.vjp(section_one, encoder, encode_weight.astype(jnp.float32), patches.astype(jnp.float32))
    encoder_grads, encode_grad, input_grad = back_one(sign_grad)
    pairs = tuple((jnp.stack([first, second]) for first, second in zip(encoder_grads, decoder_grads)))
    return (decoded.astype(jnp.bfloat16), input_grad, pairs[0], pairs[1], pairs[2], pairs[3], pairs[4], pairs[5], pairs[6], pairs[7], pairs[8], pairs[9], encode_grad, decode_grad, decode_bias_grad)
```

```python
import functools

import jax
import jax.numpy as jnp
from jax import lax
from jax.experimental import pallas as pl
from jax.experimental.pallas import tpu as pltpu
from jax.sharding import PartitionSpec as P

HD = 64
CODE = 18
epsilon = 1e-06
masked_score = -1000000000.0
MESH = pl.DeviceIdType.MESH
F32 = jnp.float32
BF16 = jnp.bfloat16
AXES = ("slot", "seq")
BIG = 60 * 1024 * 1024

NN = (((1,), (0,)), ((), ()))
NT = (((1,), (1,)), ((), ()))
TN = (((0,), (0,)), ((), ()))


def mm(a, b, dims=NN):
    return lax.dot_general(a, b, dims, preferred_element_type=F32)


def params(**more):
    return pltpu.CompilerParams(vmem_limit_bytes=BIG, **more)


def whole(shape):
    return pl.BlockSpec(shape, lambda *i: (0,) * len(shape))


def shaped(shape, dtype=BF16):
    return jax.ShapeDtypeStruct(shape, dtype)


def norm_parts(stream):
    centre = stream - jnp.mean(stream, axis=-1, keepdims=True)
    spread = jnp.mean(centre * centre, axis=-1, keepdims=True)
    scale = lax.rsqrt(spread + epsilon)
    return centre * scale, scale


def norm_back(grad, gain, hat, scale):
    lifted = grad * gain
    mean = jnp.mean(lifted, axis=-1, keepdims=True)
    mixed = jnp.mean(lifted * hat, axis=-1, keepdims=True)
    return scale * (lifted - mean - hat * mixed)


def columns(value):
    return jnp.sum(value, axis=0, keepdims=True)


def lanes_of(head):
    lane = lax.broadcasted_iota(jnp.int32, (1, 2 * HD), 1)
    return lane < HD if head == 0 else lane >= HD


def only(value, head):
    return jnp.where(lanes_of(head), value, jnp.zeros_like(value))


def gelu_parts(hidden):
    normal = 0.5 + 0.5 * lax.erf(hidden * 0.7071067811865476)
    density = jnp.exp(-0.5 * hidden * hidden) * 0.3989422804014327
    return hidden * normal, normal + hidden * density


def flip(index, bit):
    size = 1 << bit
    return index + size - 2 * size * ((index // size) % 2)


def relative(a, b):
    return 2 * ((a // 2 + b // 2) % 2) + (a + b) % 2


PARTS = 4
DMA = pltpu.SemaphoreType.DMA


def remote(src, dst, send, recv, peer):
    return pltpu.make_async_remote_copy(
        src_ref=src, dst_ref=dst, send_sem=send, recv_sem=recv, device_id=peer, device_id_type=MESH
    )


class Here:
    def __init__(self):
        self.slot, self.z = lax.axis_index("slot"), lax.axis_index("seq")
        self.across = (flip(self.slot, 1), self.z)
        self.beside = (flip(self.slot, 2), self.z)
        self.sibling = (flip(self.slot, 0), self.z)
        self.core, self.square = lax.rem(self.slot, 2), self.slot // 2

    def along(self, k):
        return (self.slot, relative(self.z, k))

    def greet(self):
        barrier = pltpu.get_barrier_semaphore()
        peers = [self.across, self.beside, self.sibling] + [self.along(k) for k in range(1, PARTS)]
        for peer in peers:
            pl.semaphore_signal(barrier, inc=1, device_id=peer, device_id_type=MESH)
        pl.semaphore_wait(barrier, len(peers))


class Line:
    @staticmethod
    def scratch(count):
        return [DMA((count, PARTS))] * 3

    def __init__(self, here, arrays, sems):
        self.here, self.arrays = here, arrays
        self.recv, self.up, self.down = sems

    def copy(self, m, block, upward):
        z = self.here.z
        to = jnp.minimum(z + 1, PARTS - 1) if upward else jnp.maximum(z - 1, 0)
        array = self.arrays[m]
        send = (self.up if upward else self.down).at[m, block]
        return remote(
            array.at[relative(block, z)], array.at[relative(block, to)], send, self.recv.at[m, block], (self.here.slot, to)
        )

    def onward(self, m, block, upward):
        z = self.here.z

        @pl.when((z < PARTS - 1) if upward else (z > 0))
        def _():
            self.copy(m, block, upward).start()

    def start(self, m):
        self.onward(m, self.here.z, True)
        self.onward(m, self.here.z, False)

    def hop(self, m, k):
        z = self.here.z

        @pl.when(z >= k)
        def _():
            self.copy(m, z - k, True).wait_recv()
            self.onward(m, z - k, True)

        @pl.when(z + k <= PARTS - 1)
        def _():
            self.copy(m, z + k, False).wait_recv()
            self.onward(m, z + k, False)

    def finish(self, m):
        z = self.here.z
        for block in range(PARTS):

            @pl.when((z < PARTS - 1) & (z >= block))
            def _():
                self.copy(m, block, True).wait_send()

            @pl.when((z > 0) & (z <= block))
            def _():
                self.copy(m, block, False).wait_send()


class Gather:
    @staticmethod
    def scratch(count):
        return [DMA((count, PARTS))] * 5 + [DMA((count,))] * 8

    def __init__(self, here, sources, outs, sems):
        self.here, self.sources, self.outs = here, sources, outs
        self.rz, self.up, self.down, self.rx, self.ry = sems[:5]
        self.local, self.sx, self.sy, self.rd, self.dx, self.dy, self.rc, self.sc = sems[5:]

    def place(self, m, block):
        return self.outs[m].at[self.here.slot, block]

    def copy(self, m, block, upward, src):
        z = self.here.z
        to = jnp.minimum(z + 1, PARTS - 1) if upward else jnp.maximum(z - 1, 0)
        send = (self.up if upward else self.down).at[m, block]
        return remote(src, self.place(m, block), send, self.rz.at[m, block], (self.here.slot, to))

    def onward(self, m, block, upward, src):
        z = self.here.z

        @pl.when((z < PARTS - 1) if upward else (z > 0))
        def _():
            self.copy(m, block, upward, src).start()

    def sideways(self, m, block, src):
        dst = self.place(m, block)
        remote(src, dst, self.sx.at[m], self.rx.at[m, block], self.here.across).start()
        remote(src, dst, self.sy.at[m], self.ry.at[m, block], self.here.beside).start()

    def keep(self, m):
        return pltpu.make_async_copy(self.sources[m], self.place(m, self.here.z), self.local.at[m])

    def start(self, m):
        src, z = self.sources[m], self.here.z
        self.onward(m, z, True, src)
        self.onward(m, z, False, src)
        self.sideways(m, z, src)
        self.keep(m).start()

    def arrived(self, m, block, upward):
        src = self.place(m, block)
        self.copy(m, block, upward, src).wait_recv()
        self.onward(m, block, upward, src)
        self.sideways(m, block, src)

    def hop(self, m, k):
        z = self.here.z

        @pl.when(z >= k)
        def _():
            self.arrived(m, z - k, True)

        @pl.when(z + k <= PARTS - 1)
        def _():
            self.arrived(m, z + k, False)

    def turned(self, m, block):
        across, beside = self.here.across, self.here.beside
        here = self.outs[m].at[across[0], block]
        remote(here, here, self.sx.at[m], self.rx.at[m, block], across).wait_recv()

        @pl.when(lax.rem(block, 2) == 0)
        def _():
            remote(here, here, self.dy.at[m], self.rd.at[m], beside).start()

        there = self.outs[m].at[beside[0], block]
        remote(there, there, self.sy.at[m], self.ry.at[m, block], beside).wait_recv()

        @pl.when(lax.rem(block, 2) == 1)
        def _():
            remote(there, there, self.dx.at[m], self.rd.at[m], across).start()

    def turn(self, m, k):
        z = self.here.z
        if k == 0:
            self.turned(m, z)
            return

        @pl.when(z >= k)
        def _():
            self.turned(m, z - k)

        @pl.when(z + k <= PARTS - 1)
        def _():
            self.turned(m, z + k)

    def share(self, m, slot):
        group = self.outs[m].at[slot]
        remote(group, group, self.sc.at[m], self.rc.at[m], self.here.sibling).start()

    def siblings(self, m):
        self.keep(m).wait()
        for slot in (self.here.slot, self.here.across[0], self.here.beside[0]):
            self.share(m, slot)

    def corner(self, m):
        slot = flip(self.here.across[0], 2)
        group = self.outs[m].at[slot]
        remote(group, group, self.dx.at[m], self.rd.at[m], self.here.across).wait_recv()
        self.share(m, slot)

    def finish(self, m):
        here, z, src = self.here, self.here.z, self.sources[m]
        for block in range(PARTS):

            @pl.when((z < PARTS - 1) & (z >= block))
            def _():
                self.copy(m, block, True, src).wait_send()

            @pl.when((z > 0) & (z <= block))
            def _():
                self.copy(m, block, False, src).wait_send()

        group = self.outs[m].at[here.slot]
        half = self.outs[m].at[here.slot, pl.ds(0, PARTS // 2)]
        remote(group, group, self.sx.at[m], self.rx.at[m, 0], here.across).wait_send()
        remote(group, group, self.sy.at[m], self.ry.at[m, 0], here.beside).wait_send()
        remote(half, half, self.dx.at[m], self.rd.at[m], here.across).wait_send()
        remote(half, half, self.dy.at[m], self.rd.at[m], here.beside).wait_send()
        four = self.outs[m].at[pl.ds(0, 4)]
        both = remote(four, four, self.sc.at[m], self.rc.at[m], here.sibling)
        both.wait_send()
        both.wait_recv()


def add_into(target, source):
    rows, units = target.shape[:2]

    def one(i, carry):
        a, b = i // units, lax.rem(i, units)
        target[a, b] = (target[a, b].astype(F32) + source[a, b].astype(F32)).astype(target.dtype)
        return carry

    lax.fori_loop(0, rows * units, one, 0)


class Square:
    @staticmethod
    def scratch(units, tail, loaded):
        held = [pltpu.VMEM((4, PARTS, units) + tail, BF16)] if loaded else []
        half = pltpu.VMEM((PARTS // 2, units) + tail, BF16)
        full = pltpu.VMEM((PARTS, units) + tail, BF16)
        return held + [half, half, full, full, DMA((9,))]

    def __init__(self, here, held, scratch, source=None):
        self.here, self.held, self.source = here, held, source
        self.corner_x, self.corner_y, self.side_x, self.side_y, self.sems = scratch

    def load(self, start=True):
        copy = pltpu.make_async_copy(self.source, self.held, self.sems.at[8])
        copy.start() if start else copy.wait()

    def move(self, n):
        half, held, sems = PARTS // 2, self.held, self.sems
        src = (held.at[3, pl.ds(0, half)], held.at[3, pl.ds(half, half)], held.at[1], held.at[2])[n]
        dst = (self.corner_x, self.corner_y, self.side_x, self.side_y)[n]
        peer = self.here.beside if n % 2 else self.here.across
        return remote(src, dst, sems.at[2 * n], sems.at[2 * n + 1], peer)

    def start(self):
        if self.source is not None:
            self.load(False)
        for n in range(2):
            self.move(n).start()

    def sides(self):
        half = PARTS // 2
        self.move(0).wait_recv()
        add_into(self.held.at[2, pl.ds(0, half)], self.corner_x)
        self.move(3).start()
        self.move(1).wait_recv()
        add_into(self.held.at[1, pl.ds(half, half)], self.corner_y)
        self.move(2).start()

    def total(self, out):
        self.move(2).wait_recv()
        self.move(3).wait_recv()
        units = out.shape[1]

        def one(i, carry):
            a, b = i // units, lax.rem(i, units)
            value = self.held[0, a, b].astype(F32) + self.side_x[a, b].astype(F32) + self.side_y[a, b].astype(F32)
            out[a, b] = value.astype(out.dtype)
            return carry

        lax.fori_loop(0, PARTS * units, one, 0)
        for n in range(4):
            self.move(n).wait_send()


class Stack:
    @staticmethod
    def scratch(units, tail):
        return [pltpu.VMEM((PARTS - 1, units) + tail, BF16), DMA((2, PARTS))]

    def __init__(self, here, held, scratch):
        self.here, self.held = here, held
        self.arrived, self.sems = scratch

    def moves(self):
        for k in range(1, PARTS):
            peer = self.here.along(k)
            yield remote(self.held.at[peer[1]], self.arrived.at[k - 1], self.sems.at[0, k], self.sems.at[1, k], peer)

    def start(self):
        for move in self.moves():
            move.start()

    def finish(self, out):
        for move in self.moves():
            move.wait_recv()
        units, z = out.shape[0], self.here.z

        def one(unit, carry):
            value = self.held[z, unit].astype(F32)
            for k in range(PARTS - 1):
                value += self.arrived[k, unit].astype(F32)
            out[unit] = value
            return carry

        lax.fori_loop(0, units, one, 0)
        for move in self.moves():
            move.wait_send()


class Cores:
    @staticmethod
    def scratch(units, tail):
        return [pltpu.VMEM((4, PARTS, units) + tail, BF16), pltpu.VMEM((2, 8, PARTS) + tail, BF16), DMA((units,)), DMA((units,))]

    def __init__(self, here, sums, scratch, hidden):
        self.here, self.sums, self.hidden = here, sums, hidden
        self.far, self.turn, self.send, self.recv = scratch

    def moves(self, n, hidden):
        here, slot = self.here, lax.rem(n, 2)
        give = 1 - here.core
        if hidden:
            to = self.far.at[relative(here.square, n), :, pl.ds(0, self.hidden)]
            return [(self.turn.at[slot, pl.ds(4 * give, 4)], to)], to
        pairs = [(self.turn.at[slot, 2 * s + give], self.far.at[relative(here.square, s), :, n]) for s in range(4)]
        return pairs, self.far.at[:, :, n]

    def each(self, n, action):
        if self.hidden:

            @pl.when(n < self.hidden)
            def _():
                action(True)

            @pl.when(n >= self.hidden)
            def _():
                action(False)
        else:
            action(False)

    def waited(self, n, hidden, recv):
        whole_ref = self.moves(n, hidden)[1]
        move = remote(whole_ref, whole_ref, self.send.at[n], self.recv.at[n], self.here.sibling)
        move.wait_recv() if recv else move.wait_send()

    def put(self, n, value):
        here, slot = self.here, lax.rem(n, 2)

        @pl.when(n >= 2)
        def _():
            self.each(n - 2, lambda hidden: self.waited(n - 2, hidden, False))

        self.turn[slot] = value.reshape(self.turn.shape[1:]).astype(BF16)

        def action(hidden):
            for src, dst in self.moves(n, hidden)[0]:
                remote(src, dst, self.send.at[n], self.recv.at[n], here.sibling).start()
            if hidden:
                self.sums[relative(here.square, n), :, pl.ds(0, self.hidden)] = self.turn[slot, pl.ds(4 * here.core, 4)]
            else:
                for s in range(4):
                    self.sums[relative(here.square, s), :, n] = self.turn[slot, 2 * s + here.core]

        self.each(n, action)

    def collect(self, n):
        def action(hidden):
            self.waited(n, hidden, True)
            if hidden:
                at = relative(self.here.square, n)
                add_into(self.sums.at[at, :, pl.ds(0, self.hidden)], self.far.at[at, :, pl.ds(0, self.hidden)])
            else:
                for s in range(4):

                    def one(a, carry):
                        value = self.sums[s, a, n].astype(F32) + self.far[s, a, n].astype(F32)
                        self.sums[s, a, n] = value.astype(BF16)
                        return carry

                    lax.fori_loop(0, PARTS, one, 0)

        self.each(n, action)

    def finish(self, count):
        for n in (count - 2, count - 1):
            self.waited(n, n < self.hidden, False)


class Item:
    def __init__(self, array, spec=None):
        self.array = array
        self.spec = spec or whole(array.shape)


def anywhere(array):
    return Item(array, pl.BlockSpec(memory_space=pl.ANY))


def run(body, steps, ins, outs, scratch, collective, name, cost):
    in_names, out_names, scratch_names = list(ins), list(outs), list(scratch)
    flat_scratch, spans = [], {}
    for key in scratch_names:
        item = scratch[key]
        many = isinstance(item, list)
        spans[key] = (len(flat_scratch), len(item) if many else None)
        flat_scratch += item if many else [item]

    def kernel(*refs):
        first, second = len(in_names), len(in_names) + len(out_names)
        in_refs = dict(zip(in_names, refs[:first]))
        out_refs = dict(zip(out_names, refs[first:second]))
        rest = refs[second:]
        own = {k: rest[at] if n is None else rest[at : at + n] for k, (at, n) in spans.items()}
        here = Here()
        step = pl.program_id(0)

        @pl.when(step == 0)
        def _():
            here.greet()

        body(here, step, in_refs, out_refs, own)

    results = pl.pallas_call(
        kernel,
        grid=(steps,),
        in_specs=[i.spec for i in ins.values()],
        out_specs=tuple(o.spec for o in outs.values()),
        out_shape=tuple(o.array for o in outs.values()),
        scratch_shapes=flat_scratch,
        compiler_params=pltpu.CompilerParams(
            vmem_limit_bytes=BIG, collective_id=collective, has_side_effects=True, dimension_semantics=("arbitrary",)
        ),
        cost_estimate=pl.CostEstimate(flops=cost * 1150000000, bytes_accessed=0, transcendentals=0),
        name=name,
    )(*[i.array for i in ins.values()])
    return dict(zip(out_names, results))


def at_step(step, n):
    def decorate(action):
        pl.when(step == n)(action)

    return decorate


def first_kernel(here, step, ins, outs, own):
    table = own["table"]
    table[...] = jnp.zeros_like(table)
    gain, shift, query_value = ins["gain"], ins["shift"], ins["query_value"]
    for start, item in ((0, gain), (4, shift), (8, query_value)):
        for i in range(4):
            table[start + i : start + i + 1, :] = item[i // 2, i % 2 : i % 2 + 1, :].astype(F32)
    table[12:14, :] = ins["output_bias"][...].astype(F32)
    table[14:16, :] = ins["shrink_bias"][...].astype(F32)
    table[16:17, :] = ins["decode_bias"][...].astype(F32)
    fine = gain.shape[2]
    wide = ins["expand_bias"][...].astype(F32)
    for i in range(8):
        table[17 + i : 18 + i, :] = wide[i // 4 : i // 4 + 1, fine * (i % 4) : fine * (i % 4 + 1)]
    table[25:43, :] = ins["encode"][...].astype(F32).T
    table[43:61, :] = ins["decode"][...].astype(F32)
    names = ("project", "output", "expand", "shrink")
    gather = Gather(
        here, [table] + [ins[n].at[1] for n in names], [outs["table"]] + [outs[n] for n in names], own["gather"]
    )
    line = Line(here, [outs["signs"], outs["patches"]], own["line"])
    keeps = [
        pltpu.make_async_copy(ins[n].at[0], outs[n].at[0], own["keep"].at[i]) for i, n in enumerate(("signs", "patches"))
    ]
    messages = range(len(names) + 1)
    gather.start(0)
    for keep in keeps:
        keep.start()
    for m in messages[1:]:
        gather.start(m)
    for keep in keeps:
        keep.wait()
    line.start(0)
    for k in range(1, PARTS):
        line.hop(0, k)
        for m in messages:
            gather.hop(m, k)
            gather.turn(m, k - 1)
        if k == 1:
            line.start(1)
        else:
            line.hop(1, k - 1)
    for m in messages:
        gather.turn(m, PARTS - 1)
        gather.siblings(m)
    line.hop(1, PARTS - 1)
    for m in messages:
        gather.corner(m)
    for m in messages:
        gather.finish(m)
    for m in range(2):
        line.finish(m)


def forward_attention(coded, layer, slots, ins, extra, collective):
    pieces, table, weight = ins["pieces"].array, ins["table"].array, ins["weight"].array
    rows = pieces.shape[1]
    width, triple = weight.shape
    length = PARTS * rows
    pairs, lanes = width // (2 * HD), 2 * HD
    steps = PARTS + pairs
    outs = {
        "qkv": Item(shaped((length, triple)), pl.BlockSpec((rows, triple), lambda i: (jnp.minimum(i, PARTS - 1), 0))),
        "normed": Item(shaped((rows, width))),
        "mixed": Item(shaped((rows, width)), pl.BlockSpec((rows, lanes), lambda i: (0, jnp.maximum(i - PARTS, 0)))),
        "logs": Item(shaped((rows, 128), F32)),
    }
    if coded:
        outs["stream"] = Item(shaped((rows, width), F32))
    scratch = {"qkv_held": pltpu.VMEM((length, triple), BF16)}
    extra.declare(ins, outs, scratch)

    def body(here, step, ins, outs, own):
        extra.events(here, step, steps, ins, outs, own)
        table = ins["table"]
        held = own["qkv_held"]

        @pl.when(step < PARTS)
        def _():
            if coded:
                decode = table[43:61, :].astype(BF16)
                stream = mm(ins["pieces"][step], decode) + table[16:17, :]
            else:
                stream = ins["pieces"][step].astype(F32)
            hat, unused = norm_parts(stream)
            normed = (hat * table[2 * layer : 2 * layer + 1, :] + table[4 + 2 * layer : 5 + 2 * layer, :]).astype(BF16)
            at = pl.ds(pl.multiple_of(step * rows, rows), rows)
            for part in range(3):
                span = pl.ds(part * width, width)
                value = mm(normed, ins["weight"][:, span])
                if part != 1:
                    shift = 8 + 2 * layer + part // 2
                    value += table[shift : shift + 1, :]
                value = value.astype(BF16)
                outs["qkv"][:, span] = value
                held[at, span] = value

            @pl.when(step == 0)
            def _():
                outs["normed"][...] = normed
                if coded:
                    outs["stream"][...] = stream

        @pl.when(step >= PARTS)
        def _():
            pair = step - PARTS
            logs = outs["logs"]
            lane = lax.broadcasted_iota(jnp.int32, (1, 128), 1)

            @pl.when(pair == 0)
            def _():
                logs[...] = jnp.zeros_like(logs)

            def span(part):
                return pl.ds(pl.multiple_of(part * width + pair * lanes, lanes), lanes)

            keys, values = held[:, span(1)], held[:, span(2)]
            segments = ins["segment_row"][...]
            for start in range(0, rows, BLOCK):
                at = pl.ds(start, BLOCK)
                same = ins["segment_column"][at, :] == segments
                queries = held[at, span(0)] * jnp.asarray(HD**-0.5, BF16)
                parts = []
                for head in range(2):
                    scores = jnp.where(same, mm(only(queries, head), keys, NT), masked_score)
                    top = jnp.max(scores, axis=-1, keepdims=True)
                    raised = jnp.exp(scores - top)
                    total = jnp.sum(raised, axis=-1, keepdims=True)
                    parts.append(mm(raised.astype(BF16), values) / total)
                    logs[at, :] += jnp.where(lane == 2 * pair + head, top + jnp.log(total), 0.0)
                outs["mixed"][at, :] = jnp.where(lanes_of(0), parts[0], parts[1]).astype(BF16)

        extra.closing(here, step, steps, ins, outs, own)

    return run(body, steps, ins, outs, scratch, collective, "forward_attention", 30)


BLOCK = 128


def middle_block(encoder, layer, slots, ins, extra, collective):
    width = ins["output"].array.shape[1]
    rows = ins["mixed"].array.shape[0]
    hidden = ins["shrink"].array.shape[0]
    fine = width // slots // PARTS
    tile = 512
    tiles = hidden // tile
    feed = 2 * tiles if encoder else tiles
    units = hidden // width + hidden // width + 1
    wide = hidden // width
    pairs, lanes = width // (2 * HD), 2 * HD
    length = PARTS * rows
    first_query = feed + units
    first_key = first_query + pairs
    steps = first_key + PARTS

    def tiled(i):
        return lax.rem(jnp.minimum(i, feed - 1), tiles)

    late = feed - tiles
    ins["expand"].spec = pl.BlockSpec((width, tile), lambda i: (0, tiled(i)))
    ins["expand_shift"].spec = pl.BlockSpec((1, tile), lambda i: (0, tiled(i)))
    ins["shrink"].spec = pl.BlockSpec((tile, width), lambda i: (tiled(i), 0))
    ins["stream"].spec = pl.BlockSpec((1, rows, width), lambda i: (0, 0, 0))
    outs = {
        "query": Item(shaped((rows, width)), pl.BlockSpec((rows, lanes), lambda i: (0, jnp.clip(i - first_query, 0, pairs - 1)))),
        "key": Item(shaped((rows, width))),
        "value": Item(shaped((rows, width))),
        "middle": Item(shaped((rows, width), F32)),
        "small": Item(shaped((8, width), F32)),
        "wide": Item(shaped((1, hidden), F32), pl.BlockSpec((1, tile), lambda i: (0, jnp.clip(i - late, 0, tiles - 1)))),
    }
    scratch = {
        "active": pltpu.VMEM((rows, hidden), BF16),
        "hidden_low": pltpu.VMEM((rows, hidden), BF16),
        "normed": pltpu.VMEM((rows, width), BF16),
        "hat": pltpu.VMEM((rows, width), F32),
        "scale": pltpu.VMEM((rows, 1), F32),
        "total": pltpu.VMEM((rows, width), F32),
        "back": pltpu.VMEM((rows, width), F32),
        "low": pltpu.VMEM((rows, width), BF16),
        "branch": pltpu.VMEM((rows, width), BF16),
        "delta": pltpu.VMEM((rows, 128), F32),
        "qkv_held": pltpu.VMEM((length, 3 * width), BF16),
        "qkv_sem": DMA((1,)),
        "mixed_back": pltpu.VMEM((PARTS, rows, width), BF16),
        "stats": pltpu.VMEM((PARTS, 32, rows), F32),
        "line": Line.scratch(2),
        "cores": Cores.scratch(units, (fine, width)),
    }
    if encoder:
        outs["code_grad"] = Item(shaped((CODE, width), F32))
        scratch["slope"] = pltpu.VMEM((tiles, rows, tile), BF16)
        scratch["sums"] = pltpu.VMEM((4, PARTS, units, fine, width), BF16)
    else:
        outs["decoded"] = Item(shaped((rows, width)))
        outs["sums"] = Item(shaped((4, PARTS, units, fine, width)))
    extra.declare(ins, outs, scratch)
    extra.marks = {"feed": feed, "grads": feed, "query": first_query, "key": first_key}

    def body(here, step, ins, outs, own):
        table = ins["table"]
        normed, hat, scale, total, back, low = (own[n] for n in ("normed", "hat", "scale", "total", "back", "low"))
        mixed_back, stats, held = own["mixed_back"], own["stats"], own["qkv_held"]
        sums = own["sums"] if encoder else outs["sums"]
        cores = Cores(here, sums, own["cores"], wide)
        line = Line(here, [mixed_back, stats], own["line"])
        load = pltpu.make_async_copy(ins["qkv"], held, own["qkv_sem"].at[0])
        gain, shift = table[2 * layer + 1 : 2 * layer + 2, :], table[5 + 2 * layer : 6 + 2 * layer, :]
        extra.events(here, step, steps, ins, outs, own)

        @at_step(step, 0)
        def _():
            load.start()
            middle = ins["stream"][0].astype(F32) + mm(ins["mixed"][...], ins["output"][...]) + table[12 + layer : 13 + layer, :]
            hat[...], scale[...] = norm_parts(middle)
            normed[...] = (hat[...] * gain + shift).astype(BF16)
            total[...] = middle + table[14 + layer : 15 + layer, :]
            back[...] = jnp.zeros_like(back)
            if not encoder:
                low[...] = ins["other"][...]

        def columns_at(n):
            return pl.ds(pl.multiple_of(n * tile, tile), tile)

        def forward(n):
            value = mm(normed[...], ins["expand"][...]) + ins["expand_shift"][...]
            active, steep = gelu_parts(value)
            active = active.astype(BF16)
            own["active"][:, columns_at(n)] = active
            total[...] += mm(active, ins["shrink"][...])
            return steep

        def backward(n, steep):
            hidden_low = (steep * mm(low[...], ins["shrink"][...], NT)).astype(BF16)
            own["hidden_low"][:, columns_at(n)] = hidden_low
            outs["wide"][...] = columns(hidden_low.astype(F32))
            back[...] += mm(hidden_low, ins["expand"][...], NT)

        if encoder:

            @pl.when(step < tiles)
            def _():
                own["slope"][step] = forward(step).astype(BF16)

            @at_step(step, tiles - 1)
            def _():
                code = table[25:43, :].astype(BF16)
                encoded_low = total[...].astype(BF16)
                coded = mm(encoded_low, code, NT)
                size = lax.rsqrt(jnp.sum(coded * coded, axis=-1, keepdims=True) + epsilon)
                unit = coded * size
                grad = ins["other"][...]
                coded_low = ((grad - unit * jnp.sum(unit * grad, axis=-1, keepdims=True)) * size).astype(BF16)
                outs["code_grad"][...] = mm(coded_low, encoded_low, TN)
                total[...] = mm(coded_low, code)
                low[...] = total[...].astype(BF16)

            @pl.when((step >= tiles) & (step < feed))
            def _():
                backward(step - tiles, own["slope"][step - tiles].astype(F32))
        else:

            @pl.when(step < tiles)
            def _():
                backward(step, forward(step))

        @at_step(step, feed - 1)
        def _():
            if encoder:
                grad_out = total[...]
            else:
                outs["decoded"][...] = total[...].astype(BF16)
                grad_out = low[...].astype(F32)
            grad = back[...]
            middle = grad_out + norm_back(grad, gain, hat[...], scale[...])
            outs["middle"][...] = middle
            branch = middle.astype(BF16)
            own["branch"][...] = branch
            mixed_low = mm(branch, ins["output"][...], NT).astype(BF16)
            mixed_back[0] = mixed_low
            product = mixed_low.astype(F32) * ins["mixed"][...].astype(F32)
            feature = lax.broadcasted_iota(jnp.int32, (width, 128), 0) // HD
            heads = (feature == lax.broadcasted_iota(jnp.int32, (width, 128), 1)).astype(F32)
            delta = lax.dot_general(product, heads, NN, preferred_element_type=F32, precision=lax.Precision.HIGHEST)
            own["delta"][...] = delta
            stats[0, pl.ds(0, 16)] = ins["logs"][...].T[:16]
            stats[0, pl.ds(16, 16)] = delta.T[:16]
            for m in range(2):
                line.start(m)
            outs["small"][...] = jnp.concatenate(
                [columns(grad * hat[...]), columns(grad), columns(branch.astype(F32)), columns(low[...].astype(F32))]
                + [jnp.zeros_like(columns(grad))] * 4
            )

        unit = step - feed

        def wide_at(n):
            return pl.ds(pl.multiple_of(n * width, width), width)

        @pl.when((unit >= 0) & (unit < wide))
        def _():
            cores.put(unit, mm(own["active"][:, wide_at(unit)], low[...], TN))

        @pl.when((unit >= wide) & (unit < 2 * wide))
        def _():
            cores.put(unit, mm(normed[...], own["hidden_low"][:, wide_at(unit - wide)], TN))

        @pl.when(unit == 2 * wide)
        def _():
            cores.put(unit, mm(ins["mixed"][...], own["branch"][...], TN))

        @pl.when((unit >= 2) & (unit < units))
        def _():
            cores.collect(unit - 2)

        @pl.when(unit == units)
        def _():
            cores.collect(unit - 2)
            cores.collect(unit - 1)
            cores.finish(units)

        for n, k in ((units - 1, 1), (units + 3, 2)):

            @pl.when(unit == n)
            def _():
                for m in range(2):
                    line.hop(m, k)

        @at_step(step, first_query)
        def _():
            load.wait()

        eighth = jnp.asarray(HD**-0.5, BF16)

        @pl.when((step >= first_query) & (step < first_key))
        def _():
            pair = step - first_query
            lane = lax.broadcasted_iota(jnp.int32, (1, 128), 1)

            def span(part):
                return pl.ds(pl.multiple_of(part * width + pair * lanes, lanes), lanes)

            keys, values = held[:, span(1)], held[:, span(2)]
            segments = ins["segment_row"][...]
            for start in range(0, rows, BLOCK):
                at = pl.ds(start, BLOCK)
                same = ins["segment_column"][at, :] == segments
                queries = held[at, span(0)] * eighth
                grads = mixed_back[0, at, span(0)]
                parts = []
                for head in range(2):
                    mine = lane == 2 * pair + head
                    log_sum = jnp.sum(jnp.where(mine, ins["logs"][at, :], 0.0), axis=-1, keepdims=True)
                    centre = jnp.sum(jnp.where(mine, own["delta"][at, :], 0.0), axis=-1, keepdims=True)
                    scores = jnp.where(same, mm(only(queries, head), keys, NT), masked_score)
                    probability = jnp.exp(scores - log_sum)
                    prob_grad = mm(only(grads, head), values, NT)
                    score_low = (probability * (prob_grad - centre)).astype(BF16)
                    parts.append(mm(score_low, keys) * HD**-0.5)
                outs["query"][at, :] = jnp.where(lanes_of(0), parts[0], parts[1]).astype(BF16)

        piece = step - first_key

        @pl.when(piece == 2)
        def _():
            for m in range(2):
                line.hop(m, 3)

        @pl.when(piece >= 0)
        def _():
            of_piece = pl.ds(pl.multiple_of(piece * rows, rows), rows)
            segments = ins["segment_row"][:, of_piece]

            def one(pair, carry):
                def span(part):
                    return pl.ds(pl.multiple_of(part * width + pair * lanes, lanes), lanes)

                queries = held[of_piece, span(0)]
                grads = mixed_back[piece, :, span(0)]
                for start in range(0, rows, BLOCK):
                    at = pl.ds(start, BLOCK)
                    same = ins["segment_column"][at, :] == segments
                    keys = held[at, span(1)] * eighth
                    values = held[at, span(2)]
                    key_parts, value_parts = [], []
                    for head in range(2):
                        log_sum = stats[piece, pl.ds(2 * pair + head, 1), :]
                        centre = stats[piece, pl.ds(16 + 2 * pair + head, 1), :]
                        scores = jnp.where(same, mm(only(keys, head), queries, NT), masked_score)
                        probability = jnp.exp(scores - log_sum)
                        value_parts.append(mm(probability.astype(BF16), grads))
                        prob_grad = mm(only(values, head), grads, NT)
                        score_low = (probability * (prob_grad - centre)).astype(BF16)
                        key_parts.append(mm(score_low, queries) * HD**-0.5)
                    key_part = jnp.where(lanes_of(0), key_parts[0], key_parts[1])
                    value_part = jnp.where(lanes_of(0), value_parts[0], value_parts[1])

                    @pl.when(piece == 0)
                    def _():
                        hat[at, span(0)] = key_part
                        total[at, span(0)] = value_part

                    @pl.when(piece > 0)
                    def _():
                        hat[at, span(0)] += key_part
                        total[at, span(0)] += value_part

                return carry

            lax.fori_loop(0, pairs, one, 0)

        @pl.when(piece == PARTS - 1)
        def _():
            outs["key"][...] = hat[...].astype(BF16)
            outs["value"][...] = total[...].astype(BF16)
            for m in range(2):
                line.finish(m)

        extra.closing(here, step, steps, ins, outs, own)

    return run(body, steps, ins, outs, scratch, collective, "encoder_middle" if encoder else "decoder_middle", 80)


def projection_back(coded, layer, slots, ins, extra, collective):
    rows, width = ins["query"].array.shape
    fine = width // slots // PARTS
    units = 3
    steps = 1 + units
    ins["stream"].spec = pl.BlockSpec((1, rows, width), lambda i: (0, 0, 0))
    outs = {"small": Item(shaped((8, width), F32)), "sums": Item(shaped((4, PARTS, units, fine, width)))}
    if coded:
        outs["unit_grad"] = Item(shaped((rows, CODE), F32))
        outs["decode_grad"] = Item(shaped((CODE, width), F32))
        ins["pieces"].spec = pl.BlockSpec((1, rows, CODE), lambda i: (0, 0, 0))
    else:
        outs["grad"] = Item(shaped((rows, width), F32))
    scratch = {"cores": Cores.scratch(units, (fine, width))}
    extra.declare(ins, outs, scratch)

    def body(here, step, ins, outs, own):
        table = ins["table"]
        cores = Cores(here, outs["sums"], own["cores"], 0)
        extra.events(here, step, steps, ins, outs, own)
        sources = (ins["query"], ins["key"], ins["value"])
        for n in range(units):

            @at_step(step, n)
            def _():
                cores.put(jnp.int32(n), mm(ins["normed"][...], sources[n][...], TN))

        @at_step(step, units)
        def _():
            query, key, value = sources
            weight = ins["weight"]
            grad = mm(query[...], weight[:, :width], NT)
            grad += mm(key[...], weight[:, width : 2 * width], NT)
            grad += mm(value[...], weight[:, 2 * width :], NT)
            hat, scale = norm_parts(ins["stream"][0].astype(F32))
            start = ins["middle"][...] + norm_back(grad, table[2 * layer : 2 * layer + 1, :], hat, scale)
            small = [columns(grad * hat), columns(grad), columns(query[...].astype(F32)), columns(value[...].astype(F32))]
            if coded:
                start_low = start.astype(BF16)
                outs["unit_grad"][...] = mm(start_low, table[43:61, :].astype(BF16), NT)
                outs["decode_grad"][...] = mm(ins["pieces"][0], start_low, TN)
                small.append(columns(start_low.astype(F32)))
            else:
                outs["grad"][...] = start
            small += [jnp.zeros_like(small[0])] * (8 - len(small))
            outs["small"][...] = jnp.concatenate(small)
            for n in range(units):
                cores.collect(jnp.int32(n))
            cores.finish(units)

        extra.closing(here, step, steps, ins, outs, own)

    return run(body, steps, ins, outs, scratch, collective, "projection_back", 12)


def last_kernel(here, step, ins, outs, own):
    square = Square(here, own["square"][0], own["square"][1:], ins["sums"])
    stack = Stack(here, own["total"], own["stack"])
    tables, arrived, sems = own["tables"], own["arrived"], own["sems"]
    square.load()
    in0, in1, mid0, mid1 = (ins[n] for n in ("in0", "in1", "mid0", "mid1"))
    rows = [in0[0:1], mid0[0:1], in1[0:1], mid1[0:1], in0[1:2], mid0[1:2], in1[1:2], mid1[1:2]]
    rows += [in0[2:4], in1[2:4], mid0[2:3], mid1[2:3], mid0[3:4], mid1[3:4], in1[4:5]]
    at = 0
    tables[0] = jnp.zeros_like(tables[0])
    for value in rows:
        tables[0, at : at + value.shape[0], :] = value
        at += value.shape[0]
    width = tables.shape[2]
    for wide in (ins["wide0"], ins["wide1"]):
        for start in range(0, wide.shape[1], width):
            tables[0, at : at + 1, :] = wide[:, start : start + width]
            at += 1
    for value in (ins["code_grad"], ins["decode_grad"]):
        tables[0, at : at + value.shape[0], :] = value[...]
        at += value.shape[0]

    def move(stage, peer, k=0):
        slot = stage + k
        return remote(tables.at[stage], arrived.at[slot], sems.at[0, slot], sems.at[1, slot], peer)

    peers = (here.sibling, here.across, here.beside)
    move(0, peers[0]).start()
    square.start()

    def meet(stage):
        move(stage, peers[stage]).wait_recv()
        tables[stage + 1] = tables[stage] + arrived[stage]
        if stage + 1 < len(peers):
            move(stage + 1, peers[stage + 1]).start()

    meet(0)
    square.sides()
    meet(1)
    square.total(own["total"])
    stack.start()
    meet(2)
    for k in range(1, PARTS):
        move(3, here.along(k), k - 1).start()
    stack.finish(outs["units"])
    value = tables[3]
    for k in range(1, PARTS):
        move(3, here.along(k), k - 1).wait_recv()
        value += arrived[2 + k]
    outs["table"][...] = value
    for stage, peer in enumerate(peers):
        move(stage, peer).wait_send()
    for k in range(1, PARTS):
        move(3, here.along(k), k - 1).wait_send()


class Nothing:
    def declare(self, ins, outs, scratch):
        pass

    def events(self, here, step, steps, ins, outs, own):
        pass

    def closing(self, here, step, steps, ins, outs, own):
        pass


class Beside(Nothing):
    def __init__(self, slots, gathers=None, gather_steps=(), squares=None, square_steps=None, stacks=None, stack_steps=None, inner=None):
        self.slots, self.gathers, self.gather_steps = slots, gathers or {}, gather_steps
        self.squares, self.square_steps = squares or {}, square_steps or {}
        self.stacks, self.stack_steps = stacks or {}, stack_steps or {}
        self.inner = inner

    def declare(self, ins, outs, scratch):
        for name, (array, layer) in self.gathers.items():
            ins["shard_" + name] = anywhere(array)
            outs["gathered_" + name] = anywhere(shaped((self.slots, PARTS) + array.shape[1:]))
        if self.gathers:
            scratch["gather"] = Gather.scratch(len(self.gathers))
        for name, (sums, first, units) in self.squares.items():
            ins["square_" + name] = anywhere(sums)
            tail = sums.shape[3:]
            outs["total_" + name] = Item(shaped((PARTS, units) + tail))
            scratch["square_" + name] = Square.scratch(units, tail, True)
        for name, array in self.stacks.items():
            ins["stack_" + name] = Item(array)
            outs["stacked_" + name] = Item(shaped(array.shape[1:], F32))
            scratch["stack_" + name] = Stack.scratch(array.shape[1], array.shape[2:])
        if self.inner:
            name, units = self.inner
            shape = scratch["sums"].shape
            outs["total_" + name] = Item(shaped(shape[1:]))
            scratch["inner"] = Square.scratch(units, shape[3:], False)

    def events(self, here, step, steps, ins, outs, own):
        if self.gathers:
            names = list(self.gathers)
            sources = [ins["shard_" + n].at[self.gathers[n][1]] for n in names]
            gather = Gather(here, sources, [outs["gathered_" + n] for n in names], own["gather"])
            count = range(len(names))

            def each(*actions):
                for action, *more in actions:
                    for m in count:
                        action(m, *more)

            start, one, two, three, turn, corner = self.gather_steps
            stages = [
                (start, [(gather.start,)]),
                (one, [(gather.hop, 1), (gather.turn, 0)]),
                (two, [(gather.hop, 2), (gather.turn, 1)]),
                (three, [(gather.hop, 3), (gather.turn, 2)]),
                (turn, [(gather.turn, 3), (gather.siblings,)]),
                (corner, [(gather.corner,)]),
                (steps - 1, [(gather.finish,)]),
            ]
            for n, actions in stages:
                at_step(step, n)(lambda actions=actions: each(*actions))
        for name, (sums, first, units) in self.squares.items():
            scratch = own["square_" + name]
            square = Square(here, scratch[0], scratch[1:], ins["square_" + name].at[:, :, pl.ds(first, units)])
            load, start, sides, total = self.square_steps[name]
            at_step(step, load)(square.load)
            at_step(step, start)(square.start)
            at_step(step, sides)(square.sides)
            at_step(step, total)(lambda square=square, name=name: square.total(outs["total_" + name]))
        for name in self.stacks:
            stack = Stack(here, ins["stack_" + name], own["stack_" + name])
            start, finish = self.stack_steps[name]
            at_step(step, start)(stack.start)
            at_step(step, finish)(lambda stack=stack, name=name: stack.finish(outs["stacked_" + name]))
        if self.inner:
            name, units = self.inner
            square = Square(here, own["sums"], own["inner"])
            start, sides = self.square_steps[name]
            at_step(step, start)(square.start)
            at_step(step, sides)(square.sides)

    def closing(self, here, step, steps, ins, outs, own):
        if self.inner:
            name, units = self.inner
            square = Square(here, own["sums"], own["inner"])
            at_step(step, steps - 1)(lambda: square.total(outs["total_" + name]))


def on_device(
    patches,
    segments,
    code_bits,
    norm_gain,
    norm_shift,
    project_weight,
    query_value_bias,
    output_weight,
    output_bias,
    expand_weight,
    expand_bias,
    shrink_weight,
    shrink_bias,
    encode_weight,
    decode_weight,
    decode_bias,
    cotangent,
):
    slots, parts = lax.axis_size("slot"), lax.axis_size("seq")
    fine, width = project_weight.shape[1], patches.shape[-1]
    if slots != 8 or parts != PARTS or fine % 8:
        return plain_device(
            patches,
            segments,
            code_bits,
            norm_gain,
            norm_shift,
            project_weight,
            query_value_bias,
            output_weight,
            output_bias,
            expand_weight,
            expand_bias,
            shrink_weight,
            shrink_bias,
            encode_weight,
            decode_weight,
            decode_bias,
            cotangent,
        )
    slot, z = lax.axis_index("slot"), lax.axis_index("seq")
    devices, rows, hidden = slots * parts, patches.shape[1], expand_weight.shape[-1]
    signs = ((2 * code_bits - 1).astype(F32) * CODE ** (-0.5)).astype(BF16)

    ins = {
        "gain": Item(norm_gain),
        "shift": Item(norm_shift),
        "query_value": Item(query_value_bias),
        "output_bias": Item(output_bias),
        "shrink_bias": Item(shrink_bias),
        "decode_bias": Item(decode_bias.reshape(1, fine)),
        "expand_bias": Item(expand_bias),
        "encode": Item(encode_weight),
        "decode": Item(decode_weight),
    }
    weights = {"project": project_weight, "output": output_weight, "expand": expand_weight, "shrink": shrink_weight}
    for name, array in (("signs", signs), ("patches", patches), *weights.items()):
        ins[name] = anywhere(array)
    outs = {
        "table": anywhere(shaped((slots, parts, 64, fine), F32)),
        "signs": anywhere(shaped((parts, rows, CODE))),
        "patches": anywhere(shaped((parts, rows, width))),
    }
    for name, array in weights.items():
        outs[name] = anywhere(shaped((slots, parts) + array.shape[1:]))
    scratch = {
        "table": pltpu.VMEM((64, fine), F32),
        "gather": Gather.scratch(5),
        "line": Line.scratch(2),
        "keep": DMA((2,)),
    }
    first = run(first_kernel, 1, ins, outs, scratch, 0, "first_gather", 70)

    small = first["table"].reshape(devices, 64, fine)
    table = small.transpose(1, 0, 2).reshape(64, width)
    expand_shifts = small[:, 17:25].reshape(devices, 2, 4, fine).transpose(1, 0, 2, 3).reshape(2, 1, hidden)
    around = jnp.arange(parts) ^ z
    pieces = segments[0].reshape(parts, rows)[around]
    segment_row = pieces.reshape(1, parts * rows)
    segment_column = pieces[0].reshape(rows, 1)

    def flat(array):
        return array.reshape(-1, array.shape[-1])

    def forward(layer, pieces, weight, extra, collective):
        ins = {
            "pieces": Item(pieces),
            "table": Item(table),
            "weight": Item(weight),
            "segment_row": Item(segment_row),
            "segment_column": Item(segment_column),
        }
        return forward_attention(layer == 1, layer, slots, ins, extra, collective)

    def middle(layer, stream, other, ahead, weights, extra, collective):
        ins = {
            "stream": Item(stream),
            "mixed": Item(ahead["mixed"]),
            "other": Item(other),
            "logs": Item(ahead["logs"]),
            "qkv": anywhere(ahead["qkv"]),
            "table": Item(table),
            "output": Item(weights["output"]),
            "expand": Item(weights["expand"]),
            "expand_shift": Item(expand_shifts[layer]),
            "shrink": Item(weights["shrink"]),
            "segment_row": Item(segment_row),
            "segment_column": Item(segment_column),
        }
        return middle_block(layer == 0, layer, slots, ins, extra, collective)

    def projection(layer, stream, ahead, between, weight, extra, collective, **more):
        ins = {
            "query": Item(between["query"]),
            "key": Item(between["key"]),
            "value": Item(between["value"]),
            "normed": Item(ahead["normed"]),
            "stream": Item(stream),
            "middle": Item(between["middle"]),
            "table": Item(table),
            "weight": Item(weight),
        }
        ins.update({k: Item(v) for k, v in more.items()})
        return projection_back(layer == 1, layer, slots, ins, extra, collective)

    decoder = {n: flat(first[n]) for n in weights}
    beside = Beside(slots, {n: (weights[n], 0) for n in ("project", "output")}, (0, 2, 4, 5, 7, 8))
    ahead1 = forward(1, first["signs"], decoder["project"], beside, 1)
    encoder = {n: flat(ahead1["gathered_" + n]) for n in ("project", "output")}

    beside = Beside(slots, {n: (weights[n], 0) for n in ("expand", "shrink")}, (0, 3, 6, 9, 14, 18))
    stream1 = ahead1["stream"][None]
    between1 = middle(1, stream1, cotangent[0], ahead1, decoder, beside, 2)
    encoder.update({n: flat(between1["gathered_" + n]) for n in ("expand", "shrink")})
    after1 = projection(1, stream1, ahead1, between1, decoder["project"], Nothing(), 3, pieces=first["signs"])

    beside = Beside(
        slots,
        squares={"one": (after1["sums"], 0, 3), "two": (between1["sums"], 0, 4)},
        square_steps={"one": (0, 1, 3, 6), "two": (0, 1, 4, 9)},
    )
    ahead0 = forward(0, first["patches"], encoder["project"], beside, 4)
    beside = Beside(
        slots,
        squares={"three": (between1["sums"], 4, 5)},
        square_steps={"three": (0, 1, 5, 12), "inner": (22, 26)},
        stacks={n: ahead0["total_" + n] for n in ("one", "two")},
        stack_steps={"one": (0, 8), "two": (2, 10)},
        inner=("inner", 9),
    )
    between0 = middle(0, first["patches"], after1["unit_grad"], ahead0, encoder, beside, 5)
    beside = Beside(
        slots,
        stacks={"three": between0["total_three"], "inner": between0["total_inner"]},
        stack_steps={"three": (0, 3), "inner": (0, 3)},
    )
    after0 = projection(0, first["patches"], ahead0, between0, encoder["project"], beside, 6)

    ins = {
        "sums": anywhere(after0["sums"]),
        "in0": Item(after0["small"]),
        "in1": Item(after1["small"]),
        "mid0": Item(between0["small"]),
        "mid1": Item(between1["small"]),
        "wide0": Item(between0["wide"]),
        "wide1": Item(between1["wide"]),
        "code_grad": Item(between0["code_grad"]),
        "decode_grad": Item(after1["decode_grad"]),
    }
    outs = {"units": Item(shaped((3, fine, width), F32)), "table": Item(shaped((64, width), F32))}
    scratch = {
        "square": Square.scratch(3, (fine, width), True),
        "total": pltpu.VMEM((parts, 3, fine, width), BF16),
        "stack": Stack.scratch(3, (fine, width)),
        "tables": pltpu.VMEM((4, 64, width), F32),
        "arrived": pltpu.VMEM((6, 64, width), F32),
        "sems": DMA((2, 6)),
    }
    last = run(last_kernel, 1, ins, outs, scratch, 7, "last_sums", 30)

    device = slot * parts + z
    mine = lax.dynamic_slice(last["table"], (0, device * fine), (64, fine))
    wide = last["table"][17:25].reshape(2, hidden)
    wide = lax.dynamic_slice(wide, (0, device * (hidden // devices)), (2, hidden // devices))
    decoder_mlp = jnp.concatenate([between0["stacked_two"], after0["stacked_three"]])
    encoder_mlp, encoder_project, decoder_project = after0["stacked_inner"], last["units"], between0["stacked_one"]

    def both(cut):
        return jnp.stack([cut(encoder_mlp), cut(decoder_mlp)])

    def joined(units):
        return units.transpose(1, 0, 2).reshape(fine, units.shape[0] * width)

    return (
        between1["decoded"][None],
        after0["grad"][None],
        mine[0:4].reshape(2, 2, fine),
        mine[4:8].reshape(2, 2, fine),
        jnp.stack([joined(encoder_project), joined(decoder_project)]),
        mine[8:12].reshape(2, 2, fine),
        both(lambda g: g[8]),
        mine[12:14],
        both(lambda g: joined(g[4:8])),
        wide,
        both(lambda g: g[0:4].reshape(4 * fine, width)),
        mine[14:16],
        mine[25:43].T,
        mine[43:61],
        mine[16],
    )


def plain_norm(stream, gains, shifts):
    centre = stream - jnp.mean(stream, axis=-1, keepdims=True)
    spread = jnp.mean(centre * centre, axis=-1, keepdims=True)
    return centre * lax.rsqrt(spread + epsilon) * gains + shifts


def normalize(coded):
    return coded / jnp.sqrt(jnp.sum(coded * coded, axis=-1, keepdims=True) + epsilon)


def gelu_exact(hidden):
    return jax.nn.gelu(hidden, approximate=False)


def gather_weights(shards):
    return (
        lax.all_gather(shards[0], ("slot", "seq"), axis=2, tiled=True),
        lax.all_gather(shards[1], ("slot", "seq"), axis=2, tiled=True),
        lax.all_gather(shards[2], ("slot", "seq"), axis=1, tiled=True),
        lax.all_gather(shards[3], ("slot", "seq"), axis=2, tiled=True),
        lax.all_gather(shards[4], ("slot", "seq"), axis=1, tiled=True),
        lax.all_gather(shards[5], ("slot", "seq"), axis=1, tiled=True),
        lax.all_gather(shards[6], ("slot", "seq"), axis=1, tiled=True),
        lax.all_gather(shards[7], ("slot", "seq"), axis=1, tiled=True),
        lax.all_gather(shards[8], ("slot", "seq"), axis=1, tiled=True),
        lax.all_gather(shards[9], ("slot", "seq"), axis=1, tiled=True),
        lax.all_gather(shards[10], ("slot", "seq"), axis=0, tiled=True),
        lax.all_gather(shards[11], ("slot", "seq"), axis=1, tiled=True),
        lax.all_gather(shards[12], ("slot", "seq"), axis=0, tiled=True),
    )


def segment_mask(segments, offset, block_rows):
    return segments[:, None, offset : offset + block_rows, None] == segments[:, None, None, :]


def scaled_scores(queries, key_rows, same_item):
    scores = jnp.einsum("sqhd,skhd->shqk", queries, key_rows, preferred_element_type=jnp.float32)
    return jnp.where(same_item, scores * HD ** (-0.5), masked_score)


def forward_block(stream, layer, segments):
    (
        gains,
        shifts,
        project,
        query_value,
        output,
        output_shift,
        expand,
        expand_shift,
        shrink,
        shrink_shift,
    ) = layer
    slot_count, row_count, model_width = stream.shape
    seq_parts = lax.axis_size("seq")
    head_width = model_width // seq_parts
    normed = plain_norm(stream, gains[0].astype(jnp.float32), shifts[0].astype(jnp.float32)).astype(
        jnp.bfloat16
    )
    bias_row = jnp.concatenate(
        [query_value[0], jnp.zeros_like(query_value[0]), query_value[1]]
    ).astype(jnp.float32)
    projected = (jnp.dot(normed, project, preferred_element_type=jnp.float32) + bias_row).astype(
        jnp.bfloat16
    )
    split_heads = lax.all_to_all(
        projected.reshape(slot_count, row_count, 3, seq_parts, head_width),
        "seq",
        split_axis=3,
        concat_axis=1,
        tiled=True,
    )
    length = split_heads.shape[1]
    local_heads = head_width // HD
    queries = split_heads[:, :, 0, 0].reshape(slot_count, length, local_heads, HD)
    key_rows = split_heads[:, :, 1, 0].reshape(slot_count, length, local_heads, HD)
    values = split_heads[:, :, 2, 0].reshape(slot_count, length, local_heads, HD)
    block_rows = min(512, length)
    pieces = []
    log_parts = []
    for offset in range(0, length, block_rows):
        scores = scaled_scores(
            queries[:, offset : offset + block_rows],
            key_rows,
            segment_mask(segments, offset, block_rows),
        )
        row_top = jnp.max(scores, axis=-1, keepdims=True)
        raised = jnp.exp(scores - row_top)
        row_total = jnp.sum(raised, axis=-1, keepdims=True)
        probability = (raised / row_total).astype(jnp.bfloat16)
        pieces.append(
            jnp.einsum(
                "shqk,skhd->sqhd", probability, values, preferred_element_type=jnp.float32
            ).astype(jnp.bfloat16)
        )
        log_parts.append(row_top + jnp.log(row_total))
    log_sums = jnp.concatenate(log_parts, axis=2)
    attended = jnp.concatenate(pieces, axis=1).reshape(slot_count, length, 1, head_width)
    mixed_rows = lax.all_to_all(attended, "seq", split_axis=1, concat_axis=2, tiled=True).reshape(
        slot_count, row_count, model_width
    )
    middle = (
        stream
        + jnp.dot(mixed_rows, output, preferred_element_type=jnp.float32)
        + output_shift.astype(jnp.float32)
    )
    normed_mid = plain_norm(
        middle, gains[1].astype(jnp.float32), shifts[1].astype(jnp.float32)
    ).astype(jnp.bfloat16)
    hidden = jnp.dot(normed_mid, expand, preferred_element_type=jnp.float32) + expand_shift.astype(
        jnp.float32
    )
    active = gelu_exact(hidden).astype(jnp.bfloat16)
    result = (
        middle
        + jnp.dot(active, shrink, preferred_element_type=jnp.float32)
        + shrink_shift.astype(jnp.float32)
    )
    saved_values = (
        normed,
        queries,
        key_rows,
        values,
        log_sums,
        mixed_rows,
        middle,
        normed_mid,
        hidden,
        active,
    )
    return (result, saved_values)


def backward_block(grad_out, stream, saved_values, layer, segments):
    (
        gains,
        shifts,
        project,
        query_value,
        output,
        output_shift,
        expand,
        expand_shift,
        shrink,
        shrink_shift,
    ) = layer
    normed, queries, key_rows, values, log_sums, mixed_rows, middle, normed_mid, hidden, active = (
        saved_values
    )
    slot_count, row_count, model_width = stream.shape
    seq_parts = lax.axis_size("seq")
    head_width = model_width // seq_parts
    branch = grad_out.astype(jnp.bfloat16)
    shrink_shift_grad = jnp.sum(branch, axis=(0, 1), dtype=jnp.float32)
    shrink_grad = jnp.einsum("stf,sto->fo", active, branch, preferred_element_type=jnp.float32)
    active_grad = jnp.einsum("sto,fo->stf", branch, shrink, preferred_element_type=jnp.float32)
    unused, gelu_back = jax.vjp(gelu_exact, hidden)
    hidden_low = gelu_back(active_grad)[0].astype(jnp.bfloat16)
    expand_shift_grad = jnp.sum(hidden_low, axis=(0, 1), dtype=jnp.float32)
    expand_grad = jnp.einsum(
        "sti,stf->if", normed_mid, hidden_low, preferred_element_type=jnp.float32
    )
    normed_mid_grad = jnp.einsum(
        "stf,if->sti", hidden_low, expand, preferred_element_type=jnp.float32
    )
    unused, norm_back = jax.vjp(
        plain_norm, middle, gains[1].astype(jnp.float32), shifts[1].astype(jnp.float32)
    )
    middle_part, gain_mid_grad, shift_mid_grad = norm_back(normed_mid_grad)
    middle_grad = grad_out + middle_part
    branch_low = middle_grad.astype(jnp.bfloat16)
    output_shift_grad = jnp.sum(branch_low, axis=(0, 1), dtype=jnp.float32)
    output_grad = jnp.einsum(
        "sti,sto->io", mixed_rows, branch_low, preferred_element_type=jnp.float32
    )
    mixed_low = jnp.einsum(
        "sto,io->sti", branch_low, output, preferred_element_type=jnp.float32
    ).astype(jnp.bfloat16)
    head_grad = lax.all_to_all(
        mixed_low.reshape(slot_count, row_count, seq_parts, head_width),
        "seq",
        split_axis=2,
        concat_axis=1,
        tiled=True,
    )
    length = head_grad.shape[1]
    local_heads = head_width // HD
    head_grad = head_grad.reshape(slot_count, length, local_heads, HD)
    scale_factor = HD ** (-0.5)
    block_rows = min(512, length)
    key_grad = jnp.zeros((slot_count, length, local_heads, HD), jnp.float32)
    value_grad = jnp.zeros((slot_count, length, local_heads, HD), jnp.float32)
    query_parts = []
    for offset in range(0, length, block_rows):
        query_block = queries[:, offset : offset + block_rows]
        scores = scaled_scores(query_block, key_rows, segment_mask(segments, offset, block_rows))
        probability = jnp.exp(scores - log_sums[:, :, offset : offset + block_rows])
        out_grad = head_grad[:, offset : offset + block_rows]
        value_grad = value_grad + jnp.einsum(
            "shqk,sqhd->skhd",
            probability.astype(jnp.bfloat16),
            out_grad,
            preferred_element_type=jnp.float32,
        )
        prob_grad = jnp.einsum(
            "sqhd,skhd->shqk", out_grad, values, preferred_element_type=jnp.float32
        )
        centre = jnp.sum(probability * prob_grad, axis=-1, keepdims=True)
        score_low = (probability * (prob_grad - centre)).astype(jnp.bfloat16)
        query_parts.append(
            jnp.einsum("shqk,skhd->sqhd", score_low, key_rows, preferred_element_type=jnp.float32)
            * scale_factor
        )
        key_grad = (
            key_grad
            + jnp.einsum(
                "shqk,sqhd->skhd", score_low, query_block, preferred_element_type=jnp.float32
            )
            * scale_factor
        )
    query_grad = jnp.concatenate(query_parts, axis=1)
    joined = (
        jnp.stack([query_grad, key_grad, value_grad], axis=2)
        .astype(jnp.bfloat16)
        .reshape(slot_count, length, 3, 1, head_width)
    )
    project_low = lax.all_to_all(joined, "seq", split_axis=1, concat_axis=3, tiled=True).reshape(
        slot_count, row_count, 3 * model_width
    )
    project_shift = jnp.sum(project_low, axis=(0, 1), dtype=jnp.float32)
    query_value_grad = jnp.stack([project_shift[:model_width], project_shift[2 * model_width :]])
    project_grad = jnp.einsum(
        "sti,stj->ij", normed, project_low, preferred_element_type=jnp.float32
    )
    normed_grad = jnp.einsum(
        "stj,ij->sti", project_low, project, preferred_element_type=jnp.float32
    )
    unused, norm_back = jax.vjp(
        plain_norm, stream, gains[0].astype(jnp.float32), shifts[0].astype(jnp.float32)
    )
    stream_part, gain_in_grad, shift_in_grad = norm_back(normed_grad)
    input_part = middle_grad + stream_part
    grads = (
        jnp.stack([gain_in_grad, gain_mid_grad]),
        jnp.stack([shift_in_grad, shift_mid_grad]),
        project_grad,
        query_value_grad,
        output_grad,
        output_shift_grad,
        expand_grad,
        expand_shift_grad,
        shrink_grad,
        shrink_shift_grad,
    )
    return (input_part, grads)


def plain_device(
    patches,
    segments,
    code_bits,
    norm_gain,
    norm_shift,
    project_weight,
    query_value_bias,
    output_weight,
    output_bias,
    expand_weight,
    expand_bias,
    shrink_weight,
    shrink_bias,
    encode_weight,
    decode_weight,
    decode_bias,
    cotangent,
):
    shards = (
        norm_gain,
        norm_shift,
        project_weight,
        query_value_bias,
        output_weight,
        output_bias,
        expand_weight,
        expand_bias,
        shrink_weight,
        shrink_bias,
        encode_weight,
        decode_weight,
        decode_bias,
    )
    gathered = gather_weights(shards)
    stream_in = patches.astype(jnp.float32)
    encoded, unused = forward_block(
        stream_in, tuple((array[0] for array in gathered[:10])), segments
    )
    encoded_low = encoded.astype(jnp.bfloat16)
    coded = jnp.einsum("sti,ic->stc", encoded_low, gathered[10], preferred_element_type=jnp.float32)
    signs = ((2 * code_bits - 1).astype(jnp.float32) * CODE ** (-0.5)).astype(jnp.bfloat16)
    start = jnp.einsum(
        "stc,ci->sti", signs, gathered[11], preferred_element_type=jnp.float32
    ) + gathered[12].astype(jnp.float32)
    decoded, decoder_saved = forward_block(
        start, tuple((array[1] for array in gathered[:10])), segments
    )
    weights_back = gather_weights(shards)
    encoder = tuple((array[0] for array in weights_back[:10]))
    decoder = tuple((array[1] for array in weights_back[:10]))
    start_grad, decoder_grads = backward_block(
        cotangent.astype(jnp.float32), start, decoder_saved, decoder, segments
    )
    start_low = start_grad.astype(jnp.bfloat16)
    decode_bias_grad = jnp.sum(start_low, axis=(0, 1), dtype=jnp.float32)
    decode_grad = jnp.einsum("stc,sti->ci", signs, start_low, preferred_element_type=jnp.float32)
    unit_grad = jnp.einsum(
        "sti,ci->stc", start_low, weights_back[11], preferred_element_type=jnp.float32
    )
    unit_rows, unit_back = jax.vjp(normalize, coded)
    coded_low = unit_back(unit_grad)[0].astype(jnp.bfloat16)
    encode_grad = jnp.einsum(
        "sti,stc->ic", encoded_low, coded_low, preferred_element_type=jnp.float32
    )
    encoded_grad = jnp.einsum(
        "stc,ic->sti", coded_low, weights_back[10], preferred_element_type=jnp.float32
    )
    unused, encoder_saved = forward_block(stream_in, encoder, segments)
    input_grad, encoder_grads = backward_block(
        encoded_grad, stream_in, encoder_saved, encoder, segments
    )
    pairs = tuple(
        (jnp.stack([first, second]) for first, second in zip(encoder_grads, decoder_grads))
    )
    totals = (
        lax.psum_scatter(pairs[0], ("slot", "seq"), scatter_dimension=2, tiled=True),
        lax.psum_scatter(pairs[1], ("slot", "seq"), scatter_dimension=2, tiled=True),
        lax.psum_scatter(pairs[2], ("slot", "seq"), scatter_dimension=1, tiled=True),
        lax.psum_scatter(pairs[3], ("slot", "seq"), scatter_dimension=2, tiled=True),
        lax.psum_scatter(pairs[4], ("slot", "seq"), scatter_dimension=1, tiled=True),
        lax.psum_scatter(pairs[5], ("slot", "seq"), scatter_dimension=1, tiled=True),
        lax.psum_scatter(pairs[6], ("slot", "seq"), scatter_dimension=1, tiled=True),
        lax.psum_scatter(pairs[7], ("slot", "seq"), scatter_dimension=1, tiled=True),
        lax.psum_scatter(pairs[8], ("slot", "seq"), scatter_dimension=1, tiled=True),
        lax.psum_scatter(pairs[9], ("slot", "seq"), scatter_dimension=1, tiled=True),
        lax.psum_scatter(encode_grad, ("slot", "seq"), scatter_dimension=0, tiled=True),
        lax.psum_scatter(decode_grad, ("slot", "seq"), scatter_dimension=1, tiled=True),
        lax.psum_scatter(decode_bias_grad, ("slot", "seq"), scatter_dimension=0, tiled=True),
    )
    return (decoded.astype(jnp.bfloat16), input_grad) + tuple(totals)


def solution(mesh):
    in_specs = (
        P("slot", "seq", None),
        P("slot", None),
        P("slot", "seq", None),
        P(None, None, ("slot", "seq")),
        P(None, None, ("slot", "seq")),
        P(None, ("slot", "seq"), None),
        P(None, None, ("slot", "seq")),
        P(None, ("slot", "seq"), None),
        P(None, ("slot", "seq")),
        P(None, ("slot", "seq"), None),
        P(None, ("slot", "seq")),
        P(None, ("slot", "seq"), None),
        P(None, ("slot", "seq")),
        P(("slot", "seq"), None),
        P(None, ("slot", "seq")),
        P(("slot", "seq")),
        P("slot", "seq", None),
    )
    out_specs = (
        P("slot", "seq", None),
        P("slot", "seq", None),
        P(None, None, ("slot", "seq")),
        P(None, None, ("slot", "seq")),
        P(None, ("slot", "seq"), None),
        P(None, None, ("slot", "seq")),
        P(None, ("slot", "seq"), None),
        P(None, ("slot", "seq")),
        P(None, ("slot", "seq"), None),
        P(None, ("slot", "seq")),
        P(None, ("slot", "seq"), None),
        P(None, ("slot", "seq")),
        P(("slot", "seq"), None),
        P(None, ("slot", "seq")),
        P(("slot", "seq")),
    )
    return jax.shard_map(
        on_device, mesh=mesh, in_specs=in_specs, out_specs=out_specs, check_vma=False
    )
```

```python
import functools

import jax
import jax.numpy as jnp
from jax import lax
from jax.experimental import pallas as pl
from jax.experimental.pallas import tpu as pltpu
from jax.sharding import PartitionSpec as P

HD = 64
CODE = 18
epsilon = 1e-06
masked_score = -1000000000.0
MESH = pl.DeviceIdType.MESH
F32 = jnp.float32
BF16 = jnp.bfloat16
AXES = ("slot", "seq")
BIG = 60 * 1024 * 1024

NN = (((1,), (0,)), ((), ()))
NT = (((1,), (1,)), ((), ()))
TN = (((0,), (0,)), ((), ()))


def mm(a, b, dims=NN):
    return lax.dot_general(a, b, dims, preferred_element_type=F32)


def params(**more):
    return pltpu.CompilerParams(vmem_limit_bytes=BIG, **more)


def whole(shape):
    return pl.BlockSpec(shape, lambda *i: (0,) * len(shape))


def shaped(shape, dtype=BF16):
    return jax.ShapeDtypeStruct(shape, dtype)


def norm_parts(stream):
    centre = stream - jnp.mean(stream, axis=-1, keepdims=True)
    spread = jnp.mean(centre * centre, axis=-1, keepdims=True)
    scale = lax.rsqrt(spread + epsilon)
    return centre * scale, scale


def norm_back(grad, gain, hat, scale):
    lifted = grad * gain
    mean = jnp.mean(lifted, axis=-1, keepdims=True)
    mixed = jnp.mean(lifted * hat, axis=-1, keepdims=True)
    return scale * (lifted - mean - hat * mixed)


def columns(value):
    return jnp.sum(value, axis=0, keepdims=True)


def lanes_of(head):
    lane = lax.broadcasted_iota(jnp.int32, (1, 2 * HD), 1)
    return lane < HD if head == 0 else lane >= HD


def only(value, head):
    return jnp.where(lanes_of(head), value, jnp.zeros_like(value))


def gelu_parts(hidden):
    normal = 0.5 + 0.5 * lax.erf(hidden * 0.7071067811865476)
    density = jnp.exp(-0.5 * hidden * hidden) * 0.3989422804014327
    return hidden * normal, normal + hidden * density


def flip(index, bit):
    size = 1 << bit
    return index + size - 2 * size * ((index // size) % 2)


def relative(a, b):
    return 2 * ((a // 2 + b // 2) % 2) + (a + b) % 2


PARTS = 4
DMA = pltpu.SemaphoreType.DMA


def remote(src, dst, send, recv, peer):
    return pltpu.make_async_remote_copy(
        src_ref=src, dst_ref=dst, send_sem=send, recv_sem=recv, device_id=peer, device_id_type=MESH
    )


class Here:
    def __init__(self):
        self.slot, self.z = lax.axis_index("slot"), lax.axis_index("seq")
        self.across = (flip(self.slot, 1), self.z)
        self.beside = (flip(self.slot, 2), self.z)
        self.sibling = (flip(self.slot, 0), self.z)
        self.core, self.square = lax.rem(self.slot, 2), self.slot // 2

    def along(self, k):
        return (self.slot, relative(self.z, k))

    def greet(self):
        barrier = pltpu.get_barrier_semaphore()
        peers = [self.across, self.beside, self.sibling] + [self.along(k) for k in range(1, PARTS)]
        for peer in peers:
            pl.semaphore_signal(barrier, inc=1, device_id=peer, device_id_type=MESH)
        pl.semaphore_wait(barrier, len(peers))


class Line:
    @staticmethod
    def scratch(count):
        return [DMA((count, PARTS))] * 3

    def __init__(self, here, arrays, sems, sources=None):
        self.here, self.arrays, self.sources = here, arrays, sources
        self.recv, self.up, self.down = sems

    def at(self, m, block, z):
        return self.arrays[m].at[relative(block, z) if self.sources is None else block]

    def copy(self, m, block, upward):
        z = self.here.z
        to = jnp.minimum(z + 1, PARTS - 1) if upward else jnp.maximum(z - 1, 0)
        send = (self.up if upward else self.down).at[m, block]
        src = self.sources[m] if self.sources is not None and block is z else self.at(m, block, z)
        return remote(src, self.at(m, block, to), send, self.recv.at[m, block], (self.here.slot, to))

    def onward(self, m, block, upward):
        z = self.here.z

        @pl.when((z < PARTS - 1) if upward else (z > 0))
        def _():
            self.copy(m, block, upward).start()

    def start(self, m):
        self.onward(m, self.here.z, True)
        self.onward(m, self.here.z, False)

    def hop(self, m, k):
        z = self.here.z

        @pl.when(z >= k)
        def _():
            self.copy(m, z - k, True).wait_recv()
            self.onward(m, z - k, True)

        @pl.when(z + k <= PARTS - 1)
        def _():
            self.copy(m, z + k, False).wait_recv()
            self.onward(m, z + k, False)

    def finish(self, m):
        z = self.here.z
        for block in range(PARTS):

            @pl.when((z < PARTS - 1) & (z >= block))
            def _():
                self.copy(m, block, True).wait_send()

            @pl.when((z > 0) & (z <= block))
            def _():
                self.copy(m, block, False).wait_send()


class Gather:
    @staticmethod
    def scratch(count):
        return [DMA((count, PARTS))] * 5 + [DMA((count,))] * 8

    def __init__(self, here, sources, outs, sems):
        self.here, self.sources, self.outs = here, sources, outs
        self.rz, self.up, self.down, self.rx, self.ry = sems[:5]
        self.local, self.sx, self.sy, self.rd, self.dx, self.dy, self.rc, self.sc = sems[5:]

    def place(self, m, block):
        return self.outs[m].at[self.here.slot, block]

    def copy(self, m, block, upward, src):
        z = self.here.z
        to = jnp.minimum(z + 1, PARTS - 1) if upward else jnp.maximum(z - 1, 0)
        send = (self.up if upward else self.down).at[m, block]
        return remote(src, self.place(m, block), send, self.rz.at[m, block], (self.here.slot, to))

    def onward(self, m, block, upward, src):
        z = self.here.z

        @pl.when((z < PARTS - 1) if upward else (z > 0))
        def _():
            self.copy(m, block, upward, src).start()

    def sideways(self, m, block, src):
        dst = self.place(m, block)
        remote(src, dst, self.sx.at[m], self.rx.at[m, block], self.here.across).start()
        remote(src, dst, self.sy.at[m], self.ry.at[m, block], self.here.beside).start()

    def keep(self, m):
        return pltpu.make_async_copy(self.sources[m], self.place(m, self.here.z), self.local.at[m])

    def start(self, m):
        src, z = self.sources[m], self.here.z
        self.onward(m, z, True, src)
        self.onward(m, z, False, src)
        self.sideways(m, z, src)
        self.keep(m).start()

    def arrived(self, m, block, upward):
        src = self.place(m, block)
        self.copy(m, block, upward, src).wait_recv()
        self.onward(m, block, upward, src)
        self.sideways(m, block, src)

    def hop(self, m, k):
        z = self.here.z

        @pl.when(z >= k)
        def _():
            self.arrived(m, z - k, True)

        @pl.when(z + k <= PARTS - 1)
        def _():
            self.arrived(m, z + k, False)

    def turned(self, m, block):
        across, beside = self.here.across, self.here.beside
        here = self.outs[m].at[across[0], block]
        remote(here, here, self.sx.at[m], self.rx.at[m, block], across).wait_recv()

        @pl.when(lax.rem(block, 2) == 0)
        def _():
            remote(here, here, self.dy.at[m], self.rd.at[m], beside).start()

        there = self.outs[m].at[beside[0], block]
        remote(there, there, self.sy.at[m], self.ry.at[m, block], beside).wait_recv()

        @pl.when(lax.rem(block, 2) == 1)
        def _():
            remote(there, there, self.dx.at[m], self.rd.at[m], across).start()

    def turn(self, m, k):
        z = self.here.z
        if k == 0:
            self.turned(m, z)
            return

        @pl.when(z >= k)
        def _():
            self.turned(m, z - k)

        @pl.when(z + k <= PARTS - 1)
        def _():
            self.turned(m, z + k)

    def share(self, m, slot):
        group = self.outs[m].at[slot]
        remote(group, group, self.sc.at[m], self.rc.at[m], self.here.sibling).start()

    def siblings(self, m):
        self.keep(m).wait()
        for slot in (self.here.slot, self.here.across[0], self.here.beside[0]):
            self.share(m, slot)

    def corner(self, m):
        slot = flip(self.here.across[0], 2)
        group = self.outs[m].at[slot]
        remote(group, group, self.dx.at[m], self.rd.at[m], self.here.across).wait_recv()
        self.share(m, slot)

    def finish(self, m):
        here, z, src = self.here, self.here.z, self.sources[m]
        for block in range(PARTS):

            @pl.when((z < PARTS - 1) & (z >= block))
            def _():
                self.copy(m, block, True, src).wait_send()

            @pl.when((z > 0) & (z <= block))
            def _():
                self.copy(m, block, False, src).wait_send()

        group = self.outs[m].at[here.slot]
        half = self.outs[m].at[here.slot, pl.ds(0, PARTS // 2)]
        remote(group, group, self.sx.at[m], self.rx.at[m, 0], here.across).wait_send()
        remote(group, group, self.sy.at[m], self.ry.at[m, 0], here.beside).wait_send()
        remote(half, half, self.dx.at[m], self.rd.at[m], here.across).wait_send()
        remote(half, half, self.dy.at[m], self.rd.at[m], here.beside).wait_send()
        four = self.outs[m].at[pl.ds(0, 4)]
        both = remote(four, four, self.sc.at[m], self.rc.at[m], here.sibling)
        both.wait_send()
        both.wait_recv()


class Spread:
    @staticmethod
    def scratch(count):
        return [DMA((11, count))]

    def __init__(self, here, sources, outs, sems):
        self.here, self.sources, self.outs, self.sems = here, sources, outs, sems[0]

    def sem(self, m, n):
        return self.sems.at[n, m]

    def keep(self, m):
        return pltpu.make_async_copy(self.sources[m], self.outs[m].at[self.here.slot], self.sem(m, 0))

    def share(self, m, src, slot):
        remote(src, self.outs[m].at[slot], self.sem(m, 1), self.sem(m, 2), self.here.sibling).start()

    def side(self, m, n, src, slot):
        peer = self.here.beside if n else self.here.across
        return remote(src, self.outs[m].at[slot], self.sem(m, 3 + 2 * n), self.sem(m, 4 + 2 * n), peer)

    def half(self, m, n, slot):
        ref = self.outs[m].at[slot, pl.ds(n * (PARTS // 2), PARTS // 2)]
        peer = self.here.across if n else self.here.beside
        return remote(ref, ref, self.sem(m, 7 + 2 * n), self.sem(m, 8 + 2 * n), peer)

    def start(self, m):
        src, slot = self.sources[m], self.here.slot
        for n in range(2):
            self.side(m, n, src, slot).start()
        self.keep(m).start()
        self.share(m, src, slot)

    def turn(self, m):
        for n, peer in enumerate((self.here.across, self.here.beside)):
            ref = self.outs[m].at[peer[0]]
            self.side(m, n, ref, peer[0]).wait_recv()
            self.half(m, n, peer[0]).start()
            self.share(m, ref, peer[0])

    def corner(self, m):
        slot = flip(self.here.across[0], 2)
        for n in range(2):
            self.half(m, n, slot).wait_recv()
        self.share(m, self.outs[m].at[slot], slot)

    def finish(self, m):
        self.keep(m).wait()
        for n in range(2):
            self.side(m, n, self.sources[m], self.here.slot).wait_send()
            self.half(m, n, self.here.slot).wait_send()
        four = self.outs[m].at[pl.ds(0, 4)]
        both = remote(four, four, self.sem(m, 1), self.sem(m, 2), self.here.sibling)
        both.wait_send()
        both.wait_recv()


def add_into(target, source):
    rows, units = target.shape[:2]

    def one(i, carry):
        a, b = i // units, lax.rem(i, units)
        target[a, b] = (target[a, b].astype(F32) + source[a, b].astype(F32)).astype(target.dtype)
        return carry

    lax.fori_loop(0, rows * units, one, 0)


class Square:
    @staticmethod
    def scratch(units, tail, loaded):
        held = [pltpu.VMEM((4, PARTS, units) + tail, BF16)] if loaded else []
        half = pltpu.VMEM((PARTS // 2, units) + tail, BF16)
        full = pltpu.VMEM((PARTS, units) + tail, BF16)
        return held + [half, half, full, full, DMA((9,))]

    def __init__(self, here, held, scratch, source=None):
        self.here, self.held, self.source = here, held, source
        self.corner_x, self.corner_y, self.side_x, self.side_y, self.sems = scratch

    def load(self, start=True):
        copy = pltpu.make_async_copy(self.source, self.held, self.sems.at[8])
        copy.start() if start else copy.wait()

    def move(self, n):
        half, held, sems = PARTS // 2, self.held, self.sems
        src = (held.at[3, pl.ds(0, half)], held.at[3, pl.ds(half, half)], held.at[1], held.at[2])[n]
        dst = (self.corner_x, self.corner_y, self.side_x, self.side_y)[n]
        peer = self.here.beside if n % 2 else self.here.across
        return remote(src, dst, sems.at[2 * n], sems.at[2 * n + 1], peer)

    def start(self):
        if self.source is not None:
            self.load(False)
        for n in range(2):
            self.move(n).start()

    def sides(self):
        half = PARTS // 2
        self.move(0).wait_recv()
        add_into(self.held.at[2, pl.ds(0, half)], self.corner_x)
        self.move(3).start()
        self.move(1).wait_recv()
        add_into(self.held.at[1, pl.ds(half, half)], self.corner_y)
        self.move(2).start()

    def total(self, out):
        self.move(2).wait_recv()
        self.move(3).wait_recv()
        units = out.shape[1]

        def one(i, carry):
            a, b = i // units, lax.rem(i, units)
            value = self.held[0, a, b].astype(F32) + self.side_x[a, b].astype(F32) + self.side_y[a, b].astype(F32)
            out[a, b] = value.astype(out.dtype)
            return carry

        lax.fori_loop(0, PARTS * units, one, 0)
        for n in range(4):
            self.move(n).wait_send()


class Stack:
    @staticmethod
    def scratch(units, tail):
        return [pltpu.VMEM((PARTS - 1, units) + tail, BF16), DMA((2, PARTS))]

    def __init__(self, here, held, scratch):
        self.here, self.held = here, held
        self.arrived, self.sems = scratch

    def moves(self):
        for k in range(1, PARTS):
            peer = self.here.along(k)
            yield remote(self.held.at[peer[1]], self.arrived.at[k - 1], self.sems.at[0, k], self.sems.at[1, k], peer)

    def start(self):
        for move in self.moves():
            move.start()

    def finish(self, out):
        for move in self.moves():
            move.wait_recv()
        units, z = out.shape[0], self.here.z

        def one(unit, carry):
            value = self.held[z, unit].astype(F32)
            for k in range(PARTS - 1):
                value += self.arrived[k, unit].astype(F32)
            out[unit] = value
            return carry

        lax.fori_loop(0, units, one, 0)
        for move in self.moves():
            move.wait_send()


class Sum:
    @staticmethod
    def scratch(rows, width):
        table, low = pltpu.VMEM((4, rows, width), F32), pltpu.VMEM((rows, width), BF16)
        return [table, pltpu.VMEM((3, rows, width), F32), low, pltpu.VMEM((PARTS - 1, rows, width), BF16), DMA((2, 6))]

    def __init__(self, here, sources, scratch):
        self.here, self.sources = here, sources
        self.tables, self.arrived, self.low, self.arrived_low, self.sems = scratch
        self.peers = (here.sibling, here.across, here.beside)

    def move(self, stage):
        sems = self.sems
        return remote(self.tables.at[stage], self.arrived.at[stage], sems.at[0, stage], sems.at[1, stage], self.peers[stage])

    def stack(self, k):
        sems = self.sems
        return remote(self.low, self.arrived_low.at[k - 1], sems.at[0, 2 + k], sems.at[1, 2 + k], self.here.along(k))

    def begin(self):
        tables = self.tables
        tables[0] = jnp.zeros_like(tables[0])
        width = tables.shape[2]
        at = 0
        for source in self.sources:
            rows, columns_held = source.shape
            for start in range(0, columns_held, width):
                tables[0, at : at + rows, :] = source[:, start : start + width]
                at += rows
        self.move(0).start()

    def meet(self, stage):
        self.move(stage).wait_recv()
        self.tables[stage + 1] = self.tables[stage] + self.arrived[stage]
        if stage < 2:
            self.move(stage + 1).start()
        else:
            self.low[...] = self.tables[3].astype(BF16)
            for k in range(1, PARTS):
                self.stack(k).start()

    def finish(self, out):
        value = self.tables[3]
        for k in range(1, PARTS):
            self.stack(k).wait_recv()
            value += self.arrived_low[k - 1].astype(F32)
        out[...] = value
        for stage in range(3):
            self.move(stage).wait_send()
        for k in range(1, PARTS):
            self.stack(k).wait_send()


class Cores:
    @staticmethod
    def scratch(units, tail):
        return [pltpu.VMEM((4, PARTS, units) + tail, BF16), pltpu.VMEM((2, 8, PARTS) + tail, BF16), DMA((units,)), DMA((units,))]

    def __init__(self, here, sums, scratch, hidden):
        self.here, self.sums, self.hidden = here, sums, hidden
        self.far, self.turn, self.send, self.recv = scratch

    def moves(self, n, hidden):
        here, slot = self.here, lax.rem(n, 2)
        give = 1 - here.core
        if hidden:
            to = self.far.at[relative(here.square, n), :, pl.ds(0, self.hidden)]
            return [(self.turn.at[slot, pl.ds(4 * give, 4)], to)], to
        pairs = [(self.turn.at[slot, 2 * s + give], self.far.at[relative(here.square, s), :, n]) for s in range(4)]
        return pairs, self.far.at[:, :, n]

    def each(self, n, action):
        if self.hidden:

            @pl.when(n < self.hidden)
            def _():
                action(True)

            @pl.when(n >= self.hidden)
            def _():
                action(False)
        else:
            action(False)

    def waited(self, n, hidden, recv):
        whole_ref = self.moves(n, hidden)[1]
        move = remote(whole_ref, whole_ref, self.send.at[n], self.recv.at[n], self.here.sibling)
        move.wait_recv() if recv else move.wait_send()

    def put(self, n, value):
        here, slot = self.here, lax.rem(n, 2)

        @pl.when(n >= 2)
        def _():
            self.each(n - 2, lambda hidden: self.waited(n - 2, hidden, False))

        self.turn[slot] = value.reshape(self.turn.shape[1:]).astype(BF16)

        def action(hidden):
            for src, dst in self.moves(n, hidden)[0]:
                remote(src, dst, self.send.at[n], self.recv.at[n], here.sibling).start()
            if hidden:
                self.sums[relative(here.square, n), :, pl.ds(0, self.hidden)] = self.turn[slot, pl.ds(4 * here.core, 4)]
            else:
                for s in range(4):
                    self.sums[relative(here.square, s), :, n] = self.turn[slot, 2 * s + here.core]

        self.each(n, action)

    def collect(self, n):
        def action(hidden):
            self.waited(n, hidden, True)
            if hidden:
                at = relative(self.here.square, n)
                add_into(self.sums.at[at, :, pl.ds(0, self.hidden)], self.far.at[at, :, pl.ds(0, self.hidden)])
            else:
                for s in range(4):

                    def one(a, carry):
                        value = self.sums[s, a, n].astype(F32) + self.far[s, a, n].astype(F32)
                        self.sums[s, a, n] = value.astype(BF16)
                        return carry

                    lax.fori_loop(0, PARTS, one, 0)

        self.each(n, action)

    def finish(self, count):
        for n in (count - 2, count - 1):
            self.waited(n, n < self.hidden, False)


class Item:
    def __init__(self, array, spec=None):
        self.array = array
        self.spec = spec or whole(array.shape)


def anywhere(array):
    return Item(array, pl.BlockSpec(memory_space=pl.ANY))


def run(body, steps, ins, outs, scratch, collective, name, cost):
    in_names, out_names, scratch_names = list(ins), list(outs), list(scratch)
    flat_scratch, spans = [], {}
    for key in scratch_names:
        item = scratch[key]
        many = isinstance(item, list)
        spans[key] = (len(flat_scratch), len(item) if many else None)
        flat_scratch += item if many else [item]

    def kernel(*refs):
        first, second = len(in_names), len(in_names) + len(out_names)
        in_refs = dict(zip(in_names, refs[:first]))
        out_refs = dict(zip(out_names, refs[first:second]))
        rest = refs[second:]
        own = {k: rest[at] if n is None else rest[at : at + n] for k, (at, n) in spans.items()}
        here = Here()
        step = pl.program_id(0)

        @pl.when(step == 0)
        def _():
            here.greet()

        body(here, step, in_refs, out_refs, own)

    results = pl.pallas_call(
        kernel,
        grid=(steps,),
        in_specs=[i.spec for i in ins.values()],
        out_specs=tuple(o.spec for o in outs.values()),
        out_shape=tuple(o.array for o in outs.values()),
        scratch_shapes=flat_scratch,
        compiler_params=pltpu.CompilerParams(
            vmem_limit_bytes=BIG, collective_id=collective, has_side_effects=True, dimension_semantics=("arbitrary",)
        ),
        cost_estimate=pl.CostEstimate(flops=cost * 1150000000, bytes_accessed=0, transcendentals=0),
        name=name,
    )(*[i.array for i in ins.values()])
    return dict(zip(out_names, results))


def at_step(step, n):
    def decorate(action):
        pl.when(step == n)(action)

    return decorate


def first_kernel(here, step, ins, outs, own):
    table = own["table"]
    table[...] = jnp.zeros_like(table)
    gain, shift, query_value = ins["gain"], ins["shift"], ins["query_value"]
    for start, item in ((0, gain), (4, shift), (8, query_value)):
        for i in range(4):
            table[start + i : start + i + 1, :] = item[i // 2, i % 2 : i % 2 + 1, :].astype(F32)
    table[12:14, :] = ins["output_bias"][...].astype(F32)
    table[14:16, :] = ins["shrink_bias"][...].astype(F32)
    table[16:17, :] = ins["decode_bias"][...].astype(F32)
    fine = gain.shape[2]
    wide = ins["expand_bias"][...].astype(F32)
    for i in range(8):
        table[17 + i : 18 + i, :] = wide[i // 4 : i // 4 + 1, fine * (i % 4) : fine * (i % 4 + 1)]
    table[25:43, :] = ins["encode"][...].astype(F32).T
    table[43:61, :] = ins["decode"][...].astype(F32)
    names = ("project", "output", "expand", "shrink")
    gather = Gather(
        here, [table] + [ins[n].at[0] for n in names], [outs["table"]] + [outs[n] for n in names], own["gather"]
    )
    line = Line(here, [outs["signs"], outs["patches"]], own["line"])
    keeps = [
        pltpu.make_async_copy(ins[n].at[0], outs[n].at[0], own["keep"].at[i]) for i, n in enumerate(("signs", "patches"))
    ]
    messages = range(len(names) + 1)
    gather.start(0)
    for keep in keeps:
        keep.start()
    for m in messages[1:]:
        gather.start(m)
    for keep in keeps:
        keep.wait()
    line.start(0)
    for k in range(1, PARTS):
        line.hop(0, k)
        for m in messages:
            gather.hop(m, k)
            gather.turn(m, k - 1)
        if k == 1:
            line.start(1)
        else:
            line.hop(1, k - 1)
    for m in messages:
        gather.turn(m, PARTS - 1)
        gather.siblings(m)
    line.hop(1, PARTS - 1)
    for m in messages:
        gather.corner(m)
    for m in messages:
        gather.finish(m)
    for m in range(2):
        line.finish(m)


def forward_attention(coded, layer, slots, ins, extra, collective):
    pieces, table, weight = ins["pieces"].array, ins["table"].array, ins["weight"].array
    rows = pieces.shape[1]
    width, triple = weight.shape
    length = PARTS * rows
    pairs, lanes = width // (2 * HD), 2 * HD
    steps = PARTS + pairs
    outs = {
        "qkv": Item(shaped((length, triple)), pl.BlockSpec((rows, triple), lambda i: (jnp.minimum(i, PARTS - 1), 0))),
        "normed": Item(shaped((rows, width))),
        "mixed": Item(shaped((rows, width)), pl.BlockSpec((rows, lanes), lambda i: (0, jnp.maximum(i - PARTS, 0)))),
        "logs": Item(shaped((rows, 128), F32)),
    }
    if coded:
        outs["stream"] = Item(shaped((rows, width), F32))
    scratch = {"qkv_held": pltpu.VMEM((length, triple), BF16)}
    extra.declare(ins, outs, scratch)

    def body(here, step, ins, outs, own):
        extra.events(here, step, steps, ins, outs, own)
        table = ins["table"]
        held = own["qkv_held"]

        @pl.when(step < PARTS)
        def _():
            if coded:
                decode = table[43:61, :].astype(BF16)
                stream = mm(ins["pieces"][step], decode) + table[16:17, :]
            else:
                stream = ins["pieces"][step].astype(F32)
            hat, unused = norm_parts(stream)
            normed = (hat * table[2 * layer : 2 * layer + 1, :] + table[4 + 2 * layer : 5 + 2 * layer, :]).astype(BF16)
            at = pl.ds(pl.multiple_of(step * rows, rows), rows)
            for part in range(3):
                span = pl.ds(part * width, width)
                value = mm(normed, ins["weight"][:, span])
                if part != 1:
                    shift = 8 + 2 * layer + part // 2
                    value += table[shift : shift + 1, :]
                value = value.astype(BF16)
                outs["qkv"][:, span] = value
                held[at, span] = value

            @pl.when(step == 0)
            def _():
                outs["normed"][...] = normed
                if coded:
                    outs["stream"][...] = stream

        @pl.when(step >= PARTS)
        def _():
            pair = step - PARTS
            logs = outs["logs"]
            lane = lax.broadcasted_iota(jnp.int32, (1, 128), 1)

            @pl.when(pair == 0)
            def _():
                logs[...] = jnp.zeros_like(logs)

            def span(part):
                return pl.ds(pl.multiple_of(part * width + pair * lanes, lanes), lanes)

            keys, values = held[:, span(1)], held[:, span(2)]
            segments = ins["segment_row"][...]
            for start in range(0, rows, BLOCK):
                at = pl.ds(start, BLOCK)
                same = ins["segment_column"][at, :] == segments
                queries = held[at, span(0)] * jnp.asarray(HD**-0.5, BF16)
                parts = []
                for head in range(2):
                    scores = jnp.where(same, mm(only(queries, head), keys, NT), masked_score)
                    top = jnp.max(scores, axis=-1, keepdims=True)
                    raised = jnp.exp(scores - top)
                    total = jnp.sum(raised, axis=-1, keepdims=True)
                    parts.append(mm(raised.astype(BF16), values) / total)
                    logs[at, :] += jnp.where(lane == 2 * pair + head, top + jnp.log(total), 0.0)
                outs["mixed"][at, :] = jnp.where(lanes_of(0), parts[0], parts[1]).astype(BF16)

        extra.closing(here, step, steps, ins, outs, own)

    return run(body, steps, ins, outs, scratch, collective, "forward_attention", 30)


BLOCK = 192
QUERY_BLOCK = 384


def middle_block(encoder, layer, slots, ins, extra, collective):
    width = ins["output"].array.shape[1]
    rows = ins["mixed"].array.shape[0]
    hidden = ins["shrink"].array.shape[0]
    fine = width // slots // PARTS
    tile = 512
    tiles = hidden // tile
    feed = 2 * tiles if encoder else tiles
    units = hidden // width + hidden // width + 1
    wide = hidden // width
    pairs, lanes = width // (2 * HD), 2 * HD
    length = PARTS * rows
    first_query = feed + units
    first_key = first_query + pairs
    steps = first_key + 2 * pairs

    def tiled(i):
        return lax.rem(jnp.minimum(i, feed - 1), tiles)

    tail = feed - tiles
    ins["expand"].spec = pl.BlockSpec((width, tile), lambda i: (0, tiled(i)))
    ins["expand_shift"].spec = pl.BlockSpec((1, tile), lambda i: (0, tiled(i)))
    ins["shrink"].spec = pl.BlockSpec((tile, width), lambda i: (tiled(i), 0))
    ins["stream"].spec = pl.BlockSpec((1, rows, width), lambda i: (0, 0, 0))
    outs = {
        "query": Item(shaped((rows, width)), pl.BlockSpec((rows, lanes), lambda i: (0, jnp.clip(i - first_query, 0, pairs - 1)))),
        "key": Item(shaped((rows, width)), pl.BlockSpec((rows, lanes), lambda i: (0, jnp.maximum(i - first_key - pairs, 0)))),
        "value": Item(shaped((rows, width)), pl.BlockSpec((rows, lanes), lambda i: (0, jnp.maximum(i - first_key - pairs, 0)))),
        "middle": Item(shaped((rows, width), F32)),
        "small": Item(shaped((8, width), F32)),
        "wide": Item(shaped((1, hidden), F32), pl.BlockSpec((1, tile), lambda i: (0, jnp.clip(i - tail, 0, tiles - 1)))),
    }
    scratch = {
        "active": pltpu.VMEM((rows, hidden), BF16),
        "hidden_low": pltpu.VMEM((rows, hidden), BF16),
        "normed": pltpu.VMEM((rows, width), BF16),
        "hat": pltpu.VMEM((rows, width), F32),
        "scale": pltpu.VMEM((rows, 1), F32),
        "total": pltpu.VMEM((rows, width), F32),
        "back": pltpu.VMEM((rows, width), F32),
        "low": pltpu.VMEM((rows, width), BF16),
        "branch": pltpu.VMEM((rows, width), BF16),
        "delta": pltpu.VMEM((rows, 128), F32),
        "qkv_held": pltpu.VMEM((length, 3 * width), BF16),
        "qkv_sem": DMA((1,)),
        "mixed_back": pltpu.VMEM((PARTS, rows, width), BF16),
        "stats": pltpu.VMEM((PARTS, 32, rows), F32),
        "line": Line.scratch(2),
        "cores": Cores.scratch(units, (fine, width)),
    }
    if encoder:
        outs["code_grad"] = Item(shaped((CODE, width), F32))
        scratch["slope"] = pltpu.VMEM((tiles, rows, tile), BF16)
        scratch["sums"] = pltpu.VMEM((4, PARTS, units, fine, width), BF16)
    else:
        outs["decoded"] = Item(shaped((rows, width)))
        outs["sums"] = Item(shaped((4, PARTS, units, fine, width)))
    extra.declare(ins, outs, scratch)

    def body(here, step, ins, outs, own):
        table = ins["table"]
        normed, hat, scale, total, back, low = (own[n] for n in ("normed", "hat", "scale", "total", "back", "low"))
        mixed_back, stats, held = own["mixed_back"], own["stats"], own["qkv_held"]
        sums = own["sums"] if encoder else outs["sums"]
        cores = Cores(here, sums, own["cores"], wide)
        line = Line(here, [mixed_back, stats], own["line"])
        load = pltpu.make_async_copy(ins["qkv"], held, own["qkv_sem"].at[0])
        gain, shift = table[2 * layer + 1 : 2 * layer + 2, :], table[5 + 2 * layer : 6 + 2 * layer, :]
        extra.events(here, step, steps, ins, outs, own)

        @at_step(step, 0)
        def _():
            load.start()
            middle = ins["stream"][0].astype(F32) + mm(ins["mixed"][...], ins["output"][...]) + table[12 + layer : 13 + layer, :]
            hat[...], scale[...] = norm_parts(middle)
            normed[...] = (hat[...] * gain + shift).astype(BF16)
            total[...] = middle + table[14 + layer : 15 + layer, :]
            back[...] = jnp.zeros_like(back)
            if not encoder:
                low[...] = ins["other"][...]

        def columns_at(n):
            return pl.ds(pl.multiple_of(n * tile, tile), tile)

        def forward(n):
            value = mm(normed[...], ins["expand"][...]) + ins["expand_shift"][...]
            active, steep = gelu_parts(value)
            active = active.astype(BF16)
            own["active"][:, columns_at(n)] = active
            total[...] += mm(active, ins["shrink"][...])
            return steep

        def backward(n, steep):
            hidden_low = (steep * mm(low[...], ins["shrink"][...], NT)).astype(BF16)
            own["hidden_low"][:, columns_at(n)] = hidden_low
            outs["wide"][...] = columns(hidden_low.astype(F32))
            back[...] += mm(hidden_low, ins["expand"][...], NT)

        if encoder:

            @pl.when(step < tiles)
            def _():
                own["slope"][step] = forward(step).astype(BF16)

            @at_step(step, tiles - 1)
            def _():
                code = table[25:43, :].astype(BF16)
                encoded_low = total[...].astype(BF16)
                coded = mm(encoded_low, code, NT)
                size = lax.rsqrt(jnp.sum(coded * coded, axis=-1, keepdims=True) + epsilon)
                unit = coded * size
                grad = ins["other"][...]
                coded_low = ((grad - unit * jnp.sum(unit * grad, axis=-1, keepdims=True)) * size).astype(BF16)
                outs["code_grad"][...] = mm(coded_low, encoded_low, TN)
                total[...] = mm(coded_low, code)
                low[...] = total[...].astype(BF16)

            @pl.when((step >= tiles) & (step < feed))
            def _():
                backward(step - tiles, own["slope"][step - tiles].astype(F32))
        else:

            @pl.when(step < tiles)
            def _():
                backward(step, forward(step))

        @at_step(step, feed - 1)
        def _():
            if encoder:
                grad_out = total[...]
            else:
                outs["decoded"][...] = total[...].astype(BF16)
                grad_out = low[...].astype(F32)
            grad = back[...]
            middle = grad_out + norm_back(grad, gain, hat[...], scale[...])
            outs["middle"][...] = middle
            branch = middle.astype(BF16)
            own["branch"][...] = branch
            mixed_low = mm(branch, ins["output"][...], NT).astype(BF16)
            mixed_back[0] = mixed_low
            product = mixed_low.astype(F32) * ins["mixed"][...].astype(F32)
            feature = lax.broadcasted_iota(jnp.int32, (width, 128), 0) // HD
            heads = (feature == lax.broadcasted_iota(jnp.int32, (width, 128), 1)).astype(F32)
            delta = lax.dot_general(product, heads, NN, preferred_element_type=F32, precision=lax.Precision.HIGHEST)
            own["delta"][...] = delta
            stats[0, pl.ds(0, 16)] = ins["logs"][...].T[:16]
            stats[0, pl.ds(16, 16)] = delta.T[:16]
            for m in range(2):
                line.start(m)
            outs["small"][...] = jnp.concatenate(
                [columns(grad * hat[...]), columns(grad), columns(branch.astype(F32)), columns(low[...].astype(F32))]
                + [jnp.zeros_like(columns(grad))] * 4
            )

        unit = step - feed

        def wide_at(n):
            return pl.ds(pl.multiple_of(n * width, width), width)

        @pl.when((unit >= 0) & (unit < wide))
        def _():
            cores.put(unit, mm(own["active"][:, wide_at(unit)], low[...], TN))

        @pl.when((unit >= wide) & (unit < 2 * wide))
        def _():
            cores.put(unit, mm(normed[...], own["hidden_low"][:, wide_at(unit - wide)], TN))

        @pl.when(unit == 2 * wide)
        def _():
            cores.put(unit, mm(ins["mixed"][...], own["branch"][...], TN))

        @pl.when((unit >= 2) & (unit < units))
        def _():
            cores.collect(unit - 2)

        @pl.when(unit == units)
        def _():
            cores.collect(unit - 2)
            cores.collect(unit - 1)
            cores.finish(units)

        for n, k in ((units - 1, 1), (units + 3, 2)):

            @pl.when(unit == n)
            def _():
                for m in range(2):
                    line.hop(m, k)

        @at_step(step, first_query)
        def _():
            load.wait()

        eighth = jnp.asarray(HD**-0.5, BF16)

        @pl.when((step >= first_query) & (step < first_key))
        def _():
            pair = step - first_query
            lane = lax.broadcasted_iota(jnp.int32, (1, 128), 1)

            def span(part):
                return pl.ds(pl.multiple_of(part * width + pair * lanes, lanes), lanes)

            keys, values = held[:, span(1)], held[:, span(2)]
            segments = ins["segment_row"][...]
            for start in range(0, rows, QUERY_BLOCK):
                at = pl.ds(start, QUERY_BLOCK)
                same = ins["segment_column"][at, :] == segments
                queries = held[at, span(0)] * eighth
                grads = mixed_back[0, at, span(0)]
                parts = []
                for head in range(2):
                    mine = lane == 2 * pair + head
                    log_sum = jnp.sum(jnp.where(mine, ins["logs"][at, :], 0.0), axis=-1, keepdims=True)
                    centre = jnp.sum(jnp.where(mine, own["delta"][at, :], 0.0), axis=-1, keepdims=True)
                    scores = jnp.where(same, mm(only(queries, head), keys, NT), masked_score)
                    probability = jnp.exp(scores - log_sum)
                    prob_grad = mm(only(grads, head), values, NT)
                    score_low = (probability * (prob_grad - centre)).astype(BF16)
                    parts.append(mm(score_low, keys) * HD**-0.5)
                outs["query"][at, :] = jnp.where(lanes_of(0), parts[0], parts[1]).astype(BF16)

        late = step - first_key

        @pl.when(late == pairs)
        def _():
            for m in range(2):
                line.hop(m, 3)

        for half in range(2):

            @pl.when((late >= half * pairs) & (late < (half + 1) * pairs))
            def _():
                pair = late - half * pairs
                pieces = range(2 * half, 2 * half + 2)

                def span(part):
                    return pl.ds(pl.multiple_of(part * width + pair * lanes, lanes), lanes)

                these = pl.ds(2 * half * rows, 2 * rows)
                queries = held[these, span(0)]
                grads = mixed_back[2 * half : 2 * half + 2, :, span(0)].reshape(2 * rows, lanes)

                def line_of(row):
                    return jnp.concatenate([stats[k, pl.ds(row, 1), :] for k in pieces], axis=1)

                same = ins["segment_column"][...] == ins["segment_row"][:, these]
                keys = held[pl.ds(0, rows), span(1)] * eighth
                values = held[pl.ds(0, rows), span(2)]
                key_parts, value_parts = [], []
                for head in range(2):
                    scores = jnp.where(same, mm(only(keys, head), queries, NT), masked_score)
                    probability = jnp.exp(scores - line_of(2 * pair + head))
                    value_parts.append(mm(probability.astype(BF16), grads))
                    prob_grad = mm(only(values, head), grads, NT)
                    score_low = (probability * (prob_grad - line_of(16 + 2 * pair + head))).astype(BF16)
                    key_parts.append(mm(score_low, queries) * HD**-0.5)
                key = jnp.where(lanes_of(0), key_parts[0], key_parts[1])
                value = jnp.where(lanes_of(0), value_parts[0], value_parts[1])
                if half == 0:
                    hat[:, span(0)] = key
                    total[:, span(0)] = value
                else:
                    outs["key"][...] = (hat[:, span(0)] + key).astype(BF16)
                    outs["value"][...] = (total[:, span(0)] + value).astype(BF16)

        @at_step(step, steps - 1)
        def _():
            for m in range(2):
                line.finish(m)

        extra.closing(here, step, steps, ins, outs, own)

    return run(body, steps, ins, outs, scratch, collective, "encoder_middle" if encoder else "decoder_middle", 80)


def projection_back(coded, layer, slots, ins, extra, collective):
    rows, width = ins["query"].array.shape
    fine = width // slots // PARTS
    units = 3
    steps = 1 + units
    ins["stream"].spec = pl.BlockSpec((1, rows, width), lambda i: (0, 0, 0))
    outs = {"small": Item(shaped((8, width), F32)), "sums": Item(shaped((4, PARTS, units, fine, width)))}
    if coded:
        outs["unit_grad"] = Item(shaped((rows, CODE), F32))
        outs["decode_grad"] = Item(shaped((CODE, width), F32))
        ins["pieces"].spec = pl.BlockSpec((1, rows, CODE), lambda i: (0, 0, 0))
    else:
        outs["grad"] = Item(shaped((rows, width), F32))
    scratch = {"cores": Cores.scratch(units, (fine, width))}
    extra.declare(ins, outs, scratch)

    def body(here, step, ins, outs, own):
        table = ins["table"]
        cores = Cores(here, outs["sums"], own["cores"], 0)
        extra.events(here, step, steps, ins, outs, own)
        sources = (ins["query"], ins["key"], ins["value"])
        for n in range(units):

            @at_step(step, n)
            def _():
                cores.put(jnp.int32(n), mm(ins["normed"][...], sources[n][...], TN))

        @at_step(step, units)
        def _():
            query, key, value = sources
            weight = ins["weight"]
            grad = mm(query[...], weight[:, :width], NT)
            grad += mm(key[...], weight[:, width : 2 * width], NT)
            grad += mm(value[...], weight[:, 2 * width :], NT)
            hat, scale = norm_parts(ins["stream"][0].astype(F32))
            start = ins["middle"][...] + norm_back(grad, table[2 * layer : 2 * layer + 1, :], hat, scale)
            small = [columns(grad * hat), columns(grad), columns(query[...].astype(F32)), columns(value[...].astype(F32))]
            if coded:
                start_low = start.astype(BF16)
                outs["unit_grad"][...] = mm(start_low, table[43:61, :].astype(BF16), NT)
                outs["decode_grad"][...] = mm(ins["pieces"][0], start_low, TN)
                small.append(columns(start_low.astype(F32)))
            else:
                outs["grad"][...] = start
            small += [jnp.zeros_like(small[0])] * (8 - len(small))
            outs["small"][...] = jnp.concatenate(small)
            for n in range(units):
                cores.collect(jnp.int32(n))
            cores.finish(units)

        extra.closing(here, step, steps, ins, outs, own)

    return run(body, steps, ins, outs, scratch, collective, "projection_back", 12)


def last_kernel(here, step, ins, outs, own):
    square = Square(here, own["square"][0], own["square"][1:], ins["sums"])
    stack = Stack(here, own["total"], own["stack"])
    rows = Sum(here, [ins["small"]], own["sum"])
    square.load()
    rows.begin()
    square.start()
    rows.meet(0)
    rows.meet(1)
    square.sides()
    rows.meet(2)
    rows.finish(outs["rows"])
    square.total(own["total"])
    stack.start()
    stack.finish(outs["units"])


class Nothing:
    def declare(self, ins, outs, scratch):
        pass

    def events(self, here, step, steps, ins, outs, own):
        pass

    def closing(self, here, step, steps, ins, outs, own):
        pass


class Beside(Nothing):
    def __init__(
        self, slots, gathers=None, gather_steps=(), squares=None, stacks=None, sums=None, lines=None, line_steps=(), spreads=None, spread_steps=()
    ):
        self.lines, self.line_steps, self.spreads, self.spread_steps = lines or {}, line_steps, spreads or {}, spread_steps
        self.slots, self.gathers, self.gather_steps = slots, gathers or {}, gather_steps
        self.squares, self.stacks, self.sums = squares or {}, stacks or {}, sums or {}

    def declare(self, ins, outs, scratch):
        for name, (array, layer) in self.gathers.items():
            block = (1,) + array.shape[1:]
            ins["shard_" + name] = Item(array, pl.BlockSpec(block, lambda i, layer=layer: (layer, 0, 0)))
            outs["gathered_" + name] = anywhere(shaped((self.slots, PARTS) + array.shape[1:]))
        if self.gathers:
            scratch["gather"] = Gather.scratch(len(self.gathers))
        for name, (array, layer) in self.lines.items():
            block = (1,) + array.shape[1:]
            ins["line_" + name] = Item(array, pl.BlockSpec(block, lambda i, layer=layer: (layer, 0, 0)))
            outs["lined_" + name] = anywhere(shaped((PARTS,) + array.shape[1:]))
        if self.lines:
            scratch["lines"] = Line.scratch(len(self.lines)) + [DMA((len(self.lines),))]
        for name, array in self.spreads.items():
            ins["spread_" + name] = Item(array)
            outs["gathered_" + name] = anywhere(shaped((self.slots,) + array.shape))
        if self.spreads:
            scratch["spreads"] = Spread.scratch(len(self.spreads))
        for name, (sums, first, units, steps) in self.squares.items():
            loaded = sums is not None
            if loaded:
                tail = sums.shape[3:]
            else:
                tail = (scratch["sums"] if "sums" in scratch else outs["sums"].array).shape[3:]
            if loaded:
                ins["square_" + name] = anywhere(sums)
            outs["total_" + name] = Item(shaped((PARTS, units) + tail))
            scratch["square_" + name] = Square.scratch(units, tail, loaded)
        for name, (array, steps) in self.stacks.items():
            if isinstance(array, str):
                shape = outs["total_" + array].array.shape
            else:
                ins["stack_" + name] = Item(array)
                shape = array.shape
            outs["stacked_" + name] = Item(shaped(shape[1:], F32))
            scratch["stack_" + name] = Stack.scratch(shape[1], shape[2:])
        for name, (arrays, steps) in self.sums.items():
            for i, array in enumerate(arrays):
                ins[f"sum_{name}{i}"] = Item(array)
            width = min(a.shape[1] for a in arrays)
            rows = -(-sum(a.shape[0] * (a.shape[1] // width) for a in arrays) // 16) * 16
            outs["summed_" + name] = Item(shaped((rows, width), F32))
            scratch["sum_" + name] = Sum.scratch(rows, width)

    def listed(self, here, ins, outs, own):
        if self.gathers:
            names = list(self.gathers)
            gather = Gather(here, [ins["shard_" + n].at[0] for n in names], [outs["gathered_" + n] for n in names], own["gather"])

            def each(*actions):
                def go():
                    for action, *more in actions:
                        for m in range(len(names)):
                            action(m, *more)

                return go

            start, one, two, three, turn, corner = self.gather_steps
            yield start, each((gather.start,))
            yield one, each((gather.hop, 1), (gather.turn, 0))
            yield two, each((gather.hop, 2), (gather.turn, 1))
            yield three, each((gather.hop, 3), (gather.turn, 2))
            yield turn, each((gather.turn, 3), (gather.siblings,))
            yield corner, each((gather.corner,))
            yield None, each((gather.finish,))
        if self.lines:
            line_names = list(self.lines)
            sources = [ins["line_" + n].at[0] for n in line_names]
            arrays = [outs["lined_" + n] for n in line_names]
            sems = own["lines"]
            line = Line(here, arrays, sems[:3], sources)
            keeps = [pltpu.make_async_copy(sources[m], arrays[m].at[here.z], sems[3].at[m]) for m in range(len(line_names))]

            def begin():
                for m in range(len(line_names)):
                    line.start(m)
                    keeps[m].start()

            def end():
                for m in range(len(line_names)):
                    line.finish(m)
                    keeps[m].wait()

            def hop(k):
                for m in range(len(line_names)):
                    line.hop(m, k)

            yield self.line_steps[0], begin
            for k in range(1, PARTS):
                yield self.line_steps[k], functools.partial(hop, k)
            yield None, end
        if self.spreads:
            spread_names = list(self.spreads)
            spread = Spread(here, [ins["spread_" + n] for n in spread_names], [outs["gathered_" + n] for n in spread_names], own["spreads"])
            for action, n in zip((spread.start, spread.turn, spread.corner, spread.finish), self.spread_steps):

                def go(action=action):
                    for m in range(len(spread_names)):
                        action(m)

                yield n, go
        for name, (sums, first, units, steps) in self.squares.items():
            scratch = own["square_" + name]
            span = pl.ds(first, units)
            if sums is None:
                held = own["sums"] if "sums" in own else outs["sums"]
                square = Square(here, held.at[:, :, span], scratch)
            else:
                square = Square(here, scratch[0], scratch[1:], ins["square_" + name].at[:, :, span])
                yield steps[0], square.load
            yield steps[1], square.start
            yield steps[2], square.sides
            yield steps[3], functools.partial(square.total, outs["total_" + name])
        for name, (array, steps) in self.stacks.items():
            held = outs["total_" + array] if isinstance(array, str) else ins["stack_" + name]
            stack = Stack(here, held, own["stack_" + name])
            yield steps[0], stack.start
            yield steps[1], functools.partial(stack.finish, outs["stacked_" + name])
        for name, (arrays, steps) in self.sums.items():
            rows = Sum(here, [ins[f"sum_{name}{i}"] for i in range(len(arrays))], own["sum_" + name])
            yield steps[0], rows.begin
            for stage in range(3):
                yield steps[1 + stage], functools.partial(rows.meet, stage)
            yield steps[4], functools.partial(rows.finish, outs["summed_" + name])

    def grouped(self, here, ins, outs, own):
        groups = {}
        for n, action in self.listed(here, ins, outs, own):
            groups.setdefault(n, []).append(action)
        return groups

    def play(self, step, n, actions):
        def go():
            for action in actions:
                action()

        at_step(step, n)(go)

    def events(self, here, step, steps, ins, outs, own):
        for n, actions in sorted((n, a) for n, a in self.grouped(here, ins, outs, own).items() if n is not None):
            self.play(step, n, actions)

    def closing(self, here, step, steps, ins, outs, own):
        actions = self.grouped(here, ins, outs, own).get(None)
        if actions:
            self.play(step, steps - 1, actions)


def on_device(
    patches,
    segments,
    code_bits,
    norm_gain,
    norm_shift,
    project_weight,
    query_value_bias,
    output_weight,
    output_bias,
    expand_weight,
    expand_bias,
    shrink_weight,
    shrink_bias,
    encode_weight,
    decode_weight,
    decode_bias,
    cotangent,
):
    slots, parts = lax.axis_size("slot"), lax.axis_size("seq")
    fine, width = project_weight.shape[1], patches.shape[-1]
    if slots != 8 or parts != PARTS or fine % 8:
        return plain_device(
            patches,
            segments,
            code_bits,
            norm_gain,
            norm_shift,
            project_weight,
            query_value_bias,
            output_weight,
            output_bias,
            expand_weight,
            expand_bias,
            shrink_weight,
            shrink_bias,
            encode_weight,
            decode_weight,
            decode_bias,
            cotangent,
        )
    slot, z = lax.axis_index("slot"), lax.axis_index("seq")
    devices, rows, hidden = slots * parts, patches.shape[1], expand_weight.shape[-1]
    signs = ((2 * code_bits - 1).astype(F32) * CODE ** (-0.5)).astype(BF16)

    ins = {
        "gain": Item(norm_gain),
        "shift": Item(norm_shift),
        "query_value": Item(query_value_bias),
        "output_bias": Item(output_bias),
        "shrink_bias": Item(shrink_bias),
        "decode_bias": Item(decode_bias.reshape(1, fine)),
        "expand_bias": Item(expand_bias),
        "encode": Item(encode_weight),
        "decode": Item(decode_weight),
    }
    weights = {"project": project_weight, "output": output_weight, "expand": expand_weight, "shrink": shrink_weight}
    ins["signs"], ins["patches"] = Item(signs), Item(patches)
    for name, array in weights.items():
        ins[name] = Item(array, pl.BlockSpec((1,) + array.shape[1:], lambda i: (1, 0, 0)))
    outs = {
        "table": anywhere(shaped((slots, parts, 64, fine), F32)),
        "signs": anywhere(shaped((parts, rows, CODE))),
        "patches": anywhere(shaped((parts, rows, width))),
    }
    for name, array in weights.items():
        outs[name] = anywhere(shaped((slots, parts) + array.shape[1:]))
    scratch = {
        "table": pltpu.VMEM((64, fine), F32),
        "gather": Gather.scratch(5),
        "line": Line.scratch(2),
        "keep": DMA((2,)),
    }
    first = run(first_kernel, 1, ins, outs, scratch, 0, "first_gather", 70)

    small = first["table"].reshape(devices, 64, fine)
    table = small.transpose(1, 0, 2).reshape(64, width)
    expand_shifts = small[:, 17:25].reshape(devices, 2, 4, fine).transpose(1, 0, 2, 3).reshape(2, 1, hidden)
    around = jnp.arange(parts) ^ z
    pieces = segments[0].reshape(parts, rows)[around]
    segment_row = pieces.reshape(1, parts * rows)
    segment_column = pieces[0].reshape(rows, 1)

    def flat(array):
        return array.reshape(-1, array.shape[-1])

    def forward(layer, pieces, weight, extra, collective):
        ins = {
            "pieces": Item(pieces),
            "table": Item(table),
            "weight": Item(weight),
            "segment_row": Item(segment_row),
            "segment_column": Item(segment_column),
        }
        return forward_attention(layer == 1, layer, slots, ins, extra, collective)

    def middle(layer, stream, other, ahead, weights, extra, collective):
        ins = {
            "stream": Item(stream),
            "mixed": Item(ahead["mixed"]),
            "other": Item(other),
            "logs": Item(ahead["logs"]),
            "qkv": anywhere(ahead["qkv"]),
            "table": Item(table),
            "output": Item(weights["output"]),
            "expand": Item(weights["expand"]),
            "expand_shift": Item(expand_shifts[layer]),
            "shrink": Item(weights["shrink"]),
            "segment_row": Item(segment_row),
            "segment_column": Item(segment_column),
        }
        return middle_block(layer == 0, layer, slots, ins, extra, collective)

    def projection(layer, stream, ahead, between, weight, extra, collective, **more):
        ins = {
            "query": Item(between["query"]),
            "key": Item(between["key"]),
            "value": Item(between["value"]),
            "normed": Item(ahead["normed"]),
            "stream": Item(stream),
            "middle": Item(between["middle"]),
            "table": Item(table),
            "weight": Item(weight),
        }
        ins.update({k: Item(v) for k, v in more.items()})
        return projection_back(layer == 1, layer, slots, ins, extra, collective)

    decoder = {n: flat(first[n]) for n in weights}
    names = ("output", "expand", "shrink")
    beside = Beside(
        slots,
        {"project": (project_weight, 0)},
        (0, 2, 4, 5, 7, 9),
        lines={n: (weights[n], 0) for n in names},
        line_steps=(1, 4, 7, None),
    )
    ahead1 = forward(1, first["signs"], decoder["project"], beside, 1)
    encoder = {"project": flat(ahead1["gathered_project"])}

    beside = Beside(
        slots,
        spreads={n: ahead1["lined_" + n] for n in names},
        spread_steps=(0, 12, 18, None),
        squares={"two": (None, 0, 4, (None, 13, 20, 27))},
    )
    stream1 = ahead1["stream"][None]
    between1 = middle(1, stream1, cotangent[0], ahead1, decoder, beside, 2)
    encoder.update({n: flat(between1["gathered_" + n]) for n in names})
    beside = Beside(slots, stacks={"two": (between1["total_two"], (0, 3))})
    after1 = projection(1, stream1, ahead1, between1, decoder["project"], beside, 3, pieces=first["signs"])

    beside = Beside(
        slots,
        squares={"three": (between1["sums"], 4, 5, (0, 1, 5, None))},
        sums={"one": ([after1["small"], between1["small"], between1["wide"], after1["decode_grad"]], (0, 1, 3, 5, None))},
    )
    ahead0 = forward(0, first["patches"], encoder["project"], beside, 4)
    beside = Beside(
        slots,
        squares={
            "one": (after1["sums"], 0, 3, (0, 1, 4, 9)),
            "five": (None, 0, 4, (None, 18, 22, 28)),
            "six": (None, 4, 5, (None, 22, 30, None)),
        },
        stacks={
            "three": (ahead0["total_three"], (0, 9)),
            "one": ("one", (10, 18)),
            "five": ("five", (33, None)),
        },
    )
    between0 = middle(0, first["patches"], after1["unit_grad"], ahead0, encoder, beside, 5)
    beside = Beside(
        slots,
        stacks={"six": (between0["total_six"], (0, 3))},
        sums={"two": ([between0["small"], between0["wide"], between0["code_grad"]], (0, 1, 2, 3, None))},
    )
    after0 = projection(0, first["patches"], ahead0, between0, encoder["project"], beside, 6)

    ins = {"sums": anywhere(after0["sums"]), "small": Item(after0["small"])}
    outs = {"units": Item(shaped((3, fine, width), F32)), "rows": Item(shaped((16, width), F32))}
    scratch = {
        "square": Square.scratch(3, (fine, width), True),
        "total": pltpu.VMEM((parts, 3, fine, width), BF16),
        "stack": Stack.scratch(3, (fine, width)),
        "sum": Sum.scratch(16, width),
    }
    last = run(last_kernel, 1, ins, outs, scratch, 7, "last_sums", 30)

    device = slot * parts + z
    one, two = ahead0["summed_one"], after0["summed_two"]
    summed = jnp.concatenate([last["rows"][:8], one, two])
    mine = lax.dynamic_slice(summed, (0, device * fine), (summed.shape[0], fine))
    in0, in1, mid1 = mine[0:4], mine[8:13], mine[16:20]
    at = 8 + one.shape[0]
    mid0, decode_grad, code_grad = mine[at : at + 4], mine[28:46], mine[at + 12 : at + 30]
    wide = jnp.stack([two[8:12].reshape(hidden), one[16:20].reshape(hidden)])
    wide = lax.dynamic_slice(wide, (0, device * (hidden // devices)), (2, hidden // devices))
    decoder_mlp = jnp.concatenate([after1["stacked_two"], between0["stacked_three"]])
    encoder_mlp = jnp.concatenate([between0["stacked_five"], after0["stacked_six"]])
    encoder_project, decoder_project = last["units"], between0["stacked_one"]

    def both(cut):
        return jnp.stack([cut(encoder_mlp), cut(decoder_mlp)])

    def joined(units):
        return units.transpose(1, 0, 2).reshape(fine, units.shape[0] * width)

    return (
        between1["decoded"][None],
        after0["grad"][None],
        jnp.stack([jnp.stack([in0[0], mid0[0]]), jnp.stack([in1[0], mid1[0]])]),
        jnp.stack([jnp.stack([in0[1], mid0[1]]), jnp.stack([in1[1], mid1[1]])]),
        jnp.stack([joined(encoder_project), joined(decoder_project)]),
        jnp.stack([in0[2:4], in1[2:4]]),
        both(lambda g: g[8]),
        jnp.stack([mid0[2], mid1[2]]),
        both(lambda g: joined(g[4:8])),
        wide,
        both(lambda g: g[0:4].reshape(4 * fine, width)),
        jnp.stack([mid0[3], mid1[3]]),
        code_grad.T,
        decode_grad,
        in1[4],
    )


def plain_norm(stream, gains, shifts):
    centre = stream - jnp.mean(stream, axis=-1, keepdims=True)
    spread = jnp.mean(centre * centre, axis=-1, keepdims=True)
    return centre * lax.rsqrt(spread + epsilon) * gains + shifts


def normalize(coded):
    return coded / jnp.sqrt(jnp.sum(coded * coded, axis=-1, keepdims=True) + epsilon)


def gelu_exact(hidden):
    return jax.nn.gelu(hidden, approximate=False)


def gather_weights(shards):
    return (
        lax.all_gather(shards[0], ("slot", "seq"), axis=2, tiled=True),
        lax.all_gather(shards[1], ("slot", "seq"), axis=2, tiled=True),
        lax.all_gather(shards[2], ("slot", "seq"), axis=1, tiled=True),
        lax.all_gather(shards[3], ("slot", "seq"), axis=2, tiled=True),
        lax.all_gather(shards[4], ("slot", "seq"), axis=1, tiled=True),
        lax.all_gather(shards[5], ("slot", "seq"), axis=1, tiled=True),
        lax.all_gather(shards[6], ("slot", "seq"), axis=1, tiled=True),
        lax.all_gather(shards[7], ("slot", "seq"), axis=1, tiled=True),
        lax.all_gather(shards[8], ("slot", "seq"), axis=1, tiled=True),
        lax.all_gather(shards[9], ("slot", "seq"), axis=1, tiled=True),
        lax.all_gather(shards[10], ("slot", "seq"), axis=0, tiled=True),
        lax.all_gather(shards[11], ("slot", "seq"), axis=1, tiled=True),
        lax.all_gather(shards[12], ("slot", "seq"), axis=0, tiled=True),
    )


def segment_mask(segments, offset, block_rows):
    return segments[:, None, offset : offset + block_rows, None] == segments[:, None, None, :]


def scaled_scores(queries, key_rows, same_item):
    scores = jnp.einsum("sqhd,skhd->shqk", queries, key_rows, preferred_element_type=jnp.float32)
    return jnp.where(same_item, scores * HD ** (-0.5), masked_score)


def forward_block(stream, layer, segments):
    (
        gains,
        shifts,
        project,
        query_value,
        output,
        output_shift,
        expand,
        expand_shift,
        shrink,
        shrink_shift,
    ) = layer
    slot_count, row_count, model_width = stream.shape
    seq_parts = lax.axis_size("seq")
    head_width = model_width // seq_parts
    normed = plain_norm(stream, gains[0].astype(jnp.float32), shifts[0].astype(jnp.float32)).astype(
        jnp.bfloat16
    )
    bias_row = jnp.concatenate(
        [query_value[0], jnp.zeros_like(query_value[0]), query_value[1]]
    ).astype(jnp.float32)
    projected = (jnp.dot(normed, project, preferred_element_type=jnp.float32) + bias_row).astype(
        jnp.bfloat16
    )
    split_heads = lax.all_to_all(
        projected.reshape(slot_count, row_count, 3, seq_parts, head_width),
        "seq",
        split_axis=3,
        concat_axis=1,
        tiled=True,
    )
    length = split_heads.shape[1]
    local_heads = head_width // HD
    queries = split_heads[:, :, 0, 0].reshape(slot_count, length, local_heads, HD)
    key_rows = split_heads[:, :, 1, 0].reshape(slot_count, length, local_heads, HD)
    values = split_heads[:, :, 2, 0].reshape(slot_count, length, local_heads, HD)
    block_rows = min(512, length)
    pieces = []
    log_parts = []
    for offset in range(0, length, block_rows):
        scores = scaled_scores(
            queries[:, offset : offset + block_rows],
            key_rows,
            segment_mask(segments, offset, block_rows),
        )
        row_top = jnp.max(scores, axis=-1, keepdims=True)
        raised = jnp.exp(scores - row_top)
        row_total = jnp.sum(raised, axis=-1, keepdims=True)
        probability = (raised / row_total).astype(jnp.bfloat16)
        pieces.append(
            jnp.einsum(
                "shqk,skhd->sqhd", probability, values, preferred_element_type=jnp.float32
            ).astype(jnp.bfloat16)
        )
        log_parts.append(row_top + jnp.log(row_total))
    log_sums = jnp.concatenate(log_parts, axis=2)
    attended = jnp.concatenate(pieces, axis=1).reshape(slot_count, length, 1, head_width)
    mixed_rows = lax.all_to_all(attended, "seq", split_axis=1, concat_axis=2, tiled=True).reshape(
        slot_count, row_count, model_width
    )
    middle = (
        stream
        + jnp.dot(mixed_rows, output, preferred_element_type=jnp.float32)
        + output_shift.astype(jnp.float32)
    )
    normed_mid = plain_norm(
        middle, gains[1].astype(jnp.float32), shifts[1].astype(jnp.float32)
    ).astype(jnp.bfloat16)
    hidden = jnp.dot(normed_mid, expand, preferred_element_type=jnp.float32) + expand_shift.astype(
        jnp.float32
    )
    active = gelu_exact(hidden).astype(jnp.bfloat16)
    result = (
        middle
        + jnp.dot(active, shrink, preferred_element_type=jnp.float32)
        + shrink_shift.astype(jnp.float32)
    )
    saved_values = (
        normed,
        queries,
        key_rows,
        values,
        log_sums,
        mixed_rows,
        middle,
        normed_mid,
        hidden,
        active,
    )
    return (result, saved_values)


def backward_block(grad_out, stream, saved_values, layer, segments):
    (
        gains,
        shifts,
        project,
        query_value,
        output,
        output_shift,
        expand,
        expand_shift,
        shrink,
        shrink_shift,
    ) = layer
    normed, queries, key_rows, values, log_sums, mixed_rows, middle, normed_mid, hidden, active = (
        saved_values
    )
    slot_count, row_count, model_width = stream.shape
    seq_parts = lax.axis_size("seq")
    head_width = model_width // seq_parts
    branch = grad_out.astype(jnp.bfloat16)
    shrink_shift_grad = jnp.sum(branch, axis=(0, 1), dtype=jnp.float32)
    shrink_grad = jnp.einsum("stf,sto->fo", active, branch, preferred_element_type=jnp.float32)
    active_grad = jnp.einsum("sto,fo->stf", branch, shrink, preferred_element_type=jnp.float32)
    unused, gelu_back = jax.vjp(gelu_exact, hidden)
    hidden_low = gelu_back(active_grad)[0].astype(jnp.bfloat16)
    expand_shift_grad = jnp.sum(hidden_low, axis=(0, 1), dtype=jnp.float32)
    expand_grad = jnp.einsum(
        "sti,stf->if", normed_mid, hidden_low, preferred_element_type=jnp.float32
    )
    normed_mid_grad = jnp.einsum(
        "stf,if->sti", hidden_low, expand, preferred_element_type=jnp.float32
    )
    unused, norm_back = jax.vjp(
        plain_norm, middle, gains[1].astype(jnp.float32), shifts[1].astype(jnp.float32)
    )
    middle_part, gain_mid_grad, shift_mid_grad = norm_back(normed_mid_grad)
    middle_grad = grad_out + middle_part
    branch_low = middle_grad.astype(jnp.bfloat16)
    output_shift_grad = jnp.sum(branch_low, axis=(0, 1), dtype=jnp.float32)
    output_grad = jnp.einsum(
        "sti,sto->io", mixed_rows, branch_low, preferred_element_type=jnp.float32
    )
    mixed_low = jnp.einsum(
        "sto,io->sti", branch_low, output, preferred_element_type=jnp.float32
    ).astype(jnp.bfloat16)
    head_grad = lax.all_to_all(
        mixed_low.reshape(slot_count, row_count, seq_parts, head_width),
        "seq",
        split_axis=2,
        concat_axis=1,
        tiled=True,
    )
    length = head_grad.shape[1]
    local_heads = head_width // HD
    head_grad = head_grad.reshape(slot_count, length, local_heads, HD)
    scale_factor = HD ** (-0.5)
    block_rows = min(512, length)
    key_grad = jnp.zeros((slot_count, length, local_heads, HD), jnp.float32)
    value_grad = jnp.zeros((slot_count, length, local_heads, HD), jnp.float32)
    query_parts = []
    for offset in range(0, length, block_rows):
        query_block = queries[:, offset : offset + block_rows]
        scores = scaled_scores(query_block, key_rows, segment_mask(segments, offset, block_rows))
        probability = jnp.exp(scores - log_sums[:, :, offset : offset + block_rows])
        out_grad = head_grad[:, offset : offset + block_rows]
        value_grad = value_grad + jnp.einsum(
            "shqk,sqhd->skhd",
            probability.astype(jnp.bfloat16),
            out_grad,
            preferred_element_type=jnp.float32,
        )
        prob_grad = jnp.einsum(
            "sqhd,skhd->shqk", out_grad, values, preferred_element_type=jnp.float32
        )
        centre = jnp.sum(probability * prob_grad, axis=-1, keepdims=True)
        score_low = (probability * (prob_grad - centre)).astype(jnp.bfloat16)
        query_parts.append(
            jnp.einsum("shqk,skhd->sqhd", score_low, key_rows, preferred_element_type=jnp.float32)
            * scale_factor
        )
        key_grad = (
            key_grad
            + jnp.einsum(
                "shqk,sqhd->skhd", score_low, query_block, preferred_element_type=jnp.float32
            )
            * scale_factor
        )
    query_grad = jnp.concatenate(query_parts, axis=1)
    joined = (
        jnp.stack([query_grad, key_grad, value_grad], axis=2)
        .astype(jnp.bfloat16)
        .reshape(slot_count, length, 3, 1, head_width)
    )
    project_low = lax.all_to_all(joined, "seq", split_axis=1, concat_axis=3, tiled=True).reshape(
        slot_count, row_count, 3 * model_width
    )
    project_shift = jnp.sum(project_low, axis=(0, 1), dtype=jnp.float32)
    query_value_grad = jnp.stack([project_shift[:model_width], project_shift[2 * model_width :]])
    project_grad = jnp.einsum(
        "sti,stj->ij", normed, project_low, preferred_element_type=jnp.float32
    )
    normed_grad = jnp.einsum(
        "stj,ij->sti", project_low, project, preferred_element_type=jnp.float32
    )
    unused, norm_back = jax.vjp(
        plain_norm, stream, gains[0].astype(jnp.float32), shifts[0].astype(jnp.float32)
    )
    stream_part, gain_in_grad, shift_in_grad = norm_back(normed_grad)
    input_part = middle_grad + stream_part
    grads = (
        jnp.stack([gain_in_grad, gain_mid_grad]),
        jnp.stack([shift_in_grad, shift_mid_grad]),
        project_grad,
        query_value_grad,
        output_grad,
        output_shift_grad,
        expand_grad,
        expand_shift_grad,
        shrink_grad,
        shrink_shift_grad,
    )
    return (input_part, grads)


def plain_device(
    patches,
    segments,
    code_bits,
    norm_gain,
    norm_shift,
    project_weight,
    query_value_bias,
    output_weight,
    output_bias,
    expand_weight,
    expand_bias,
    shrink_weight,
    shrink_bias,
    encode_weight,
    decode_weight,
    decode_bias,
    cotangent,
):
    shards = (
        norm_gain,
        norm_shift,
        project_weight,
        query_value_bias,
        output_weight,
        output_bias,
        expand_weight,
        expand_bias,
        shrink_weight,
        shrink_bias,
        encode_weight,
        decode_weight,
        decode_bias,
    )
    gathered = gather_weights(shards)
    stream_in = patches.astype(jnp.float32)
    encoded, unused = forward_block(
        stream_in, tuple((array[0] for array in gathered[:10])), segments
    )
    encoded_low = encoded.astype(jnp.bfloat16)
    coded = jnp.einsum("sti,ic->stc", encoded_low, gathered[10], preferred_element_type=jnp.float32)
    signs = ((2 * code_bits - 1).astype(jnp.float32) * CODE ** (-0.5)).astype(jnp.bfloat16)
    start = jnp.einsum(
        "stc,ci->sti", signs, gathered[11], preferred_element_type=jnp.float32
    ) + gathered[12].astype(jnp.float32)
    decoded, decoder_saved = forward_block(
        start, tuple((array[1] for array in gathered[:10])), segments
    )
    weights_back = gather_weights(shards)
    encoder = tuple((array[0] for array in weights_back[:10]))
    decoder = tuple((array[1] for array in weights_back[:10]))
    start_grad, decoder_grads = backward_block(
        cotangent.astype(jnp.float32), start, decoder_saved, decoder, segments
    )
    start_low = start_grad.astype(jnp.bfloat16)
    decode_bias_grad = jnp.sum(start_low, axis=(0, 1), dtype=jnp.float32)
    decode_grad = jnp.einsum("stc,sti->ci", signs, start_low, preferred_element_type=jnp.float32)
    unit_grad = jnp.einsum(
        "sti,ci->stc", start_low, weights_back[11], preferred_element_type=jnp.float32
    )
    unit_rows, unit_back = jax.vjp(normalize, coded)
    coded_low = unit_back(unit_grad)[0].astype(jnp.bfloat16)
    encode_grad = jnp.einsum(
        "sti,stc->ic", encoded_low, coded_low, preferred_element_type=jnp.float32
    )
    encoded_grad = jnp.einsum(
        "stc,ic->sti", coded_low, weights_back[10], preferred_element_type=jnp.float32
    )
    unused, encoder_saved = forward_block(stream_in, encoder, segments)
    input_grad, encoder_grads = backward_block(
        encoded_grad, stream_in, encoder_saved, encoder, segments
    )
    pairs = tuple(
        (jnp.stack([first, second]) for first, second in zip(encoder_grads, decoder_grads))
    )
    totals = (
        lax.psum_scatter(pairs[0], ("slot", "seq"), scatter_dimension=2, tiled=True),
        lax.psum_scatter(pairs[1], ("slot", "seq"), scatter_dimension=2, tiled=True),
        lax.psum_scatter(pairs[2], ("slot", "seq"), scatter_dimension=1, tiled=True),
        lax.psum_scatter(pairs[3], ("slot", "seq"), scatter_dimension=2, tiled=True),
        lax.psum_scatter(pairs[4], ("slot", "seq"), scatter_dimension=1, tiled=True),
        lax.psum_scatter(pairs[5], ("slot", "seq"), scatter_dimension=1, tiled=True),
        lax.psum_scatter(pairs[6], ("slot", "seq"), scatter_dimension=1, tiled=True),
        lax.psum_scatter(pairs[7], ("slot", "seq"), scatter_dimension=1, tiled=True),
        lax.psum_scatter(pairs[8], ("slot", "seq"), scatter_dimension=1, tiled=True),
        lax.psum_scatter(pairs[9], ("slot", "seq"), scatter_dimension=1, tiled=True),
        lax.psum_scatter(encode_grad, ("slot", "seq"), scatter_dimension=0, tiled=True),
        lax.psum_scatter(decode_grad, ("slot", "seq"), scatter_dimension=1, tiled=True),
        lax.psum_scatter(decode_bias_grad, ("slot", "seq"), scatter_dimension=0, tiled=True),
    )
    return (decoded.astype(jnp.bfloat16), input_grad) + tuple(totals)


def solution(mesh):
    in_specs = (
        P("slot", "seq", None),
        P("slot", None),
        P("slot", "seq", None),
        P(None, None, ("slot", "seq")),
        P(None, None, ("slot", "seq")),
        P(None, ("slot", "seq"), None),
        P(None, None, ("slot", "seq")),
        P(None, ("slot", "seq"), None),
        P(None, ("slot", "seq")),
        P(None, ("slot", "seq"), None),
        P(None, ("slot", "seq")),
        P(None, ("slot", "seq"), None),
        P(None, ("slot", "seq")),
        P(("slot", "seq"), None),
        P(None, ("slot", "seq")),
        P(("slot", "seq")),
        P("slot", "seq", None),
    )
    out_specs = (
        P("slot", "seq", None),
        P("slot", "seq", None),
        P(None, None, ("slot", "seq")),
        P(None, None, ("slot", "seq")),
        P(None, ("slot", "seq"), None),
        P(None, None, ("slot", "seq")),
        P(None, ("slot", "seq"), None),
        P(None, ("slot", "seq")),
        P(None, ("slot", "seq"), None),
        P(None, ("slot", "seq")),
        P(None, ("slot", "seq"), None),
        P(None, ("slot", "seq")),
        P(("slot", "seq"), None),
        P(None, ("slot", "seq")),
        P(("slot", "seq")),
    )
    return jax.shard_map(
        on_device, mesh=mesh, in_specs=in_specs, out_specs=out_specs, check_vma=False
    )
```

```python
import functools

import jax
import jax.numpy as jnp
from jax import lax
from jax.experimental import pallas as pl
from jax.experimental.pallas import tpu as pltpu
from jax.sharding import PartitionSpec as P

HD = 64
CODE = 18
epsilon = 1e-06
masked_score = -1000000000.0
MESH = pl.DeviceIdType.MESH
F32 = jnp.float32
BF16 = jnp.bfloat16
AXES = ("slot", "seq")
BIG = 60 * 1024 * 1024

NN = (((1,), (0,)), ((), ()))
NT = (((1,), (1,)), ((), ()))
TN = (((0,), (0,)), ((), ()))


def mm(a, b, dims=NN):
    return lax.dot_general(a, b, dims, preferred_element_type=F32)


def params(**more):
    return pltpu.CompilerParams(vmem_limit_bytes=BIG, **more)


def whole(shape):
    return pl.BlockSpec(shape, lambda *i: (0,) * len(shape))


def shaped(shape, dtype=BF16):
    return jax.ShapeDtypeStruct(shape, dtype)


def norm_parts(stream):
    centre = stream - jnp.mean(stream, axis=-1, keepdims=True)
    spread = jnp.mean(centre * centre, axis=-1, keepdims=True)
    scale = lax.rsqrt(spread + epsilon)
    return centre * scale, scale


def norm_back(grad, gain, hat, scale):
    lifted = grad * gain
    mean = jnp.mean(lifted, axis=-1, keepdims=True)
    mixed = jnp.mean(lifted * hat, axis=-1, keepdims=True)
    return scale * (lifted - mean - hat * mixed)


def columns(value):
    return jnp.sum(value, axis=0, keepdims=True)


def lanes_of(head):
    lane = lax.broadcasted_iota(jnp.int32, (1, 2 * HD), 1)
    return lane < HD if head == 0 else lane >= HD


def only(value, head):
    return jnp.where(lanes_of(head), value, jnp.zeros_like(value))


def gelu_parts(hidden):
    normal = 0.5 + 0.5 * lax.erf(hidden * 0.7071067811865476)
    density = jnp.exp(-0.5 * hidden * hidden) * 0.3989422804014327
    return hidden * normal, normal + hidden * density


def flip(index, bit):
    size = 1 << bit
    return index + size - 2 * size * ((index // size) % 2)


def relative(a, b):
    return 2 * ((a // 2 + b // 2) % 2) + (a + b) % 2


PARTS = 4
DMA = pltpu.SemaphoreType.DMA


def remote(src, dst, send, recv, peer):
    return pltpu.make_async_remote_copy(
        src_ref=src, dst_ref=dst, send_sem=send, recv_sem=recv, device_id=peer, device_id_type=MESH
    )


class Here:
    def __init__(self):
        self.slot, self.z = lax.axis_index("slot"), lax.axis_index("seq")
        self.across = (flip(self.slot, 1), self.z)
        self.beside = (flip(self.slot, 2), self.z)
        self.sibling = (flip(self.slot, 0), self.z)
        self.core, self.square = lax.rem(self.slot, 2), self.slot // 2

    def along(self, k):
        return (self.slot, relative(self.z, k))

    def greet(self):
        barrier = pltpu.get_barrier_semaphore()
        peers = [self.across, self.beside, self.sibling] + [self.along(k) for k in range(1, PARTS)]
        for peer in peers:
            pl.semaphore_signal(barrier, inc=1, device_id=peer, device_id_type=MESH)
        pl.semaphore_wait(barrier, len(peers))


class Line:
    @staticmethod
    def scratch(count):
        return [DMA((count, PARTS))] * 3

    def __init__(self, here, arrays, sems, sources, absolute):
        self.here, self.arrays, self.sources, self.absolute = here, arrays, sources, absolute
        self.recv, self.up, self.down = sems

    def at(self, m, block, z):
        return self.arrays[m].at[block if self.absolute[m] else relative(block, z)]

    def copy(self, m, block, upward):
        z = self.here.z
        to = jnp.minimum(z + 1, PARTS - 1) if upward else jnp.maximum(z - 1, 0)
        send = (self.up if upward else self.down).at[m, block]
        src = self.sources[m] if self.sources is not None and block is z else self.at(m, block, z)
        return remote(src, self.at(m, block, to), send, self.recv.at[m, block], (self.here.slot, to))

    def onward(self, m, block, upward):
        z = self.here.z

        @pl.when((z < PARTS - 1) if upward else (z > 0))
        def _():
            self.copy(m, block, upward).start()

    def start(self, m):
        self.onward(m, self.here.z, True)
        self.onward(m, self.here.z, False)

    def hop(self, m, k):
        z = self.here.z

        @pl.when(z >= k)
        def _():
            self.copy(m, z - k, True).wait_recv()
            self.onward(m, z - k, True)

        @pl.when(z + k <= PARTS - 1)
        def _():
            self.copy(m, z + k, False).wait_recv()
            self.onward(m, z + k, False)

    def finish(self, m):
        z = self.here.z
        for block in range(PARTS):

            @pl.when((z < PARTS - 1) & (z >= block))
            def _():
                self.copy(m, block, True).wait_send()

            @pl.when((z > 0) & (z <= block))
            def _():
                self.copy(m, block, False).wait_send()


class Hop:
    @staticmethod
    def scratch():
        return [DMA((4,))]

    def __init__(self, here, k, source, out, sems):
        self.here, self.k, self.source, self.out, self.sems = here, k, source, out, sems[0]

    def copy(self, upward, block):
        z = self.here.z
        to = jnp.minimum(z + 1, PARTS - 1) if upward else jnp.maximum(z - 1, 0)
        src = self.source if self.k == 1 else self.source.at[relative(block, z)]
        n = 0 if upward else 2
        return remote(src, self.out.at[relative(block, to)], self.sems.at[n], self.sems.at[n + 1], (self.here.slot, to))

    def start(self, wait=False):
        z, back = self.here.z, self.k - 1
        for upward, meets in ((True, (z >= back) & (z < PARTS - 1)), (False, (z + back <= PARTS - 1) & (z > 0))):

            @pl.when(meets)
            def _():
                move = self.copy(upward, z - back if upward else z + back)
                move.wait_send() if wait else move.start()

    def finish(self):
        z, k = self.here.z, self.k
        for upward, meets in ((True, z >= k), (False, z + k <= PARTS - 1)):

            @pl.when(meets)
            def _():
                self.copy(upward, jnp.clip(z, 0, PARTS - 1)).wait_recv()

        self.start(True)


class Gather:
    @staticmethod
    def scratch(count):
        return [DMA((count, PARTS))] * 5 + [DMA((count,))] * 8

    def __init__(self, here, sources, outs, sems):
        self.here, self.sources, self.outs = here, sources, outs
        self.rz, self.up, self.down, self.rx, self.ry = sems[:5]
        self.local, self.sx, self.sy, self.rd, self.dx, self.dy, self.rc, self.sc = sems[5:]

    def place(self, m, block):
        return self.outs[m].at[self.here.slot, block]

    def copy(self, m, block, upward, src):
        z = self.here.z
        to = jnp.minimum(z + 1, PARTS - 1) if upward else jnp.maximum(z - 1, 0)
        send = (self.up if upward else self.down).at[m, block]
        return remote(src, self.place(m, block), send, self.rz.at[m, block], (self.here.slot, to))

    def onward(self, m, block, upward, src):
        z = self.here.z

        @pl.when((z < PARTS - 1) if upward else (z > 0))
        def _():
            self.copy(m, block, upward, src).start()

    def sideways(self, m, block, src):
        dst = self.place(m, block)
        remote(src, dst, self.sx.at[m], self.rx.at[m, block], self.here.across).start()
        remote(src, dst, self.sy.at[m], self.ry.at[m, block], self.here.beside).start()

    def keep(self, m):
        return pltpu.make_async_copy(self.sources[m], self.place(m, self.here.z), self.local.at[m])

    def start(self, m):
        src, z = self.sources[m], self.here.z
        self.onward(m, z, True, src)
        self.onward(m, z, False, src)
        self.sideways(m, z, src)
        self.keep(m).start()

    def arrived(self, m, block, upward):
        src = self.place(m, block)
        self.copy(m, block, upward, src).wait_recv()
        self.onward(m, block, upward, src)
        self.sideways(m, block, src)

    def hop(self, m, k):
        z = self.here.z

        @pl.when(z >= k)
        def _():
            self.arrived(m, z - k, True)

        @pl.when(z + k <= PARTS - 1)
        def _():
            self.arrived(m, z + k, False)

    def turned(self, m, block):
        across, beside = self.here.across, self.here.beside
        here = self.outs[m].at[across[0], block]
        remote(here, here, self.sx.at[m], self.rx.at[m, block], across).wait_recv()

        @pl.when(lax.rem(block, 2) == 0)
        def _():
            remote(here, here, self.dy.at[m], self.rd.at[m], beside).start()

        there = self.outs[m].at[beside[0], block]
        remote(there, there, self.sy.at[m], self.ry.at[m, block], beside).wait_recv()

        @pl.when(lax.rem(block, 2) == 1)
        def _():
            remote(there, there, self.dx.at[m], self.rd.at[m], across).start()

    def turn(self, m, k):
        z = self.here.z
        if k == 0:
            self.turned(m, z)
            return

        @pl.when(z >= k)
        def _():
            self.turned(m, z - k)

        @pl.when(z + k <= PARTS - 1)
        def _():
            self.turned(m, z + k)

    def share(self, m, slot):
        group = self.outs[m].at[slot]
        remote(group, group, self.sc.at[m], self.rc.at[m], self.here.sibling).start()

    def siblings(self, m):
        self.keep(m).wait()
        for slot in (self.here.slot, self.here.across[0], self.here.beside[0]):
            self.share(m, slot)

    def corner(self, m):
        slot = flip(self.here.across[0], 2)
        group = self.outs[m].at[slot]
        remote(group, group, self.dx.at[m], self.rd.at[m], self.here.across).wait_recv()
        self.share(m, slot)

    def finish(self, m):
        here, z, src = self.here, self.here.z, self.sources[m]
        for block in range(PARTS):

            @pl.when((z < PARTS - 1) & (z >= block))
            def _():
                self.copy(m, block, True, src).wait_send()

            @pl.when((z > 0) & (z <= block))
            def _():
                self.copy(m, block, False, src).wait_send()

        group = self.outs[m].at[here.slot]
        half = self.outs[m].at[here.slot, pl.ds(0, PARTS // 2)]
        remote(group, group, self.sx.at[m], self.rx.at[m, 0], here.across).wait_send()
        remote(group, group, self.sy.at[m], self.ry.at[m, 0], here.beside).wait_send()
        remote(half, half, self.dx.at[m], self.rd.at[m], here.across).wait_send()
        remote(half, half, self.dy.at[m], self.rd.at[m], here.beside).wait_send()
        four = self.outs[m].at[pl.ds(0, 4)]
        both = remote(four, four, self.sc.at[m], self.rc.at[m], here.sibling)
        both.wait_send()
        both.wait_recv()


class Spread:
    @staticmethod
    def scratch(count):
        return [DMA((11, count))]

    def __init__(self, here, sources, outs, sems):
        self.here, self.sources, self.outs, self.sems = here, sources, outs, sems[0]

    def sem(self, m, n):
        return self.sems.at[n, m]

    def keep(self, m):
        return pltpu.make_async_copy(self.sources[m], self.outs[m].at[self.here.slot], self.sem(m, 0))

    def share(self, m, src, slot):
        remote(src, self.outs[m].at[slot], self.sem(m, 1), self.sem(m, 2), self.here.sibling).start()

    def side(self, m, n, src, slot):
        peer = self.here.beside if n else self.here.across
        return remote(src, self.outs[m].at[slot], self.sem(m, 3 + 2 * n), self.sem(m, 4 + 2 * n), peer)

    def half(self, m, n, slot):
        ref = self.outs[m].at[slot, pl.ds(n * (PARTS // 2), PARTS // 2)]
        peer = self.here.across if n else self.here.beside
        return remote(ref, ref, self.sem(m, 7 + 2 * n), self.sem(m, 8 + 2 * n), peer)

    def start(self, m):
        src, slot = self.sources[m], self.here.slot
        for n in range(2):
            self.side(m, n, src, slot).start()
        self.keep(m).start()
        self.share(m, src, slot)

    def turn(self, m):
        for n, peer in enumerate((self.here.across, self.here.beside)):
            ref = self.outs[m].at[peer[0]]
            self.side(m, n, ref, peer[0]).wait_recv()
            self.half(m, n, peer[0]).start()
            self.share(m, ref, peer[0])

    def corner(self, m):
        slot = flip(self.here.across[0], 2)
        for n in range(2):
            self.half(m, n, slot).wait_recv()
        self.share(m, self.outs[m].at[slot], slot)

    def finish(self, m):
        self.keep(m).wait()
        for n in range(2):
            self.side(m, n, self.sources[m], self.here.slot).wait_send()
            self.half(m, n, self.here.slot).wait_send()
        four = self.outs[m].at[pl.ds(0, 4)]
        both = remote(four, four, self.sem(m, 1), self.sem(m, 2), self.here.sibling)
        both.wait_send()
        both.wait_recv()


def add_into(target, source):
    def one(a, carry):
        target[a] = (target[a].astype(F32) + source[a].astype(F32)).astype(target.dtype)
        return carry

    lax.fori_loop(0, target.shape[0], one, 0)


class Square:
    @staticmethod
    def scratch(units, tail, loaded):
        held = [pltpu.VMEM((4, PARTS, units) + tail, BF16)] if loaded else []
        half = pltpu.VMEM((PARTS // 2, units) + tail, BF16)
        full = pltpu.VMEM((PARTS, units) + tail, BF16)
        return held + [half, half, full, full, DMA((9,))]

    def __init__(self, here, held, scratch, source=None):
        self.here, self.held, self.source = here, held, source
        self.corner_x, self.corner_y, self.side_x, self.side_y, self.sems = scratch

    def load(self, start=True):
        copy = pltpu.make_async_copy(self.source, self.held, self.sems.at[8])
        copy.start() if start else copy.wait()

    def move(self, n):
        half, held, sems = PARTS // 2, self.held, self.sems
        src = (held.at[3, pl.ds(0, half)], held.at[3, pl.ds(half, half)], held.at[1], held.at[2])[n]
        dst = (self.corner_x, self.corner_y, self.side_x, self.side_y)[n]
        peer = self.here.beside if n % 2 else self.here.across
        return remote(src, dst, sems.at[2 * n], sems.at[2 * n + 1], peer)

    def start(self):
        if self.source is not None:
            self.load(False)
        for n in range(2):
            self.move(n).start()

    def sides(self):
        half = PARTS // 2
        self.move(0).wait_recv()
        add_into(self.held.at[2, pl.ds(0, half)], self.corner_x)
        self.move(3).start()
        self.move(1).wait_recv()
        add_into(self.held.at[1, pl.ds(half, half)], self.corner_y)
        self.move(2).start()

    def total(self, out):
        self.move(2).wait_recv()
        self.move(3).wait_recv()

        def one(a, carry):
            value = self.held[0, a].astype(F32) + self.side_x[a].astype(F32) + self.side_y[a].astype(F32)
            out[a] = value.astype(out.dtype)
            return carry

        lax.fori_loop(0, PARTS, one, 0)
        for n in range(4):
            self.move(n).wait_send()


class Stack:
    @staticmethod
    def scratch(units, tail):
        return [pltpu.VMEM((PARTS - 1, units) + tail, BF16), DMA((2, PARTS))]

    def __init__(self, here, held, scratch):
        self.here, self.held = here, held
        self.arrived, self.sems = scratch

    def moves(self):
        for k in range(1, PARTS):
            peer = self.here.along(k)
            yield remote(self.held.at[peer[1]], self.arrived.at[k - 1], self.sems.at[0, k], self.sems.at[1, k], peer)

    def start(self):
        for move in self.moves():
            move.start()

    def finish(self, out):
        for move in self.moves():
            move.wait_recv()
        units, z = out.shape[0], self.here.z

        def one(unit, carry):
            value = self.held[z, unit].astype(F32)
            for k in range(PARTS - 1):
                value += self.arrived[k, unit].astype(F32)
            out[unit] = value
            return carry

        lax.fori_loop(0, units, one, 0)
        for move in self.moves():
            move.wait_send()


class Sum:
    @staticmethod
    def scratch(rows, width):
        table, low = pltpu.VMEM((4, rows, width), F32), pltpu.VMEM((rows, width), BF16)
        return [table, pltpu.VMEM((3, rows, width), F32), low, pltpu.VMEM((PARTS - 1, rows, width), BF16), DMA((2, 6))]

    def __init__(self, here, sources, scratch):
        self.here, self.sources = here, sources
        self.tables, self.arrived, self.low, self.arrived_low, self.sems = scratch
        self.peers = (here.sibling, here.across, here.beside)

    def move(self, stage):
        sems = self.sems
        return remote(self.tables.at[stage], self.arrived.at[stage], sems.at[0, stage], sems.at[1, stage], self.peers[stage])

    def stack(self, k):
        sems = self.sems
        return remote(self.low, self.arrived_low.at[k - 1], sems.at[0, 2 + k], sems.at[1, 2 + k], self.here.along(k))

    def begin(self):
        tables = self.tables
        tables[0] = jnp.zeros_like(tables[0])
        width = tables.shape[2]
        at = 0
        for source in self.sources:
            rows, columns_held = source.shape
            for start in range(0, columns_held, width):
                tables[0, at : at + rows, :] = source[:, start : start + width]
                at += rows
        self.move(0).start()

    def meet(self, stage):
        self.move(stage).wait_recv()
        self.tables[stage + 1] = self.tables[stage] + self.arrived[stage]
        if stage < 2:
            self.move(stage + 1).start()
        else:
            self.low[...] = self.tables[3].astype(BF16)
            for k in range(1, PARTS):
                self.stack(k).start()

    def finish(self, out):
        value = self.tables[3]
        for k in range(1, PARTS):
            self.stack(k).wait_recv()
            value += self.arrived_low[k - 1].astype(F32)
        out[...] = value
        for stage in range(3):
            self.move(stage).wait_send()
        for k in range(1, PARTS):
            self.stack(k).wait_send()


class Cores:
    @staticmethod
    def scratch(units, tail):
        return [pltpu.VMEM((4, PARTS, units) + tail, BF16), pltpu.VMEM((2, 8, PARTS) + tail, BF16), DMA((units,)), DMA((units,))]

    def __init__(self, here, sums, scratch, hidden):
        self.here, self.sums, self.hidden = here, sums, hidden
        self.far, self.turn, self.send, self.recv = scratch

    def moves(self, n, hidden):
        here, slot = self.here, lax.rem(n, 2)
        give = 1 - here.core
        if hidden:
            to = self.far.at[relative(here.square, n), :, pl.ds(0, self.hidden)]
            return [(self.turn.at[slot, pl.ds(4 * give, 4)], to)], to
        pairs = [(self.turn.at[slot, 2 * s + give], self.far.at[relative(here.square, s), :, n]) for s in range(4)]
        return pairs, self.far.at[:, :, n]

    def each(self, n, action):
        if self.hidden:

            @pl.when(n < self.hidden)
            def _():
                action(True)

            @pl.when(n >= self.hidden)
            def _():
                action(False)
        else:
            action(False)

    def waited(self, n, hidden, recv):
        whole_ref = self.moves(n, hidden)[1]
        move = remote(whole_ref, whole_ref, self.send.at[n], self.recv.at[n], self.here.sibling)
        move.wait_recv() if recv else move.wait_send()

    def put(self, n, value):
        here, slot = self.here, lax.rem(n, 2)

        @pl.when(n >= 2)
        def _():
            self.each(n - 2, lambda hidden: self.waited(n - 2, hidden, False))

        self.turn[slot] = value.reshape(self.turn.shape[1:]).astype(BF16)

        def action(hidden):
            for src, dst in self.moves(n, hidden)[0]:
                remote(src, dst, self.send.at[n], self.recv.at[n], here.sibling).start()
            if hidden:
                self.sums[relative(here.square, n), :, pl.ds(0, self.hidden)] = self.turn[slot, pl.ds(4 * here.core, 4)]
            else:
                for s in range(4):
                    self.sums[relative(here.square, s), :, n] = self.turn[slot, 2 * s + here.core]

        self.each(n, action)

    def collect(self, n):
        def action(hidden):
            self.waited(n, hidden, True)
            if hidden:
                at = relative(self.here.square, n)
                add_into(self.sums.at[at, :, pl.ds(0, self.hidden)], self.far.at[at, :, pl.ds(0, self.hidden)])
            else:

                def one(s, carry):
                    value = self.sums[s, :, n].astype(F32) + self.far[s, :, n].astype(F32)
                    self.sums[s, :, n] = value.astype(BF16)
                    return carry

                lax.fori_loop(0, 4, one, 0)

        self.each(n, action)

    def finish(self, count):
        for n in (count - 2, count - 1):
            self.waited(n, n < self.hidden, False)


class Item:
    def __init__(self, array, spec=None):
        self.array = array
        self.spec = spec or whole(array.shape)


def anywhere(array):
    return Item(array, pl.BlockSpec(memory_space=pl.ANY))


def run(body, steps, ins, outs, scratch, collective, name, cost):
    in_names, out_names, scratch_names = list(ins), list(outs), list(scratch)
    flat_scratch, spans = [], {}
    for key in scratch_names:
        item = scratch[key]
        many = isinstance(item, list)
        spans[key] = (len(flat_scratch), len(item) if many else None)
        flat_scratch += item if many else [item]

    def kernel(*refs):
        first, second = len(in_names), len(in_names) + len(out_names)
        in_refs = dict(zip(in_names, refs[:first]))
        out_refs = dict(zip(out_names, refs[first:second]))
        rest = refs[second:]
        own = {k: rest[at] if n is None else rest[at : at + n] for k, (at, n) in spans.items()}
        here = Here()
        step = pl.program_id(0)

        @pl.when(step == 0)
        def _():
            here.greet()

        body(here, step, in_refs, out_refs, own)

    results = pl.pallas_call(
        kernel,
        grid=(steps,),
        in_specs=[i.spec for i in ins.values()],
        out_specs=tuple(o.spec for o in outs.values()),
        out_shape=tuple(o.array for o in outs.values()),
        scratch_shapes=flat_scratch,
        compiler_params=pltpu.CompilerParams(
            vmem_limit_bytes=BIG, collective_id=collective, has_side_effects=True, dimension_semantics=("arbitrary",)
        ),
        cost_estimate=pl.CostEstimate(flops=cost * 1150000000, bytes_accessed=0, transcendentals=0),
        name=name,
    )(*[i.array for i in ins.values()])
    return dict(zip(out_names, results))


def at_step(step, n):
    def decorate(action):
        pl.when(step == n)(action)

    return decorate


def first_kernel(here, step, ins, outs, own):
    table = own["table"]
    table[...] = jnp.zeros_like(table)
    gain, shift, query_value = ins["gain"], ins["shift"], ins["query_value"]
    for start, item in ((0, gain), (4, shift), (8, query_value)):
        for i in range(4):
            table[start + i : start + i + 1, :] = item[i // 2, i % 2 : i % 2 + 1, :].astype(F32)
    table[12:14, :] = ins["output_bias"][...].astype(F32)
    table[14:16, :] = ins["shrink_bias"][...].astype(F32)
    table[16:17, :] = ins["decode_bias"][...].astype(F32)
    fine = gain.shape[2]
    wide = ins["expand_bias"][...].astype(F32)
    for i in range(8):
        table[17 + i : 18 + i, :] = wide[i // 4 : i // 4 + 1, fine * (i % 4) : fine * (i % 4 + 1)]
    table[25:43, :] = ins["encode"][...].astype(F32).T
    table[43:61, :] = ins["decode"][...].astype(F32)
    gather = Gather(here, [table, ins["project"].at[0]], [outs["table"], outs["project"]], own["gather"])
    signs = ins["signs"].at[0]
    line = Line(here, [outs["signs"]], own["line"], [signs], (False,))
    keep = pltpu.make_async_copy(signs, outs["signs"].at[0], own["keep"].at[0])
    patches = Hop(here, 1, ins["patches"].at[0], outs["patches"], own["patches"])
    for m in range(2):
        gather.start(m)
    line.start(0)
    keep.start()
    patches.start()
    for k in range(1, PARTS):
        for m in range(2):
            gather.hop(m, k)
        line.hop(0, k)
        for m in range(2):
            gather.turn(m, k - 1)
    for m in range(2):
        gather.turn(m, PARTS - 1)
        gather.siblings(m)
    for m in range(2):
        gather.corner(m)
    for m in range(2):
        gather.finish(m)
    line.finish(0)
    patches.finish()
    keep.wait()


def forward_attention(coded, layer, slots, ins, extra, collective):
    weight = ins["weight"].array
    rows = ins["segment_column"].array.shape[0]
    width, triple = weight.shape
    length = PARTS * rows
    pairs, lanes = width // (2 * HD), 2 * HD
    steps = PARTS + pairs
    outs = {
        "qkv": Item(shaped((length, triple)), pl.BlockSpec((rows, triple), lambda i: (jnp.minimum(i, PARTS - 1), 0))),
        "normed": Item(shaped((rows, width))),
        "mixed": Item(shaped((rows, width)), pl.BlockSpec((rows, lanes), lambda i: (0, jnp.maximum(i - PARTS, 0)))),
        "logs": Item(shaped((rows, 128), F32)),
    }
    if coded:
        outs["stream"] = Item(shaped((rows, width), F32))
    scratch = {"qkv_held": pltpu.VMEM((length, triple), BF16), "piece": pltpu.VMEM((rows, width), BF16)}
    extra.declare(ins, outs, scratch)

    def body(here, step, ins, outs, own):
        extra.events(here, step, steps, ins, outs, own)
        table = ins["table"]
        held = own["qkv_held"]

        @pl.when(step < PARTS)
        def _():
            if coded:
                decode = table[43:61, :].astype(BF16)
                stream = mm(ins["pieces"][step], decode) + table[16:17, :]
            else:
                inner = (here.z > 0) & (here.z < PARTS - 1)
                choices = [step == 0, step == 1, step == 2, (step == 3) & inner, (step == 3) & jnp.logical_not(inner)]
                for n, meets in enumerate(choices):

                    @pl.when(meets)
                    def _():
                        own["piece"][...] = ins[f"piece{n}"][0]

                stream = own["piece"][...].astype(F32)
            hat, unused = norm_parts(stream)
            normed = (hat * table[2 * layer : 2 * layer + 1, :] + table[4 + 2 * layer : 5 + 2 * layer, :]).astype(BF16)
            at = pl.ds(pl.multiple_of(step * rows, rows), rows)
            for part in range(3):
                span = pl.ds(part * width, width)
                value = mm(normed, ins["weight"][:, span])
                if part != 1:
                    shift = 8 + 2 * layer + part // 2
                    value += table[shift : shift + 1, :]
                value = value.astype(BF16)
                outs["qkv"][:, span] = value
                held[at, span] = value

            @pl.when(step == 0)
            def _():
                outs["normed"][...] = normed
                if coded:
                    outs["stream"][...] = stream

        @pl.when(step >= PARTS)
        def _():
            pair = step - PARTS
            logs = outs["logs"]
            lane = lax.broadcasted_iota(jnp.int32, (1, 128), 1)

            @pl.when(pair == 0)
            def _():
                logs[...] = jnp.zeros_like(logs)

            def span(part):
                return pl.ds(pl.multiple_of(part * width + pair * lanes, lanes), lanes)

            keys, values = held[:, span(1)], held[:, span(2)]
            segments = ins["segment_row"][...]
            for start in range(0, rows, BLOCK):
                at = pl.ds(start, BLOCK)
                same = ins["segment_column"][at, :] == segments
                queries = held[at, span(0)] * jnp.asarray(HD**-0.5, BF16)
                parts = []
                for head in range(2):
                    scores = jnp.where(same, mm(only(queries, head), keys, NT), masked_score)
                    top = jnp.max(scores, axis=-1, keepdims=True)
                    raised = jnp.exp(scores - top)
                    total = jnp.sum(raised, axis=-1, keepdims=True)
                    parts.append(mm(raised.astype(BF16), values) / total)
                    logs[at, :] += jnp.where(lane == 2 * pair + head, top + jnp.log(total), 0.0)
                outs["mixed"][at, :] = jnp.where(lanes_of(0), parts[0], parts[1]).astype(BF16)

        extra.closing(here, step, steps, ins, outs, own)

    return run(body, steps, ins, outs, scratch, collective, "forward_attention", 30)


BLOCK = 192
QUERY_BLOCK = 384


def middle_block(encoder, layer, slots, ins, extra, collective):
    width = ins["output"].array.shape[1]
    rows = ins["mixed"].array.shape[0]
    hidden = ins["shrink"].array.shape[0]
    fine = width // slots // PARTS
    tile = 512
    tiles = hidden // tile
    feed = 2 * tiles if encoder else tiles
    units = hidden // width + hidden // width + 1
    wide = hidden // width
    pairs, lanes = width // (2 * HD), 2 * HD
    length = PARTS * rows
    first_query = feed + units
    first_key = first_query + pairs
    steps = first_key + 2 * pairs

    def tiled(i):
        return lax.rem(jnp.minimum(i, feed - 1), tiles)

    ins["expand"].spec = pl.BlockSpec((width, tile), lambda i: (0, tiled(i)))
    ins["expand_shift"].spec = pl.BlockSpec((1, tile), lambda i: (0, tiled(i)))
    ins["shrink"].spec = pl.BlockSpec((tile, width), lambda i: (tiled(i), 0))
    ins["stream"].spec = pl.BlockSpec((1, rows, width), lambda i: (0, 0, 0))
    outs = {
        "query": Item(shaped((rows, width)), pl.BlockSpec((rows, lanes), lambda i: (0, jnp.clip(i - first_query, 0, pairs - 1)))),
        "key": Item(shaped((rows, width)), pl.BlockSpec((rows, lanes), lambda i: (0, jnp.maximum(i - first_key - pairs, 0)))),
        "value": Item(shaped((rows, width)), pl.BlockSpec((rows, lanes), lambda i: (0, jnp.maximum(i - first_key - pairs, 0)))),
        "middle": Item(shaped((rows, width), F32)),
        "small": Item(shaped((8, width), F32)),
        "wide": Item(shaped((1, hidden), F32)),
    }
    scratch = {
        "active": pltpu.VMEM((rows, hidden), BF16),
        "hidden_low": pltpu.VMEM((rows, hidden), BF16),
        "normed": pltpu.VMEM((rows, width), BF16),
        "hat": pltpu.VMEM((rows, width), F32),
        "scale": pltpu.VMEM((rows, 1), F32),
        "total": pltpu.VMEM((rows, width), F32),
        "back": pltpu.VMEM((rows, width), F32),
        "low": pltpu.VMEM((rows, width), BF16),
        "branch": pltpu.VMEM((rows, width), BF16),
        "delta": pltpu.VMEM((rows, 128), F32),
        "qkv_held": pltpu.VMEM((length, 3 * width), BF16),
        "qkv_sem": DMA((1,)),
        "mixed_back": pltpu.VMEM((PARTS, rows, width), BF16),
        "stats": pltpu.VMEM((PARTS, 32, rows), F32),
        "line": Line.scratch(2),
        "cores": Cores.scratch(units, (fine, width)),
    }
    if encoder:
        outs["code_grad"] = Item(shaped((CODE, width), F32))
        scratch["slope"] = pltpu.VMEM((tiles, rows, tile), BF16)
        scratch["sums"] = pltpu.VMEM((4, PARTS, units, fine, width), BF16)
    else:
        outs["decoded"] = Item(shaped((rows, width)))
        outs["sums"] = Item(shaped((4, PARTS, units, fine, width)))
    extra.declare(ins, outs, scratch)

    def body(here, step, ins, outs, own):
        table = ins["table"]
        normed, hat, scale, total, back, low = (own[n] for n in ("normed", "hat", "scale", "total", "back", "low"))
        mixed_back, stats, held = own["mixed_back"], own["stats"], own["qkv_held"]
        sums = own["sums"] if encoder else outs["sums"]
        cores = Cores(here, sums, own["cores"], wide)
        line = Line(here, [mixed_back, stats], own["line"], None, (False, False))
        load = pltpu.make_async_copy(ins["qkv"], held, own["qkv_sem"].at[0])
        gain, shift = table[2 * layer + 1 : 2 * layer + 2, :], table[5 + 2 * layer : 6 + 2 * layer, :]
        extra.events(here, step, steps, ins, outs, own)

        @at_step(step, 0)
        def _():
            load.start()
            middle = ins["stream"][0].astype(F32) + mm(ins["mixed"][...], ins["output"][...]) + table[12 + layer : 13 + layer, :]
            hat[...], scale[...] = norm_parts(middle)
            normed[...] = (hat[...] * gain + shift).astype(BF16)
            total[...] = middle + table[14 + layer : 15 + layer, :]
            back[...] = jnp.zeros_like(back)
            if not encoder:
                low[...] = ins["other"][...]

        def columns_at(n):
            return pl.ds(pl.multiple_of(n * tile, tile), tile)

        def forward(n):
            value = mm(normed[...], ins["expand"][...]) + ins["expand_shift"][...]
            active, steep = gelu_parts(value)
            active = active.astype(BF16)
            own["active"][:, columns_at(n)] = active
            total[...] += mm(active, ins["shrink"][...])
            return steep

        def backward(n, steep):
            hidden_low = (steep * mm(low[...], ins["shrink"][...], NT)).astype(BF16)
            own["hidden_low"][:, columns_at(n)] = hidden_low
            outs["wide"][:, columns_at(n)] = columns(hidden_low.astype(F32))
            back[...] += mm(hidden_low, ins["expand"][...], NT)

        if encoder:

            @pl.when(step < tiles)
            def _():
                own["slope"][step] = forward(step).astype(BF16)

            @at_step(step, tiles - 1)
            def _():
                code = table[25:43, :].astype(BF16)
                encoded_low = total[...].astype(BF16)
                coded = mm(encoded_low, code, NT)
                size = lax.rsqrt(jnp.sum(coded * coded, axis=-1, keepdims=True) + epsilon)
                unit = coded * size
                grad = ins["other"][...]
                coded_low = ((grad - unit * jnp.sum(unit * grad, axis=-1, keepdims=True)) * size).astype(BF16)
                outs["code_grad"][...] = mm(coded_low, encoded_low, TN)
                total[...] = mm(coded_low, code)
                low[...] = total[...].astype(BF16)

            @pl.when((step >= tiles) & (step < feed))
            def _():
                backward(step - tiles, own["slope"][step - tiles].astype(F32))
        else:

            @pl.when(step < tiles)
            def _():
                backward(step, forward(step))

        @at_step(step, feed - 1)
        def _():
            if encoder:
                grad_out = total[...]
            else:
                outs["decoded"][...] = total[...].astype(BF16)
                grad_out = low[...].astype(F32)
            grad = back[...]
            middle = grad_out + norm_back(grad, gain, hat[...], scale[...])
            outs["middle"][...] = middle
            branch = middle.astype(BF16)
            own["branch"][...] = branch
            mixed_low = mm(branch, ins["output"][...], NT).astype(BF16)
            mixed_back[0] = mixed_low
            product = mixed_low.astype(F32) * ins["mixed"][...].astype(F32)
            feature = lax.broadcasted_iota(jnp.int32, (width, 128), 0) // HD
            heads = (feature == lax.broadcasted_iota(jnp.int32, (width, 128), 1)).astype(F32)
            delta = lax.dot_general(product, heads, NN, preferred_element_type=F32, precision=lax.Precision.HIGHEST)
            own["delta"][...] = delta
            stats[0, pl.ds(0, 16)] = ins["logs"][...].T[:16]
            stats[0, pl.ds(16, 16)] = delta.T[:16]
            for m in range(2):
                line.start(m)
            outs["small"][...] = jnp.concatenate(
                [columns(grad * hat[...]), columns(grad), columns(branch.astype(F32)), columns(low[...].astype(F32))]
                + [jnp.zeros_like(columns(grad))] * 4
            )

        unit = step - feed

        def wide_at(n):
            return pl.ds(pl.multiple_of(n * width, width), width)

        @pl.when((unit >= 0) & (unit < wide))
        def _():
            cores.put(unit, mm(own["active"][:, wide_at(unit)], low[...], TN))

        @pl.when((unit >= wide) & (unit < 2 * wide))
        def _():
            cores.put(unit, mm(normed[...], own["hidden_low"][:, wide_at(unit - wide)], TN))

        @pl.when(unit == 2 * wide)
        def _():
            cores.put(unit, mm(ins["mixed"][...], own["branch"][...], TN))

        @pl.when((unit >= 2) & (unit < units))
        def _():
            cores.collect(unit - 2)

        @pl.when(unit == units)
        def _():
            cores.collect(unit - 2)
            cores.collect(unit - 1)
            cores.finish(units)

        for n, k in ((units - 1, 1), (units + 3, 2)):

            @pl.when(unit == n)
            def _():
                for m in range(2):
                    line.hop(m, k)

        @at_step(step, first_query)
        def _():
            load.wait()

        eighth = jnp.asarray(HD**-0.5, BF16)

        @pl.when((step >= first_query) & (step < first_key))
        def _():
            pair = step - first_query
            lane = lax.broadcasted_iota(jnp.int32, (1, 128), 1)

            def span(part):
                return pl.ds(pl.multiple_of(part * width + pair * lanes, lanes), lanes)

            keys, values = held[:, span(1)], held[:, span(2)]
            segments = ins["segment_row"][...]
            for start in range(0, rows, QUERY_BLOCK):
                at = pl.ds(start, QUERY_BLOCK)
                same = ins["segment_column"][at, :] == segments
                queries = held[at, span(0)] * eighth
                grads = mixed_back[0, at, span(0)]
                parts = []
                for head in range(2):
                    mine = lane == 2 * pair + head
                    log_sum = jnp.sum(jnp.where(mine, ins["logs"][at, :], 0.0), axis=-1, keepdims=True)
                    centre = jnp.sum(jnp.where(mine, own["delta"][at, :], 0.0), axis=-1, keepdims=True)
                    scores = jnp.where(same, mm(only(queries, head), keys, NT), masked_score)
                    probability = jnp.exp(scores - log_sum)
                    prob_grad = mm(only(grads, head), values, NT)
                    score_low = (probability * (prob_grad - centre)).astype(BF16)
                    parts.append(mm(score_low, keys) * HD**-0.5)
                outs["query"][at, :] = jnp.where(lanes_of(0), parts[0], parts[1]).astype(BF16)

        late = step - first_key

        @pl.when(late == pairs)
        def _():
            for m in range(2):
                line.hop(m, 3)

        for half in range(2):

            @pl.when((late >= half * pairs) & (late < (half + 1) * pairs))
            def _():
                pair = late - half * pairs
                pieces = range(2 * half, 2 * half + 2)

                def span(part):
                    return pl.ds(pl.multiple_of(part * width + pair * lanes, lanes), lanes)

                these = pl.ds(2 * half * rows, 2 * rows)
                queries = held[these, span(0)]
                grads = mixed_back[2 * half : 2 * half + 2, :, span(0)].reshape(2 * rows, lanes)

                def line_of(row):
                    return jnp.concatenate([stats[k, pl.ds(row, 1), :] for k in pieces], axis=1)

                same = ins["segment_column"][...] == ins["segment_row"][:, these]
                keys = held[pl.ds(0, rows), span(1)] * eighth
                values = held[pl.ds(0, rows), span(2)]
                key_parts, value_parts = [], []
                for head in range(2):
                    scores = jnp.where(same, mm(only(keys, head), queries, NT), masked_score)
                    probability = jnp.exp(scores - line_of(2 * pair + head))
                    value_parts.append(mm(probability.astype(BF16), grads))
                    prob_grad = mm(only(values, head), grads, NT)
                    score_low = (probability * (prob_grad - line_of(16 + 2 * pair + head))).astype(BF16)
                    key_parts.append(mm(score_low, queries) * HD**-0.5)
                key = jnp.where(lanes_of(0), key_parts[0], key_parts[1])
                value = jnp.where(lanes_of(0), value_parts[0], value_parts[1])
                if half == 0:
                    hat[:, span(0)] = key
                    total[:, span(0)] = value
                else:
                    outs["key"][...] = (hat[:, span(0)] + key).astype(BF16)
                    outs["value"][...] = (total[:, span(0)] + value).astype(BF16)

        @at_step(step, steps - 1)
        def _():
            for m in range(2):
                line.finish(m)

        extra.closing(here, step, steps, ins, outs, own)

    return run(body, steps, ins, outs, scratch, collective, "encoder_middle" if encoder else "decoder_middle", 80)


def projection_back(coded, layer, slots, ins, extra, collective):
    rows, width = ins["query"].array.shape
    fine = width // slots // PARTS
    units = 3
    steps = 2 + units
    ins["stream"].spec = pl.BlockSpec((1, rows, width), lambda i: (0, 0, 0))
    outs = {"small": Item(shaped((8, width), F32)), "sums": Item(shaped((4, PARTS, units, fine, width)))}
    if coded:
        outs["unit_grad"] = Item(shaped((rows, CODE), F32))
        outs["decode_grad"] = Item(shaped((CODE, width), F32))
        ins["pieces"].spec = pl.BlockSpec((1, rows, CODE), lambda i: (0, 0, 0))
    else:
        outs["grad"] = Item(shaped((rows, width), F32))
    scratch = {"cores": Cores.scratch(units, (fine, width))}
    extra.declare(ins, outs, scratch)

    def body(here, step, ins, outs, own):
        table = ins["table"]
        cores = Cores(here, outs["sums"], own["cores"], 0)
        extra.events(here, step, steps, ins, outs, own)
        sources = (ins["query"], ins["key"], ins["value"])
        for n in range(units):

            @at_step(step, n)
            def _():
                cores.put(jnp.int32(n), mm(ins["normed"][...], sources[n][...], TN))

        for n in range(units):

            @at_step(step, n + 1)
            def _():
                cores.collect(jnp.int32(n))

        @at_step(step, units)
        def _():
            cores.finish(units)

        @at_step(step, units + 1)
        def _():
            query, key, value = sources
            weight = ins["weight"]
            grad = mm(query[...], weight[:, :width], NT)
            grad += mm(key[...], weight[:, width : 2 * width], NT)
            grad += mm(value[...], weight[:, 2 * width :], NT)
            hat, scale = norm_parts(ins["stream"][0].astype(F32))
            start = ins["middle"][...] + norm_back(grad, table[2 * layer : 2 * layer + 1, :], hat, scale)
            small = [columns(grad * hat), columns(grad), columns(query[...].astype(F32)), columns(value[...].astype(F32))]
            if coded:
                start_low = start.astype(BF16)
                outs["unit_grad"][...] = mm(start_low, table[43:61, :].astype(BF16), NT)
                outs["decode_grad"][...] = mm(ins["pieces"][0], start_low, TN)
                small.append(columns(start_low.astype(F32)))
            else:
                outs["grad"][...] = start
            small += [jnp.zeros_like(small[0])] * (8 - len(small))
            outs["small"][...] = jnp.concatenate(small)

        extra.closing(here, step, steps, ins, outs, own)

    return run(body, steps, ins, outs, scratch, collective, "projection_back", 12)


def last_kernel(here, step, ins, outs, own):
    stacks = [Stack(here, ins[f"total{n}"], own[f"stack{n}"]) for n in range(3)]
    rows = Sum(here, [ins["small"]], own["sum"])
    rows.begin()
    for stack in stacks:
        stack.start()
    for stage in range(3):
        rows.meet(stage)
    for n, stack in enumerate(stacks):
        stack.finish(outs["units"].at[pl.ds(n, 1)])
    rows.finish(outs["rows"])


def assemble_kernel(project0, project1, five, six, two, three, four, project, output, expand, shrink):
    encoder = [(five, n) for n in range(five.shape[0])] + [(six, n) for n in range(six.shape[0])]
    decoder = [(part, n) for part in (two, three, four) for n in range(part.shape[0])]
    fine, width = project0.shape[1:]
    for layer, units, triple in ((0, encoder, project0), (1, decoder, project1)):
        for n in range(3):
            project[layer, :, n * width : (n + 1) * width] = triple[n]
        for n in range(4):
            ref, at = units[n]
            shrink[layer, n * fine : (n + 1) * fine, :] = ref[at]
            ref, at = units[4 + n]
            expand[layer, :, n * width : (n + 1) * width] = ref[at]
        ref, at = units[8]
        output[layer] = ref[at]


class Nothing:
    def declare(self, ins, outs, scratch):
        pass

    def events(self, here, step, steps, ins, outs, own):
        pass

    def closing(self, here, step, steps, ins, outs, own):
        pass


class Beside(Nothing):
    def __init__(
        self, slots, gathers=None, gather_steps=(), squares=None, stacks=None, sums=None, lines=None, line_steps=(), spreads=None, spread_steps=(), hop=None
    ):
        self.hop = hop
        self.lines, self.line_steps, self.spreads, self.spread_steps = lines or {}, line_steps, spreads or {}, spread_steps
        self.slots, self.gathers, self.gather_steps = slots, gathers or {}, gather_steps
        self.squares, self.stacks, self.sums = squares or {}, stacks or {}, sums or {}

    def declare(self, ins, outs, scratch):
        if self.hop:
            array = self.hop[1]
            ins["hop"] = anywhere(array)
            outs["hopped"] = anywhere(shaped(array.shape))
            scratch["hop"] = Hop.scratch()
        for name, (array, layer) in self.gathers.items():
            block = (1,) + array.shape[1:]
            ins["shard_" + name] = Item(array, pl.BlockSpec(block, lambda i, layer=layer: (layer, 0, 0)))
            outs["gathered_" + name] = anywhere(shaped((self.slots, PARTS) + array.shape[1:]))
        if self.gathers:
            scratch["gather"] = Gather.scratch(len(self.gathers))
        for name, (item, absolute) in self.lines.items():
            ins["line_" + name] = item
            outs["lined_" + name] = anywhere(shaped((PARTS,) + item.spec.block_shape[1:]))
        if self.lines:
            scratch["lines"] = Line.scratch(len(self.lines)) + [DMA((len(self.lines),))]
        for name, array in self.spreads.items():
            ins["spread_" + name] = Item(array)
            outs["gathered_" + name] = anywhere(shaped((self.slots,) + array.shape))
        if self.spreads:
            scratch["spreads"] = Spread.scratch(len(self.spreads))
        for name, (sums, first, units, steps) in self.squares.items():
            loaded = sums is not None
            if loaded:
                tail = sums.shape[3:]
            else:
                tail = (scratch["sums"] if "sums" in scratch else outs["sums"].array).shape[3:]
            if loaded:
                ins["square_" + name] = anywhere(sums)
            outs["total_" + name] = Item(shaped((PARTS, units) + tail))
            scratch["square_" + name] = Square.scratch(units, tail, loaded)
        for name, (array, steps) in self.stacks.items():
            if isinstance(array, str):
                shape = outs["total_" + array].array.shape
            else:
                ins["stack_" + name] = Item(array)
                shape = array.shape
            outs["stacked_" + name] = Item(shaped(shape[1:], F32))
            scratch["stack_" + name] = Stack.scratch(shape[1], shape[2:])
        for name, (arrays, steps) in self.sums.items():
            for i, array in enumerate(arrays):
                if isinstance(array, str):
                    arrays = arrays[:i] + [outs[array].array] + arrays[i + 1 :]
                else:
                    ins[f"sum_{name}{i}"] = Item(array)
            width = min(a.shape[1] for a in arrays)
            rows = -(-sum(a.shape[0] * (a.shape[1] // width) for a in arrays) // 16) * 16
            outs["summed_" + name] = Item(shaped((rows, width), F32))
            scratch["sum_" + name] = Sum.scratch(rows, width)

    def listed(self, here, ins, outs, own):
        if self.hop:
            hop_task = Hop(here, self.hop[0], ins["hop"], outs["hopped"], own["hop"])
            yield self.hop[2], hop_task.start
            yield None, hop_task.finish
        if self.gathers:
            names = list(self.gathers)
            gather = Gather(here, [ins["shard_" + n].at[0] for n in names], [outs["gathered_" + n] for n in names], own["gather"])

            def each(*actions):
                def go():
                    for action, *more in actions:
                        for m in range(len(names)):
                            action(m, *more)

                return go

            start, one, two, three, turn, corner = self.gather_steps
            yield start, each((gather.start,))
            yield one, each((gather.hop, 1), (gather.turn, 0))
            yield two, each((gather.hop, 2), (gather.turn, 1))
            yield three, each((gather.hop, 3), (gather.turn, 2))
            yield turn, each((gather.turn, 3), (gather.siblings,))
            yield corner, each((gather.corner,))
            yield None, each((gather.finish,))
        if self.lines:
            line_names = list(self.lines)
            sources = [ins["line_" + n].at[0] for n in line_names]
            arrays = [outs["lined_" + n] for n in line_names]
            sems = own["lines"]
            line = Line(here, arrays, sems[:3], sources, [absolute for item, absolute in self.lines.values()])
            keeps = [
                pltpu.make_async_copy(sources[m], line.at(m, here.z, here.z), sems[3].at[m]) for m in range(len(line_names))
            ]

            def begin():
                for m in range(len(line_names)):
                    line.start(m)
                    keeps[m].start()

            def end():
                for m in range(len(line_names)):
                    line.finish(m)
                    keeps[m].wait()

            def hop(k):
                for m in range(len(line_names)):
                    line.hop(m, k)

            yield self.line_steps[0], begin
            for k in range(1, PARTS):
                yield self.line_steps[k], functools.partial(hop, k)
            yield None, end
        if self.spreads:
            spread_names = list(self.spreads)
            spread = Spread(here, [ins["spread_" + n] for n in spread_names], [outs["gathered_" + n] for n in spread_names], own["spreads"])
            for action, n in zip((spread.start, spread.turn, spread.corner, spread.finish), self.spread_steps):

                def go(action=action):
                    for m in range(len(spread_names)):
                        action(m)

                yield n, go
        for name, (sums, first, units, steps) in self.squares.items():
            scratch = own["square_" + name]
            span = pl.ds(first, units)
            if sums is None:
                held = own["sums"] if "sums" in own else outs["sums"]
                square = Square(here, held.at[:, :, span], scratch)
            else:
                square = Square(here, scratch[0], scratch[1:], ins["square_" + name].at[:, :, span])
                yield steps[0], square.load
            yield steps[1], square.start
            yield steps[2], square.sides
            yield steps[3], functools.partial(square.total, outs["total_" + name])
        for name, (array, steps) in self.stacks.items():
            held = outs["total_" + array] if isinstance(array, str) else ins["stack_" + name]
            stack = Stack(here, held, own["stack_" + name])
            yield steps[0], stack.start
            yield steps[1], functools.partial(stack.finish, outs["stacked_" + name])
        for name, (arrays, steps) in self.sums.items():
            sources = [outs[a] if isinstance(a, str) else ins[f"sum_{name}{i}"] for i, a in enumerate(arrays)]
            rows = Sum(here, sources, own["sum_" + name])
            yield steps[0], rows.begin
            for stage in range(3):
                yield steps[1 + stage], functools.partial(rows.meet, stage)
            yield steps[4], functools.partial(rows.finish, outs["summed_" + name])

    def grouped(self, here, ins, outs, own):
        groups = {}
        for n, action in self.listed(here, ins, outs, own):
            groups.setdefault(n, []).append(action)
        return groups

    def play(self, step, n, actions):
        def go():
            for action in actions:
                action()

        at_step(step, n)(go)

    def events(self, here, step, steps, ins, outs, own):
        for n, actions in sorted((n, a) for n, a in self.grouped(here, ins, outs, own).items() if n is not None):
            self.play(step, n, actions)

    def closing(self, here, step, steps, ins, outs, own):
        actions = self.grouped(here, ins, outs, own).get(None)
        if actions:
            self.play(step, steps - 1, actions)


FORWARD1_GATHER = (0, 3, 6, 9, None, None)
MIDDLE1_GATHER = (0, 5, 15, 21, 27, 31)
FORWARD0_SQUARE = (0, 1, 4, None)


def on_device(
    patches,
    segments,
    code_bits,
    norm_gain,
    norm_shift,
    project_weight,
    query_value_bias,
    output_weight,
    output_bias,
    expand_weight,
    expand_bias,
    shrink_weight,
    shrink_bias,
    encode_weight,
    decode_weight,
    decode_bias,
    cotangent,
):
    slots, parts = lax.axis_size("slot"), lax.axis_size("seq")
    fine, width = project_weight.shape[1], patches.shape[-1]
    if slots != 8 or parts != PARTS or fine % 8:
        return plain_device(
            patches,
            segments,
            code_bits,
            norm_gain,
            norm_shift,
            project_weight,
            query_value_bias,
            output_weight,
            output_bias,
            expand_weight,
            expand_bias,
            shrink_weight,
            shrink_bias,
            encode_weight,
            decode_weight,
            decode_bias,
            cotangent,
        )
    slot, z = lax.axis_index("slot"), lax.axis_index("seq")
    devices, rows, hidden = slots * parts, patches.shape[1], expand_weight.shape[-1]
    signs = ((2 * code_bits - 1).astype(F32) * CODE ** (-0.5)).astype(BF16)

    ins = {
        "gain": Item(norm_gain),
        "shift": Item(norm_shift),
        "query_value": Item(query_value_bias),
        "output_bias": Item(output_bias),
        "shrink_bias": Item(shrink_bias),
        "decode_bias": Item(decode_bias.reshape(1, fine)),
        "expand_bias": Item(expand_bias),
        "encode": Item(encode_weight),
        "decode": Item(decode_weight),
    }
    weights = {"project": project_weight, "output": output_weight, "expand": expand_weight, "shrink": shrink_weight}

    def shard(name, layer):
        array = weights[name]
        return Item(array, pl.BlockSpec((1,) + array.shape[1:], lambda i: (layer, 0, 0)))

    ins["signs"], ins["patches"], ins["project"] = Item(signs), Item(patches), shard("project", 1)
    outs = {
        "table": anywhere(shaped((slots, parts, 64, fine), F32)),
        "project": anywhere(shaped((slots, parts) + project_weight.shape[1:])),
        "signs": anywhere(shaped((parts, rows, CODE))),
        "patches": anywhere(shaped((parts, rows, width))),
    }
    names = ("output", "expand", "shrink")
    scratch = {
        "table": pltpu.VMEM((64, fine), F32),
        "gather": Gather.scratch(2),
        "line": Line.scratch(1),
        "keep": DMA((1,)),
        "patches": Hop.scratch(),
    }
    first = run(first_kernel, 1, ins, outs, scratch, 0, "first_gather", 30)

    small = first["table"].reshape(devices, 64, fine)
    table = small.transpose(1, 0, 2).reshape(64, width)
    expand_shifts = small[:, 17:25].reshape(devices, 2, 4, fine).transpose(1, 0, 2, 3).reshape(2, 1, hidden)
    around = jnp.arange(parts) ^ z
    pieces = segments[0].reshape(parts, rows)[around]
    segment_row = pieces.reshape(1, parts * rows)
    segment_column = pieces[0].reshape(rows, 1)

    def flat(array):
        return array.reshape(-1, array.shape[-1])

    def piece(array, n):
        return Item(array, pl.BlockSpec((1, rows, width), lambda i: (n, 0, 0)))

    def forward(layer, pieces, weight, extra, collective):
        ins = {
            **pieces,
            "table": Item(table),
            "weight": Item(weight),
            "segment_row": Item(segment_row),
            "segment_column": Item(segment_column),
        }
        return forward_attention(layer == 1, layer, slots, ins, extra, collective)

    def middle(layer, stream, other, ahead, weights, extra, collective):
        ins = {
            "stream": Item(stream),
            "mixed": Item(ahead["mixed"]),
            "other": Item(other),
            "logs": Item(ahead["logs"]),
            "qkv": anywhere(ahead["qkv"]),
            "table": Item(table),
            "output": Item(weights["output"]),
            "expand": Item(weights["expand"]),
            "expand_shift": Item(expand_shifts[layer]),
            "shrink": Item(weights["shrink"]),
            "segment_row": Item(segment_row),
            "segment_column": Item(segment_column),
        }
        return middle_block(layer == 0, layer, slots, ins, extra, collective)

    def projection(layer, stream, ahead, between, weight, extra, collective, **more):
        ins = {
            "query": Item(between["query"]),
            "key": Item(between["key"]),
            "value": Item(between["value"]),
            "normed": Item(ahead["normed"]),
            "stream": Item(stream),
            "middle": Item(between["middle"]),
            "table": Item(table),
            "weight": Item(weight),
        }
        ins.update({k: Item(v) for k, v in more.items()})
        return projection_back(layer == 1, layer, slots, ins, extra, collective)

    decoder = {"project": flat(first["project"])}
    beside = Beside(slots, {n: (weights[n], 1) for n in names}, FORWARD1_GATHER, hop=(2, first["patches"], 1))
    ahead1 = forward(1, {"pieces": Item(first["signs"])}, decoder["project"], beside, 1)
    decoder.update({n: flat(ahead1["gathered_" + n]) for n in names})

    beside = Beside(slots, {n: (weights[n], 0) for n in weights}, MIDDLE1_GATHER)
    stream1 = ahead1["stream"][None]
    between1 = middle(1, stream1, cotangent[0], ahead1, decoder, beside, 2)
    encoder = {n: flat(between1["gathered_" + n]) for n in weights}
    beside = Beside(slots, squares={"two": (between1["sums"], 0, 3, (0, 1, 3, None))}, hop=(3, ahead1["hopped"], 0))
    after1 = projection(1, stream1, ahead1, between1, decoder["project"], beside, 3, pieces=first["signs"])

    beside = Beside(
        slots,
        squares={"three": (between1["sums"], 3, 5, FORWARD0_SQUARE)},
        stacks={"two": (after1["total_two"], (0, 6))},
        sums={"one": ([after1["small"], between1["small"], between1["wide"], after1["decode_grad"]], (0, 1, 3, 6, None))},
    )
    pieces = [piece(patches, 0), piece(first["patches"], 1), piece(ahead1["hopped"], 2)]
    pieces += [piece(first["patches"], 3), piece(after1["hopped"], 3)]
    ahead0 = forward(0, {f"piece{n}": item for n, item in enumerate(pieces)}, encoder["project"], beside, 4)
    beside = Beside(
        slots,
        squares={
            "one": (after1["sums"], 0, 3, (0, 1, 4, 9)),
            "four": (between1["sums"], 8, 1, (0, 1, 4, 9)),
            "five": (None, 0, 4, (None, 18, 22, 28)),
            "six": (None, 4, 5, (None, 22, 30, None)),
        },
        stacks={
            "three": (ahead0["total_three"], (0, 9)),
            "one": ("one", (10, 18)),
            "five": ("five", (33, None)),
        },
        sums={"two": (["small", "wide", "code_grad"], (13, 15, 17, 20, 28))},
    )
    between0 = middle(0, patches, after1["unit_grad"], ahead0, encoder, beside, 5)
    beside = Beside(
        slots,
        squares={f"seven{n}": (None, n, 1, (None, n + 2, 4, None)) for n in range(3)},
        stacks={n: (between0["total_" + n], (0, None)) for n in ("six", "four")},
    )
    after0 = projection(0, patches, ahead0, between0, encoder["project"], beside, 6)

    ins = {f"total{n}": Item(after0[f"total_seven{n}"]) for n in range(3)}
    ins["small"] = Item(after0["small"])
    outs = {"units": Item(shaped((3, fine, width), F32)), "rows": Item(shaped((16, width), F32))}
    scratch = {f"stack{n}": Stack.scratch(1, (fine, width)) for n in range(3)}
    scratch["sum"] = Sum.scratch(16, width)
    last = run(last_kernel, 1, ins, outs, scratch, 7, "last_sums", 20)

    units = [last["units"], between0["stacked_one"], between0["stacked_five"], after0["stacked_six"]]
    units += [ahead0["stacked_two"], between0["stacked_three"], after0["stacked_four"]]
    project_grad, output_grad, expand_grad, shrink_grad = pl.pallas_call(
        assemble_kernel,
        out_shape=tuple(shaped(weights[n].shape, F32) for n in ("project", "output", "expand", "shrink")),
        compiler_params=pltpu.CompilerParams(vmem_limit_bytes=BIG),
        name="assemble",
    )(*units)

    device = slot * parts + z
    one, two = ahead0["summed_one"], between0["summed_two"]
    summed = jnp.concatenate([last["rows"][:8], one, two])
    mine = lax.dynamic_slice(summed, (0, device * fine), (summed.shape[0], fine))
    in0, in1, mid1 = mine[0:4], mine[8:13], mine[16:20]
    at = 8 + one.shape[0]
    mid0, decode_grad, code_grad = mine[at : at + 4], mine[28:46], mine[at + 12 : at + 30]
    wide = jnp.stack([two[8:12].reshape(hidden), one[16:20].reshape(hidden)])
    wide = lax.dynamic_slice(wide, (0, device * (hidden // devices)), (2, hidden // devices))
    return (
        between1["decoded"][None],
        after0["grad"][None],
        jnp.stack([jnp.stack([in0[0], mid0[0]]), jnp.stack([in1[0], mid1[0]])]),
        jnp.stack([jnp.stack([in0[1], mid0[1]]), jnp.stack([in1[1], mid1[1]])]),
        project_grad,
        jnp.stack([in0[2:4], in1[2:4]]),
        output_grad,
        jnp.stack([mid0[2], mid1[2]]),
        expand_grad,
        wide,
        shrink_grad,
        jnp.stack([mid0[3], mid1[3]]),
        code_grad.T,
        decode_grad,
        in1[4],
    )


def plain_norm(stream, gains, shifts):
    centre = stream - jnp.mean(stream, axis=-1, keepdims=True)
    spread = jnp.mean(centre * centre, axis=-1, keepdims=True)
    return centre * lax.rsqrt(spread + epsilon) * gains + shifts


def normalize(coded):
    return coded / jnp.sqrt(jnp.sum(coded * coded, axis=-1, keepdims=True) + epsilon)


def gelu_exact(hidden):
    return jax.nn.gelu(hidden, approximate=False)


def gather_weights(shards):
    return (
        lax.all_gather(shards[0], ("slot", "seq"), axis=2, tiled=True),
        lax.all_gather(shards[1], ("slot", "seq"), axis=2, tiled=True),
        lax.all_gather(shards[2], ("slot", "seq"), axis=1, tiled=True),
        lax.all_gather(shards[3], ("slot", "seq"), axis=2, tiled=True),
        lax.all_gather(shards[4], ("slot", "seq"), axis=1, tiled=True),
        lax.all_gather(shards[5], ("slot", "seq"), axis=1, tiled=True),
        lax.all_gather(shards[6], ("slot", "seq"), axis=1, tiled=True),
        lax.all_gather(shards[7], ("slot", "seq"), axis=1, tiled=True),
        lax.all_gather(shards[8], ("slot", "seq"), axis=1, tiled=True),
        lax.all_gather(shards[9], ("slot", "seq"), axis=1, tiled=True),
        lax.all_gather(shards[10], ("slot", "seq"), axis=0, tiled=True),
        lax.all_gather(shards[11], ("slot", "seq"), axis=1, tiled=True),
        lax.all_gather(shards[12], ("slot", "seq"), axis=0, tiled=True),
    )


def segment_mask(segments, offset, block_rows):
    return segments[:, None, offset : offset + block_rows, None] == segments[:, None, None, :]


def scaled_scores(queries, key_rows, same_item):
    scores = jnp.einsum("sqhd,skhd->shqk", queries, key_rows, preferred_element_type=jnp.float32)
    return jnp.where(same_item, scores * HD ** (-0.5), masked_score)


def forward_block(stream, layer, segments):
    (
        gains,
        shifts,
        project,
        query_value,
        output,
        output_shift,
        expand,
        expand_shift,
        shrink,
        shrink_shift,
    ) = layer
    slot_count, row_count, model_width = stream.shape
    seq_parts = lax.axis_size("seq")
    head_width = model_width // seq_parts
    normed = plain_norm(stream, gains[0].astype(jnp.float32), shifts[0].astype(jnp.float32)).astype(
        jnp.bfloat16
    )
    bias_row = jnp.concatenate(
        [query_value[0], jnp.zeros_like(query_value[0]), query_value[1]]
    ).astype(jnp.float32)
    projected = (jnp.dot(normed, project, preferred_element_type=jnp.float32) + bias_row).astype(
        jnp.bfloat16
    )
    split_heads = lax.all_to_all(
        projected.reshape(slot_count, row_count, 3, seq_parts, head_width),
        "seq",
        split_axis=3,
        concat_axis=1,
        tiled=True,
    )
    length = split_heads.shape[1]
    local_heads = head_width // HD
    queries = split_heads[:, :, 0, 0].reshape(slot_count, length, local_heads, HD)
    key_rows = split_heads[:, :, 1, 0].reshape(slot_count, length, local_heads, HD)
    values = split_heads[:, :, 2, 0].reshape(slot_count, length, local_heads, HD)
    block_rows = min(512, length)
    pieces = []
    log_parts = []
    for offset in range(0, length, block_rows):
        scores = scaled_scores(
            queries[:, offset : offset + block_rows],
            key_rows,
            segment_mask(segments, offset, block_rows),
        )
        row_top = jnp.max(scores, axis=-1, keepdims=True)
        raised = jnp.exp(scores - row_top)
        row_total = jnp.sum(raised, axis=-1, keepdims=True)
        probability = (raised / row_total).astype(jnp.bfloat16)
        pieces.append(
            jnp.einsum(
                "shqk,skhd->sqhd", probability, values, preferred_element_type=jnp.float32
            ).astype(jnp.bfloat16)
        )
        log_parts.append(row_top + jnp.log(row_total))
    log_sums = jnp.concatenate(log_parts, axis=2)
    attended = jnp.concatenate(pieces, axis=1).reshape(slot_count, length, 1, head_width)
    mixed_rows = lax.all_to_all(attended, "seq", split_axis=1, concat_axis=2, tiled=True).reshape(
        slot_count, row_count, model_width
    )
    middle = (
        stream
        + jnp.dot(mixed_rows, output, preferred_element_type=jnp.float32)
        + output_shift.astype(jnp.float32)
    )
    normed_mid = plain_norm(
        middle, gains[1].astype(jnp.float32), shifts[1].astype(jnp.float32)
    ).astype(jnp.bfloat16)
    hidden = jnp.dot(normed_mid, expand, preferred_element_type=jnp.float32) + expand_shift.astype(
        jnp.float32
    )
    active = gelu_exact(hidden).astype(jnp.bfloat16)
    result = (
        middle
        + jnp.dot(active, shrink, preferred_element_type=jnp.float32)
        + shrink_shift.astype(jnp.float32)
    )
    saved_values = (
        normed,
        queries,
        key_rows,
        values,
        log_sums,
        mixed_rows,
        middle,
        normed_mid,
        hidden,
        active,
    )
    return (result, saved_values)


def backward_block(grad_out, stream, saved_values, layer, segments):
    (
        gains,
        shifts,
        project,
        query_value,
        output,
        output_shift,
        expand,
        expand_shift,
        shrink,
        shrink_shift,
    ) = layer
    normed, queries, key_rows, values, log_sums, mixed_rows, middle, normed_mid, hidden, active = (
        saved_values
    )
    slot_count, row_count, model_width = stream.shape
    seq_parts = lax.axis_size("seq")
    head_width = model_width // seq_parts
    branch = grad_out.astype(jnp.bfloat16)
    shrink_shift_grad = jnp.sum(branch, axis=(0, 1), dtype=jnp.float32)
    shrink_grad = jnp.einsum("stf,sto->fo", active, branch, preferred_element_type=jnp.float32)
    active_grad = jnp.einsum("sto,fo->stf", branch, shrink, preferred_element_type=jnp.float32)
    unused, gelu_back = jax.vjp(gelu_exact, hidden)
    hidden_low = gelu_back(active_grad)[0].astype(jnp.bfloat16)
    expand_shift_grad = jnp.sum(hidden_low, axis=(0, 1), dtype=jnp.float32)
    expand_grad = jnp.einsum(
        "sti,stf->if", normed_mid, hidden_low, preferred_element_type=jnp.float32
    )
    normed_mid_grad = jnp.einsum(
        "stf,if->sti", hidden_low, expand, preferred_element_type=jnp.float32
    )
    unused, norm_back = jax.vjp(
        plain_norm, middle, gains[1].astype(jnp.float32), shifts[1].astype(jnp.float32)
    )
    middle_part, gain_mid_grad, shift_mid_grad = norm_back(normed_mid_grad)
    middle_grad = grad_out + middle_part
    branch_low = middle_grad.astype(jnp.bfloat16)
    output_shift_grad = jnp.sum(branch_low, axis=(0, 1), dtype=jnp.float32)
    output_grad = jnp.einsum(
        "sti,sto->io", mixed_rows, branch_low, preferred_element_type=jnp.float32
    )
    mixed_low = jnp.einsum(
        "sto,io->sti", branch_low, output, preferred_element_type=jnp.float32
    ).astype(jnp.bfloat16)
    head_grad = lax.all_to_all(
        mixed_low.reshape(slot_count, row_count, seq_parts, head_width),
        "seq",
        split_axis=2,
        concat_axis=1,
        tiled=True,
    )
    length = head_grad.shape[1]
    local_heads = head_width // HD
    head_grad = head_grad.reshape(slot_count, length, local_heads, HD)
    scale_factor = HD ** (-0.5)
    block_rows = min(512, length)
    key_grad = jnp.zeros((slot_count, length, local_heads, HD), jnp.float32)
    value_grad = jnp.zeros((slot_count, length, local_heads, HD), jnp.float32)
    query_parts = []
    for offset in range(0, length, block_rows):
        query_block = queries[:, offset : offset + block_rows]
        scores = scaled_scores(query_block, key_rows, segment_mask(segments, offset, block_rows))
        probability = jnp.exp(scores - log_sums[:, :, offset : offset + block_rows])
        out_grad = head_grad[:, offset : offset + block_rows]
        value_grad = value_grad + jnp.einsum(
            "shqk,sqhd->skhd",
            probability.astype(jnp.bfloat16),
            out_grad,
            preferred_element_type=jnp.float32,
        )
        prob_grad = jnp.einsum(
            "sqhd,skhd->shqk", out_grad, values, preferred_element_type=jnp.float32
        )
        centre = jnp.sum(probability * prob_grad, axis=-1, keepdims=True)
        score_low = (probability * (prob_grad - centre)).astype(jnp.bfloat16)
        query_parts.append(
            jnp.einsum("shqk,skhd->sqhd", score_low, key_rows, preferred_element_type=jnp.float32)
            * scale_factor
        )
        key_grad = (
            key_grad
            + jnp.einsum(
                "shqk,sqhd->skhd", score_low, query_block, preferred_element_type=jnp.float32
            )
            * scale_factor
        )
    query_grad = jnp.concatenate(query_parts, axis=1)
    joined = (
        jnp.stack([query_grad, key_grad, value_grad], axis=2)
        .astype(jnp.bfloat16)
        .reshape(slot_count, length, 3, 1, head_width)
    )
    project_low = lax.all_to_all(joined, "seq", split_axis=1, concat_axis=3, tiled=True).reshape(
        slot_count, row_count, 3 * model_width
    )
    project_shift = jnp.sum(project_low, axis=(0, 1), dtype=jnp.float32)
    query_value_grad = jnp.stack([project_shift[:model_width], project_shift[2 * model_width :]])
    project_grad = jnp.einsum(
        "sti,stj->ij", normed, project_low, preferred_element_type=jnp.float32
    )
    normed_grad = jnp.einsum(
        "stj,ij->sti", project_low, project, preferred_element_type=jnp.float32
    )
    unused, norm_back = jax.vjp(
        plain_norm, stream, gains[0].astype(jnp.float32), shifts[0].astype(jnp.float32)
    )
    stream_part, gain_in_grad, shift_in_grad = norm_back(normed_grad)
    input_part = middle_grad + stream_part
    grads = (
        jnp.stack([gain_in_grad, gain_mid_grad]),
        jnp.stack([shift_in_grad, shift_mid_grad]),
        project_grad,
        query_value_grad,
        output_grad,
        output_shift_grad,
        expand_grad,
        expand_shift_grad,
        shrink_grad,
        shrink_shift_grad,
    )
    return (input_part, grads)


def plain_device(
    patches,
    segments,
    code_bits,
    norm_gain,
    norm_shift,
    project_weight,
    query_value_bias,
    output_weight,
    output_bias,
    expand_weight,
    expand_bias,
    shrink_weight,
    shrink_bias,
    encode_weight,
    decode_weight,
    decode_bias,
    cotangent,
):
    shards = (
        norm_gain,
        norm_shift,
        project_weight,
        query_value_bias,
        output_weight,
        output_bias,
        expand_weight,
        expand_bias,
        shrink_weight,
        shrink_bias,
        encode_weight,
        decode_weight,
        decode_bias,
    )
    gathered = gather_weights(shards)
    stream_in = patches.astype(jnp.float32)
    encoded, unused = forward_block(
        stream_in, tuple((array[0] for array in gathered[:10])), segments
    )
    encoded_low = encoded.astype(jnp.bfloat16)
    coded = jnp.einsum("sti,ic->stc", encoded_low, gathered[10], preferred_element_type=jnp.float32)
    signs = ((2 * code_bits - 1).astype(jnp.float32) * CODE ** (-0.5)).astype(jnp.bfloat16)
    start = jnp.einsum(
        "stc,ci->sti", signs, gathered[11], preferred_element_type=jnp.float32
    ) + gathered[12].astype(jnp.float32)
    decoded, decoder_saved = forward_block(
        start, tuple((array[1] for array in gathered[:10])), segments
    )
    weights_back = gather_weights(shards)
    encoder = tuple((array[0] for array in weights_back[:10]))
    decoder = tuple((array[1] for array in weights_back[:10]))
    start_grad, decoder_grads = backward_block(
        cotangent.astype(jnp.float32), start, decoder_saved, decoder, segments
    )
    start_low = start_grad.astype(jnp.bfloat16)
    decode_bias_grad = jnp.sum(start_low, axis=(0, 1), dtype=jnp.float32)
    decode_grad = jnp.einsum("stc,sti->ci", signs, start_low, preferred_element_type=jnp.float32)
    unit_grad = jnp.einsum(
        "sti,ci->stc", start_low, weights_back[11], preferred_element_type=jnp.float32
    )
    unit_rows, unit_back = jax.vjp(normalize, coded)
    coded_low = unit_back(unit_grad)[0].astype(jnp.bfloat16)
    encode_grad = jnp.einsum(
        "sti,stc->ic", encoded_low, coded_low, preferred_element_type=jnp.float32
    )
    encoded_grad = jnp.einsum(
        "stc,ic->sti", coded_low, weights_back[10], preferred_element_type=jnp.float32
    )
    unused, encoder_saved = forward_block(stream_in, encoder, segments)
    input_grad, encoder_grads = backward_block(
        encoded_grad, stream_in, encoder_saved, encoder, segments
    )
    pairs = tuple(
        (jnp.stack([first, second]) for first, second in zip(encoder_grads, decoder_grads))
    )
    totals = (
        lax.psum_scatter(pairs[0], ("slot", "seq"), scatter_dimension=2, tiled=True),
        lax.psum_scatter(pairs[1], ("slot", "seq"), scatter_dimension=2, tiled=True),
        lax.psum_scatter(pairs[2], ("slot", "seq"), scatter_dimension=1, tiled=True),
        lax.psum_scatter(pairs[3], ("slot", "seq"), scatter_dimension=2, tiled=True),
        lax.psum_scatter(pairs[4], ("slot", "seq"), scatter_dimension=1, tiled=True),
        lax.psum_scatter(pairs[5], ("slot", "seq"), scatter_dimension=1, tiled=True),
        lax.psum_scatter(pairs[6], ("slot", "seq"), scatter_dimension=1, tiled=True),
        lax.psum_scatter(pairs[7], ("slot", "seq"), scatter_dimension=1, tiled=True),
        lax.psum_scatter(pairs[8], ("slot", "seq"), scatter_dimension=1, tiled=True),
        lax.psum_scatter(pairs[9], ("slot", "seq"), scatter_dimension=1, tiled=True),
        lax.psum_scatter(encode_grad, ("slot", "seq"), scatter_dimension=0, tiled=True),
        lax.psum_scatter(decode_grad, ("slot", "seq"), scatter_dimension=1, tiled=True),
        lax.psum_scatter(decode_bias_grad, ("slot", "seq"), scatter_dimension=0, tiled=True),
    )
    return (decoded.astype(jnp.bfloat16), input_grad) + tuple(totals)


def solution(mesh):
    in_specs = (
        P("slot", "seq", None),
        P("slot", None),
        P("slot", "seq", None),
        P(None, None, ("slot", "seq")),
        P(None, None, ("slot", "seq")),
        P(None, ("slot", "seq"), None),
        P(None, None, ("slot", "seq")),
        P(None, ("slot", "seq"), None),
        P(None, ("slot", "seq")),
        P(None, ("slot", "seq"), None),
        P(None, ("slot", "seq")),
        P(None, ("slot", "seq"), None),
        P(None, ("slot", "seq")),
        P(("slot", "seq"), None),
        P(None, ("slot", "seq")),
        P(("slot", "seq")),
        P("slot", "seq", None),
    )
    out_specs = (
        P("slot", "seq", None),
        P("slot", "seq", None),
        P(None, None, ("slot", "seq")),
        P(None, None, ("slot", "seq")),
        P(None, ("slot", "seq"), None),
        P(None, None, ("slot", "seq")),
        P(None, ("slot", "seq"), None),
        P(None, ("slot", "seq")),
        P(None, ("slot", "seq"), None),
        P(None, ("slot", "seq")),
        P(None, ("slot", "seq"), None),
        P(None, ("slot", "seq")),
        P(("slot", "seq"), None),
        P(None, ("slot", "seq")),
        P(("slot", "seq")),
    )
    return jax.shard_map(
        on_device, mesh=mesh, in_specs=in_specs, out_specs=out_specs, check_vma=False
    )
```

```python
import functools

import jax
import jax.numpy as jnp
from jax import lax
from jax.experimental import pallas as pl
from jax.experimental.pallas import tpu as pltpu
from jax.sharding import PartitionSpec as P

HD = 64
CODE = 18
epsilon = 1e-06
masked_score = -1000000000.0
MESH = pl.DeviceIdType.MESH
F32 = jnp.float32
BF16 = jnp.bfloat16
AXES = ("slot", "seq")
BIG = 60 * 1024 * 1024

NN = (((1,), (0,)), ((), ()))
NT = (((1,), (1,)), ((), ()))
TN = (((0,), (0,)), ((), ()))


def mm(a, b, dims=NN):
    return lax.dot_general(a, b, dims, preferred_element_type=F32)


def params(**more):
    return pltpu.CompilerParams(vmem_limit_bytes=BIG, **more)


def whole(shape):
    return pl.BlockSpec(shape, lambda *i: (0,) * len(shape))


def shaped(shape, dtype=BF16):
    return jax.ShapeDtypeStruct(shape, dtype)


def norm_parts(stream):
    centre = stream - jnp.mean(stream, axis=-1, keepdims=True)
    spread = jnp.mean(centre * centre, axis=-1, keepdims=True)
    scale = lax.rsqrt(spread + epsilon)
    return centre * scale, scale


def norm_back(grad, gain, hat, scale):
    lifted = grad * gain
    mean = jnp.mean(lifted, axis=-1, keepdims=True)
    mixed = jnp.mean(lifted * hat, axis=-1, keepdims=True)
    return scale * (lifted - mean - hat * mixed)


def columns(value):
    return jnp.sum(value, axis=0, keepdims=True)


def lanes_of(head):
    lane = lax.broadcasted_iota(jnp.int32, (1, 2 * HD), 1)
    return lane < HD if head == 0 else lane >= HD


def only(value, head):
    return jnp.where(lanes_of(head), value, jnp.zeros_like(value))


def gelu_parts(hidden):
    normal = 0.5 + 0.5 * lax.erf(hidden * 0.7071067811865476)
    density = jnp.exp(-0.5 * hidden * hidden) * 0.3989422804014327
    return hidden * normal, normal + hidden * density


def flip(index, bit):
    size = 1 << bit
    return index + size - 2 * size * ((index // size) % 2)


def relative(a, b):
    return 2 * ((a // 2 + b // 2) % 2) + (a + b) % 2


PARTS = 4
DMA = pltpu.SemaphoreType.DMA


def remote(src, dst, send, recv, peer):
    return pltpu.make_async_remote_copy(
        src_ref=src, dst_ref=dst, send_sem=send, recv_sem=recv, device_id=peer, device_id_type=MESH
    )


class Here:
    def __init__(self):
        self.slot, self.z = lax.axis_index("slot"), lax.axis_index("seq")
        self.across = (flip(self.slot, 1), self.z)
        self.beside = (flip(self.slot, 2), self.z)
        self.sibling = (flip(self.slot, 0), self.z)
        self.core, self.square = lax.rem(self.slot, 2), self.slot // 2

    def along(self, k):
        return (self.slot, relative(self.z, k))

    def greet(self):
        barrier = pltpu.get_barrier_semaphore()
        peers = [self.across, self.beside, self.sibling] + [self.along(k) for k in range(1, PARTS)]
        for peer in peers:
            pl.semaphore_signal(barrier, inc=1, device_id=peer, device_id_type=MESH)
        pl.semaphore_wait(barrier, len(peers))


class Line:
    @staticmethod
    def scratch(count):
        return [DMA((count, PARTS))] * 3

    def __init__(self, here, arrays, sems, sources, absolute):
        self.here, self.arrays, self.sources, self.absolute = here, arrays, sources, absolute
        self.recv, self.up, self.down = sems

    def at(self, m, block, z):
        return self.arrays[m].at[block if self.absolute[m] else relative(block, z)]

    def copy(self, m, block, upward):
        z = self.here.z
        to = jnp.minimum(z + 1, PARTS - 1) if upward else jnp.maximum(z - 1, 0)
        send = (self.up if upward else self.down).at[m, block]
        src = self.sources[m] if self.sources is not None and block is z else self.at(m, block, z)
        return remote(src, self.at(m, block, to), send, self.recv.at[m, block], (self.here.slot, to))

    def onward(self, m, block, upward):
        z = self.here.z

        @pl.when((z < PARTS - 1) if upward else (z > 0))
        def _():
            self.copy(m, block, upward).start()

    def start(self, m):
        self.onward(m, self.here.z, True)
        self.onward(m, self.here.z, False)

    def hop(self, m, k):
        z = self.here.z

        @pl.when(z >= k)
        def _():
            self.copy(m, z - k, True).wait_recv()
            self.onward(m, z - k, True)

        @pl.when(z + k <= PARTS - 1)
        def _():
            self.copy(m, z + k, False).wait_recv()
            self.onward(m, z + k, False)

    def finish(self, m):
        z = self.here.z
        for block in range(PARTS):

            @pl.when((z < PARTS - 1) & (z >= block))
            def _():
                self.copy(m, block, True).wait_send()

            @pl.when((z > 0) & (z <= block))
            def _():
                self.copy(m, block, False).wait_send()


class Hop:
    @staticmethod
    def scratch():
        return [DMA((4,))]

    def __init__(self, here, k, source, out, sems):
        self.here, self.k, self.source, self.out, self.sems = here, k, source, out, sems[0]

    def copy(self, upward, block):
        z = self.here.z
        to = jnp.minimum(z + 1, PARTS - 1) if upward else jnp.maximum(z - 1, 0)
        src = self.source if self.k == 1 else self.source.at[relative(block, z)]
        n = 0 if upward else 2
        return remote(src, self.out.at[relative(block, to)], self.sems.at[n], self.sems.at[n + 1], (self.here.slot, to))

    def start(self, wait=False):
        z, back = self.here.z, self.k - 1
        for upward, meets in ((True, (z >= back) & (z < PARTS - 1)), (False, (z + back <= PARTS - 1) & (z > 0))):

            @pl.when(meets)
            def _():
                move = self.copy(upward, z - back if upward else z + back)
                move.wait_send() if wait else move.start()

    def finish(self):
        z, k = self.here.z, self.k
        for upward, meets in ((True, z >= k), (False, z + k <= PARTS - 1)):

            @pl.when(meets)
            def _():
                self.copy(upward, jnp.clip(z, 0, PARTS - 1)).wait_recv()

        self.start(True)


class Gather:
    @staticmethod
    def scratch(count):
        return [DMA((count, PARTS))] * 5 + [DMA((count,))] * 8

    def __init__(self, here, sources, outs, sems):
        self.here, self.sources, self.outs = here, sources, outs
        self.rz, self.up, self.down, self.rx, self.ry = sems[:5]
        self.local, self.sx, self.sy, self.rd, self.dx, self.dy, self.rc, self.sc = sems[5:]

    def place(self, m, block):
        return self.outs[m].at[self.here.slot, block]

    def copy(self, m, block, upward, src):
        z = self.here.z
        to = jnp.minimum(z + 1, PARTS - 1) if upward else jnp.maximum(z - 1, 0)
        send = (self.up if upward else self.down).at[m, block]
        return remote(src, self.place(m, block), send, self.rz.at[m, block], (self.here.slot, to))

    def onward(self, m, block, upward, src):
        z = self.here.z

        @pl.when((z < PARTS - 1) if upward else (z > 0))
        def _():
            self.copy(m, block, upward, src).start()

    def sideways(self, m, block, src):
        dst = self.place(m, block)
        remote(src, dst, self.sx.at[m], self.rx.at[m, block], self.here.across).start()
        remote(src, dst, self.sy.at[m], self.ry.at[m, block], self.here.beside).start()

    def keep(self, m):
        return pltpu.make_async_copy(self.sources[m], self.place(m, self.here.z), self.local.at[m])

    def start(self, m):
        src, z = self.sources[m], self.here.z
        self.onward(m, z, True, src)
        self.onward(m, z, False, src)
        self.sideways(m, z, src)
        self.keep(m).start()

    def arrived(self, m, block, upward):
        src = self.place(m, block)
        self.copy(m, block, upward, src).wait_recv()
        self.onward(m, block, upward, src)
        self.sideways(m, block, src)

    def hop(self, m, k):
        z = self.here.z

        @pl.when(z >= k)
        def _():
            self.arrived(m, z - k, True)

        @pl.when(z + k <= PARTS - 1)
        def _():
            self.arrived(m, z + k, False)

    def turned(self, m, block):
        across, beside = self.here.across, self.here.beside
        here = self.outs[m].at[across[0], block]
        remote(here, here, self.sx.at[m], self.rx.at[m, block], across).wait_recv()

        @pl.when(lax.rem(block, 2) == 0)
        def _():
            remote(here, here, self.dy.at[m], self.rd.at[m], beside).start()

        there = self.outs[m].at[beside[0], block]
        remote(there, there, self.sy.at[m], self.ry.at[m, block], beside).wait_recv()

        @pl.when(lax.rem(block, 2) == 1)
        def _():
            remote(there, there, self.dx.at[m], self.rd.at[m], across).start()

    def turn(self, m, k):
        z = self.here.z
        if k == 0:
            self.turned(m, z)
            return

        @pl.when(z >= k)
        def _():
            self.turned(m, z - k)

        @pl.when(z + k <= PARTS - 1)
        def _():
            self.turned(m, z + k)

    def share(self, m, slot):
        group = self.outs[m].at[slot]
        remote(group, group, self.sc.at[m], self.rc.at[m], self.here.sibling).start()

    def siblings(self, m):
        self.keep(m).wait()
        for slot in (self.here.slot, self.here.across[0], self.here.beside[0]):
            self.share(m, slot)

    def corner(self, m):
        slot = flip(self.here.across[0], 2)
        group = self.outs[m].at[slot]
        remote(group, group, self.dx.at[m], self.rd.at[m], self.here.across).wait_recv()
        self.share(m, slot)

    def finish(self, m):
        here, z, src = self.here, self.here.z, self.sources[m]
        for block in range(PARTS):

            @pl.when((z < PARTS - 1) & (z >= block))
            def _():
                self.copy(m, block, True, src).wait_send()

            @pl.when((z > 0) & (z <= block))
            def _():
                self.copy(m, block, False, src).wait_send()

        group = self.outs[m].at[here.slot]
        half = self.outs[m].at[here.slot, pl.ds(0, PARTS // 2)]
        remote(group, group, self.sx.at[m], self.rx.at[m, 0], here.across).wait_send()
        remote(group, group, self.sy.at[m], self.ry.at[m, 0], here.beside).wait_send()
        remote(half, half, self.dx.at[m], self.rd.at[m], here.across).wait_send()
        remote(half, half, self.dy.at[m], self.rd.at[m], here.beside).wait_send()
        four = self.outs[m].at[pl.ds(0, 4)]
        both = remote(four, four, self.sc.at[m], self.rc.at[m], here.sibling)
        both.wait_send()
        both.wait_recv()


class Spread:
    @staticmethod
    def scratch(count):
        return [DMA((11, count))]

    def __init__(self, here, sources, outs, sems):
        self.here, self.sources, self.outs, self.sems = here, sources, outs, sems[0]

    def sem(self, m, n):
        return self.sems.at[n, m]

    def keep(self, m):
        return pltpu.make_async_copy(self.sources[m], self.outs[m].at[self.here.slot], self.sem(m, 0))

    def share(self, m, src, slot):
        remote(src, self.outs[m].at[slot], self.sem(m, 1), self.sem(m, 2), self.here.sibling).start()

    def side(self, m, n, src, slot):
        peer = self.here.beside if n else self.here.across
        return remote(src, self.outs[m].at[slot], self.sem(m, 3 + 2 * n), self.sem(m, 4 + 2 * n), peer)

    def half(self, m, n, slot):
        ref = self.outs[m].at[slot, pl.ds(n * (PARTS // 2), PARTS // 2)]
        peer = self.here.across if n else self.here.beside
        return remote(ref, ref, self.sem(m, 7 + 2 * n), self.sem(m, 8 + 2 * n), peer)

    def start(self, m):
        src, slot = self.sources[m], self.here.slot
        for n in range(2):
            self.side(m, n, src, slot).start()
        self.keep(m).start()
        self.share(m, src, slot)

    def turn(self, m):
        for n, peer in enumerate((self.here.across, self.here.beside)):
            ref = self.outs[m].at[peer[0]]
            self.side(m, n, ref, peer[0]).wait_recv()
            self.half(m, n, peer[0]).start()
            self.share(m, ref, peer[0])

    def corner(self, m):
        slot = flip(self.here.across[0], 2)
        for n in range(2):
            self.half(m, n, slot).wait_recv()
        self.share(m, self.outs[m].at[slot], slot)

    def finish(self, m):
        self.keep(m).wait()
        for n in range(2):
            self.side(m, n, self.sources[m], self.here.slot).wait_send()
            self.half(m, n, self.here.slot).wait_send()
        four = self.outs[m].at[pl.ds(0, 4)]
        both = remote(four, four, self.sem(m, 1), self.sem(m, 2), self.here.sibling)
        both.wait_send()
        both.wait_recv()


def add_into(target, source):
    def one(a, carry):
        target[a] = (target[a].astype(F32) + source[a].astype(F32)).astype(target.dtype)
        return carry

    lax.fori_loop(0, target.shape[0], one, 0)


class Square:
    @staticmethod
    def scratch(units, tail, loaded):
        held = [pltpu.VMEM((4, PARTS, units) + tail, BF16)] if loaded else []
        half = pltpu.VMEM((PARTS // 2, units) + tail, BF16)
        full = pltpu.VMEM((PARTS, units) + tail, BF16)
        return held + [half, half, full, full, DMA((9,))]

    def __init__(self, here, held, scratch, source=None):
        self.here, self.held, self.source = here, held, source
        self.corner_x, self.corner_y, self.side_x, self.side_y, self.sems = scratch

    def load(self, start=True):
        copy = pltpu.make_async_copy(self.source, self.held, self.sems.at[8])
        copy.start() if start else copy.wait()

    def move(self, n):
        half, held, sems = PARTS // 2, self.held, self.sems
        src = (held.at[3, pl.ds(0, half)], held.at[3, pl.ds(half, half)], held.at[1], held.at[2])[n]
        dst = (self.corner_x, self.corner_y, self.side_x, self.side_y)[n]
        peer = self.here.beside if n % 2 else self.here.across
        return remote(src, dst, sems.at[2 * n], sems.at[2 * n + 1], peer)

    def start(self):
        if self.source is not None:
            self.load(False)
        for n in range(2):
            self.move(n).start()

    def sides(self):
        half = PARTS // 2
        self.move(0).wait_recv()
        add_into(self.held.at[2, pl.ds(0, half)], self.corner_x)
        self.move(3).start()
        self.move(1).wait_recv()
        add_into(self.held.at[1, pl.ds(half, half)], self.corner_y)
        self.move(2).start()

    def total(self, out):
        self.move(2).wait_recv()
        self.move(3).wait_recv()

        def one(a, carry):
            value = self.held[0, a].astype(F32) + self.side_x[a].astype(F32) + self.side_y[a].astype(F32)
            out[a] = value.astype(out.dtype)
            return carry

        lax.fori_loop(0, PARTS, one, 0)
        for n in range(4):
            self.move(n).wait_send()


class Stack:
    @staticmethod
    def scratch(units, tail):
        return [pltpu.VMEM((PARTS - 1, units) + tail, BF16), DMA((2, PARTS))]

    def __init__(self, here, held, scratch):
        self.here, self.held = here, held
        self.arrived, self.sems = scratch

    def moves(self):
        for k in range(1, PARTS):
            peer = self.here.along(k)
            yield remote(self.held.at[peer[1]], self.arrived.at[k - 1], self.sems.at[0, k], self.sems.at[1, k], peer)

    def start(self):
        for move in self.moves():
            move.start()

    def finish(self, out):
        for move in self.moves():
            move.wait_recv()
        units, z = out.shape[0], self.here.z

        def one(unit, carry):
            value = self.held[z, unit].astype(F32)
            for k in range(PARTS - 1):
                value += self.arrived[k, unit].astype(F32)
            out[unit] = value
            return carry

        lax.fori_loop(0, units, one, 0)
        for move in self.moves():
            move.wait_send()


class Sum:
    @staticmethod
    def scratch(rows, width):
        table, low = pltpu.VMEM((4, rows, width), F32), pltpu.VMEM((rows, width), BF16)
        return [table, pltpu.VMEM((3, rows, width), F32), low, pltpu.VMEM((PARTS - 1, rows, width), BF16), DMA((2, 6))]

    def __init__(self, here, sources, scratch):
        self.here, self.sources = here, sources
        self.tables, self.arrived, self.low, self.arrived_low, self.sems = scratch
        self.peers = (here.sibling, here.across, here.beside)

    def move(self, stage):
        sems = self.sems
        return remote(self.tables.at[stage], self.arrived.at[stage], sems.at[0, stage], sems.at[1, stage], self.peers[stage])

    def stack(self, k):
        sems = self.sems
        return remote(self.low, self.arrived_low.at[k - 1], sems.at[0, 2 + k], sems.at[1, 2 + k], self.here.along(k))

    def begin(self):
        tables = self.tables
        tables[0] = jnp.zeros_like(tables[0])
        width = tables.shape[2]
        at = 0
        for source in self.sources:
            rows, columns_held = source.shape
            for start in range(0, columns_held, width):
                tables[0, at : at + rows, :] = source[:, start : start + width]
                at += rows
        self.move(0).start()

    def meet(self, stage):
        self.move(stage).wait_recv()
        self.tables[stage + 1] = self.tables[stage] + self.arrived[stage]
        if stage < 2:
            self.move(stage + 1).start()
        else:
            self.low[...] = self.tables[3].astype(BF16)
            for k in range(1, PARTS):
                self.stack(k).start()

    def finish(self, out):
        value = self.tables[3]
        for k in range(1, PARTS):
            self.stack(k).wait_recv()
            value += self.arrived_low[k - 1].astype(F32)
        out[...] = value
        for stage in range(3):
            self.move(stage).wait_send()
        for k in range(1, PARTS):
            self.stack(k).wait_send()


class Cores:
    @staticmethod
    def scratch(units, tail):
        return [pltpu.VMEM((4, PARTS, units) + tail, BF16), pltpu.VMEM((2, 8, PARTS) + tail, BF16), DMA((units,)), DMA((units,))]

    def __init__(self, here, sums, scratch, hidden):
        self.here, self.sums, self.hidden = here, sums, hidden
        self.far, self.turn, self.send, self.recv = scratch

    def moves(self, n, hidden):
        here, slot = self.here, lax.rem(n, 2)
        give = 1 - here.core
        if hidden:
            to = self.far.at[relative(here.square, n), :, pl.ds(0, self.hidden)]
            return [(self.turn.at[slot, pl.ds(4 * give, 4)], to)], to
        pairs = [(self.turn.at[slot, 2 * s + give], self.far.at[relative(here.square, s), :, n]) for s in range(4)]
        return pairs, self.far.at[:, :, n]

    def each(self, n, action):
        if self.hidden:

            @pl.when(n < self.hidden)
            def _():
                action(True)

            @pl.when(n >= self.hidden)
            def _():
                action(False)
        else:
            action(False)

    def waited(self, n, hidden, recv):
        whole_ref = self.moves(n, hidden)[1]
        move = remote(whole_ref, whole_ref, self.send.at[n], self.recv.at[n], self.here.sibling)
        move.wait_recv() if recv else move.wait_send()

    def put(self, n, value):
        here, slot = self.here, lax.rem(n, 2)

        @pl.when(n >= 2)
        def _():
            self.each(n - 2, lambda hidden: self.waited(n - 2, hidden, False))

        self.turn[slot] = value.reshape(self.turn.shape[1:]).astype(BF16)

        def action(hidden):
            for src, dst in self.moves(n, hidden)[0]:
                remote(src, dst, self.send.at[n], self.recv.at[n], here.sibling).start()
            if hidden:
                self.sums[relative(here.square, n), :, pl.ds(0, self.hidden)] = self.turn[slot, pl.ds(4 * here.core, 4)]
            else:
                for s in range(4):
                    self.sums[relative(here.square, s), :, n] = self.turn[slot, 2 * s + here.core]

        self.each(n, action)

    def collect(self, n):
        def action(hidden):
            self.waited(n, hidden, True)
            if hidden:
                at = relative(self.here.square, n)
                add_into(self.sums.at[at, :, pl.ds(0, self.hidden)], self.far.at[at, :, pl.ds(0, self.hidden)])
            else:

                def one(s, carry):
                    value = self.sums[s, :, n].astype(F32) + self.far[s, :, n].astype(F32)
                    self.sums[s, :, n] = value.astype(BF16)
                    return carry

                lax.fori_loop(0, 4, one, 0)

        self.each(n, action)

    def finish(self, count):
        for n in (count - 2, count - 1):
            self.waited(n, n < self.hidden, False)


class Item:
    def __init__(self, array, spec=None):
        self.array = array
        self.spec = spec or whole(array.shape)


def anywhere(array):
    return Item(array, pl.BlockSpec(memory_space=pl.ANY))


def run(body, steps, ins, outs, scratch, collective, name, cost):
    in_names, out_names, scratch_names = list(ins), list(outs), list(scratch)
    flat_scratch, spans = [], {}
    for key in scratch_names:
        item = scratch[key]
        many = isinstance(item, list)
        spans[key] = (len(flat_scratch), len(item) if many else None)
        flat_scratch += item if many else [item]

    def kernel(*refs):
        first, second = len(in_names), len(in_names) + len(out_names)
        in_refs = dict(zip(in_names, refs[:first]))
        out_refs = dict(zip(out_names, refs[first:second]))
        rest = refs[second:]
        own = {k: rest[at] if n is None else rest[at : at + n] for k, (at, n) in spans.items()}
        here = Here()
        step = pl.program_id(0)

        @pl.when(step == 0)
        def _():
            here.greet()

        body(here, step, in_refs, out_refs, own)

    results = pl.pallas_call(
        kernel,
        grid=(steps,),
        in_specs=[i.spec for i in ins.values()],
        out_specs=tuple(o.spec for o in outs.values()),
        out_shape=tuple(o.array for o in outs.values()),
        scratch_shapes=flat_scratch,
        compiler_params=pltpu.CompilerParams(
            vmem_limit_bytes=BIG, collective_id=collective, has_side_effects=True, dimension_semantics=("arbitrary",)
        ),
        cost_estimate=pl.CostEstimate(flops=cost * 1150000000, bytes_accessed=0, transcendentals=0),
        name=name,
    )(*[i.array for i in ins.values()])
    return dict(zip(out_names, results))


def at_step(step, n):
    def decorate(action):
        pl.when(step == n)(action)

    return decorate


def first_kernel(here, step, ins, outs, own):
    table = own["table"]
    table[...] = jnp.zeros_like(table)
    gain, shift, query_value = ins["gain"], ins["shift"], ins["query_value"]
    for start, item in ((0, gain), (4, shift), (8, query_value)):
        for i in range(4):
            table[start + i : start + i + 1, :] = item[i // 2, i % 2 : i % 2 + 1, :].astype(F32)
    table[12:14, :] = ins["output_bias"][...].astype(F32)
    table[14:16, :] = ins["shrink_bias"][...].astype(F32)
    table[16:17, :] = ins["decode_bias"][...].astype(F32)
    fine = gain.shape[2]
    wide = ins["expand_bias"][...].astype(F32)
    for i in range(8):
        table[17 + i : 18 + i, :] = wide[i // 4 : i // 4 + 1, fine * (i % 4) : fine * (i % 4 + 1)]
    table[25:43, :] = ins["encode"][...].astype(F32).T
    table[43:61, :] = ins["decode"][...].astype(F32)
    gather = Gather(
        here,
        [table, ins["project"].at[0], ins["output"].at[0]],
        [outs["table"], outs["project"], outs["output"]],
        own["gather"],
    )
    signs = ins["signs"].at[0]
    line = Line(here, [outs["signs"]], own["line"], [signs], (False,))
    keep = pltpu.make_async_copy(signs, outs["signs"].at[0], own["keep"].at[0])
    patches = Hop(here, 1, ins["patches"].at[0], outs["patches"], own["patches"])
    for m in range(3):
        gather.start(m)
    line.start(0)
    keep.start()
    patches.start()
    for k in range(1, PARTS):
        for m in range(3):
            gather.hop(m, k)
        line.hop(0, k)
        for m in range(3):
            gather.turn(m, k - 1)
    for m in range(3):
        gather.turn(m, PARTS - 1)
        gather.siblings(m)
    for m in range(3):
        gather.corner(m)
    for m in range(3):
        gather.finish(m)
    line.finish(0)
    patches.finish()
    keep.wait()


def forward_attention(coded, layer, slots, ins, extra, collective):
    weight = ins["weight"].array
    rows = ins["segment_column"].array.shape[0]
    width, triple = weight.shape
    length = PARTS * rows
    pairs, lanes = width // (2 * HD), 2 * HD
    steps = PARTS + pairs
    outs = {
        "qkv": Item(shaped((length, triple)), pl.BlockSpec((rows, triple), lambda i: (jnp.minimum(i, PARTS - 1), 0))),
        "normed": Item(shaped((rows, width))),
        "mixed": Item(shaped((rows, width)), pl.BlockSpec((rows, lanes), lambda i: (0, jnp.maximum(i - PARTS, 0)))),
        "logs": Item(shaped((rows, 128), F32)),
    }
    if coded:
        outs["stream"] = Item(shaped((rows, width), F32))
    scratch = {"qkv_held": pltpu.VMEM((length, triple), BF16), "piece": pltpu.VMEM((rows, width), BF16)}
    extra.declare(ins, outs, scratch)

    def body(here, step, ins, outs, own):
        extra.events(here, step, steps, ins, outs, own)
        table = ins["table"]
        held = own["qkv_held"]

        @pl.when(step < PARTS)
        def _():
            if coded:
                decode = table[43:61, :].astype(BF16)
                stream = mm(ins["pieces"][step], decode) + table[16:17, :]
            else:
                inner = (here.z > 0) & (here.z < PARTS - 1)
                choices = [step == 0, step == 1, step == 2, (step == 3) & inner, (step == 3) & jnp.logical_not(inner)]
                for n, meets in enumerate(choices):

                    @pl.when(meets)
                    def _():
                        own["piece"][...] = ins[f"piece{n}"][0]

                stream = own["piece"][...].astype(F32)
            hat, unused = norm_parts(stream)
            normed = (hat * table[2 * layer : 2 * layer + 1, :] + table[4 + 2 * layer : 5 + 2 * layer, :]).astype(BF16)
            at = pl.ds(pl.multiple_of(step * rows, rows), rows)
            for part in range(3):
                span = pl.ds(part * width, width)
                value = mm(normed, ins["weight"][:, span])
                if part != 1:
                    shift = 8 + 2 * layer + part // 2
                    value += table[shift : shift + 1, :]
                value = value.astype(BF16)
                outs["qkv"][:, span] = value
                held[at, span] = value

            @pl.when(step == 0)
            def _():
                outs["normed"][...] = normed
                if coded:
                    outs["stream"][...] = stream

        @pl.when(step >= PARTS)
        def _():
            pair = step - PARTS
            logs = outs["logs"]
            lane = lax.broadcasted_iota(jnp.int32, (1, 128), 1)

            @pl.when(pair == 0)
            def _():
                logs[...] = jnp.zeros_like(logs)

            def span(part):
                return pl.ds(pl.multiple_of(part * width + pair * lanes, lanes), lanes)

            keys, values = held[:, span(1)], held[:, span(2)]
            segments = ins["segment_row"][...]
            for start in range(0, rows, BLOCK):
                at = pl.ds(start, BLOCK)
                same = ins["segment_column"][at, :] == segments
                queries = held[at, span(0)] * jnp.asarray(HD**-0.5, BF16)
                parts = []
                for head in range(2):
                    scores = jnp.where(same, mm(only(queries, head), keys, NT), masked_score)
                    top = jnp.max(scores, axis=-1, keepdims=True)
                    raised = jnp.exp(scores - top)
                    total = jnp.sum(raised, axis=-1, keepdims=True)
                    parts.append(mm(raised.astype(BF16), values) / total)
                    logs[at, :] += jnp.where(lane == 2 * pair + head, top + jnp.log(total), 0.0)
                outs["mixed"][at, :] = jnp.where(lanes_of(0), parts[0], parts[1]).astype(BF16)

        extra.closing(here, step, steps, ins, outs, own)

    return run(body, steps, ins, outs, scratch, collective, "forward_attention", 30)


BLOCK = 192
QUERY_BLOCK = 384


def middle_block(encoder, layer, slots, ins, extra, collective):
    width = ins["output"].array.shape[1]
    rows = ins["mixed"].array.shape[0]
    hidden = ins["shrink"].array.shape[0]
    fine = width // slots // PARTS
    tile = 512
    tiles = hidden // tile
    feed = 2 * tiles if encoder else tiles
    units = hidden // width + hidden // width + 1
    wide = hidden // width
    pairs, lanes = width // (2 * HD), 2 * HD
    length = PARTS * rows
    first_query = feed + units
    first_key = first_query + pairs
    steps = first_key + 2 * pairs

    def tiled(i):
        return lax.rem(jnp.minimum(i, feed - 1), tiles)

    ins["expand"].spec = pl.BlockSpec((width, tile), lambda i: (0, tiled(i)))
    ins["expand_shift"].spec = pl.BlockSpec((1, tile), lambda i: (0, tiled(i)))
    ins["shrink"].spec = pl.BlockSpec((tile, width), lambda i: (tiled(i), 0))
    ins["stream"].spec = pl.BlockSpec((1, rows, width), lambda i: (0, 0, 0))
    outs = {
        "query": Item(shaped((rows, width)), pl.BlockSpec((rows, lanes), lambda i: (0, jnp.clip(i - first_query, 0, pairs - 1)))),
        "key": Item(shaped((rows, width)), pl.BlockSpec((rows, lanes), lambda i: (0, jnp.maximum(i - first_key - pairs, 0)))),
        "value": Item(shaped((rows, width)), pl.BlockSpec((rows, lanes), lambda i: (0, jnp.maximum(i - first_key - pairs, 0)))),
        "middle": Item(shaped((rows, width), F32)),
        "small": Item(shaped((8, width), F32)),
        "wide": Item(shaped((1, hidden), F32)),
    }
    scratch = {
        "active": pltpu.VMEM((rows, hidden), BF16),
        "hidden_low": pltpu.VMEM((rows, hidden), BF16),
        "normed": pltpu.VMEM((rows, width), BF16),
        "hat": pltpu.VMEM((rows, width), F32),
        "scale": pltpu.VMEM((rows, 1), F32),
        "total": pltpu.VMEM((rows, width), F32),
        "back": pltpu.VMEM((rows, width), F32),
        "low": pltpu.VMEM((rows, width), BF16),
        "branch": pltpu.VMEM((rows, width), BF16),
        "delta": pltpu.VMEM((rows, 128), F32),
        "qkv_held": pltpu.VMEM((length, 3 * width), BF16),
        "qkv_sem": DMA((1,)),
        "mixed_back": pltpu.VMEM((PARTS, rows, width), BF16),
        "stats": pltpu.VMEM((PARTS, 32, rows), F32),
        "line": Line.scratch(2),
        "cores": Cores.scratch(units, (fine, width)),
    }
    if encoder:
        outs["code_grad"] = Item(shaped((CODE, width), F32))
        scratch["slope"] = pltpu.VMEM((tiles, rows, tile), BF16)
        scratch["sums"] = pltpu.VMEM((4, PARTS, units, fine, width), BF16)
    else:
        outs["decoded"] = Item(shaped((rows, width)))
        outs["sums"] = Item(shaped((4, PARTS, units, fine, width)))
    extra.declare(ins, outs, scratch)

    def body(here, step, ins, outs, own):
        table = ins["table"]
        normed, hat, scale, total, back, low = (own[n] for n in ("normed", "hat", "scale", "total", "back", "low"))
        mixed_back, stats, held = own["mixed_back"], own["stats"], own["qkv_held"]
        sums = own["sums"] if encoder else outs["sums"]
        cores = Cores(here, sums, own["cores"], wide)
        line = Line(here, [mixed_back, stats], own["line"], None, (False, False))
        load = pltpu.make_async_copy(ins["qkv"], held, own["qkv_sem"].at[0])
        gain, shift = table[2 * layer + 1 : 2 * layer + 2, :], table[5 + 2 * layer : 6 + 2 * layer, :]
        extra.events(here, step, steps, ins, outs, own)

        @at_step(step, 0)
        def _():
            load.start()
            middle = ins["stream"][0].astype(F32) + mm(ins["mixed"][...], ins["output"][...]) + table[12 + layer : 13 + layer, :]
            hat[...], scale[...] = norm_parts(middle)
            normed[...] = (hat[...] * gain + shift).astype(BF16)
            total[...] = middle + table[14 + layer : 15 + layer, :]
            back[...] = jnp.zeros_like(back)
            if not encoder:
                low[...] = ins["other"][...]

        def columns_at(n):
            return pl.ds(pl.multiple_of(n * tile, tile), tile)

        def forward(n):
            value = mm(normed[...], ins["expand"][...]) + ins["expand_shift"][...]
            active, steep = gelu_parts(value)
            active = active.astype(BF16)
            own["active"][:, columns_at(n)] = active
            total[...] += mm(active, ins["shrink"][...])
            return steep

        def backward(n, steep):
            hidden_low = (steep * mm(low[...], ins["shrink"][...], NT)).astype(BF16)
            own["hidden_low"][:, columns_at(n)] = hidden_low
            outs["wide"][:, columns_at(n)] = columns(hidden_low.astype(F32))
            back[...] += mm(hidden_low, ins["expand"][...], NT)

        if encoder:

            @pl.when(step < tiles)
            def _():
                own["slope"][step] = forward(step).astype(BF16)

            @at_step(step, tiles - 1)
            def _():
                code = table[25:43, :].astype(BF16)
                encoded_low = total[...].astype(BF16)
                coded = mm(encoded_low, code, NT)
                size = lax.rsqrt(jnp.sum(coded * coded, axis=-1, keepdims=True) + epsilon)
                unit = coded * size
                grad = ins["other"][...]
                coded_low = ((grad - unit * jnp.sum(unit * grad, axis=-1, keepdims=True)) * size).astype(BF16)
                outs["code_grad"][...] = mm(coded_low, encoded_low, TN)
                total[...] = mm(coded_low, code)
                low[...] = total[...].astype(BF16)

            @pl.when((step >= tiles) & (step < feed))
            def _():
                backward(step - tiles, own["slope"][step - tiles].astype(F32))
        else:

            @pl.when(step < tiles)
            def _():
                backward(step, forward(step))

        @at_step(step, feed - 1)
        def _():
            if encoder:
                grad_out = total[...]
            else:
                outs["decoded"][...] = total[...].astype(BF16)
                grad_out = low[...].astype(F32)
            grad = back[...]
            middle = grad_out + norm_back(grad, gain, hat[...], scale[...])
            outs["middle"][...] = middle
            branch = middle.astype(BF16)
            own["branch"][...] = branch
            mixed_low = mm(branch, ins["output"][...], NT).astype(BF16)
            mixed_back[0] = mixed_low
            product = mixed_low.astype(F32) * ins["mixed"][...].astype(F32)
            feature = lax.broadcasted_iota(jnp.int32, (width, 128), 0) // HD
            heads = (feature == lax.broadcasted_iota(jnp.int32, (width, 128), 1)).astype(F32)
            delta = lax.dot_general(product, heads, NN, preferred_element_type=F32, precision=lax.Precision.HIGHEST)
            own["delta"][...] = delta
            stats[0, pl.ds(0, 16)] = ins["logs"][...].T[:16]
            stats[0, pl.ds(16, 16)] = delta.T[:16]
            for m in range(2):
                line.start(m)
            outs["small"][...] = jnp.concatenate(
                [columns(grad * hat[...]), columns(grad), columns(branch.astype(F32)), columns(low[...].astype(F32))]
                + [jnp.zeros_like(columns(grad))] * 4
            )

        unit = step - feed

        def wide_at(n):
            return pl.ds(pl.multiple_of(n * width, width), width)

        @pl.when((unit >= 0) & (unit < wide))
        def _():
            cores.put(unit, mm(own["active"][:, wide_at(unit)], low[...], TN))

        @pl.when((unit >= wide) & (unit < 2 * wide))
        def _():
            cores.put(unit, mm(normed[...], own["hidden_low"][:, wide_at(unit - wide)], TN))

        @pl.when(unit == 2 * wide)
        def _():
            cores.put(unit, mm(ins["mixed"][...], own["branch"][...], TN))

        @pl.when((unit >= 2) & (unit < units))
        def _():
            cores.collect(unit - 2)

        @pl.when(unit == units)
        def _():
            cores.collect(unit - 2)
            cores.collect(unit - 1)
            cores.finish(units)

        for n, k in ((units, 1), (units + 5, 2)):

            @pl.when(unit == n)
            def _():
                for m in range(2):
                    line.hop(m, k)

        @at_step(step, first_query)
        def _():
            load.wait()

        eighth = jnp.asarray(HD**-0.5, BF16)

        @pl.when((step >= first_query) & (step < first_key))
        def _():
            pair = step - first_query
            lane = lax.broadcasted_iota(jnp.int32, (1, 128), 1)

            def span(part):
                return pl.ds(pl.multiple_of(part * width + pair * lanes, lanes), lanes)

            keys, values = held[:, span(1)], held[:, span(2)]
            segments = ins["segment_row"][...]
            for start in range(0, rows, QUERY_BLOCK):
                at = pl.ds(start, QUERY_BLOCK)
                same = ins["segment_column"][at, :] == segments
                queries = held[at, span(0)] * eighth
                grads = mixed_back[0, at, span(0)]
                parts = []
                for head in range(2):
                    mine = lane == 2 * pair + head
                    log_sum = jnp.sum(jnp.where(mine, ins["logs"][at, :], 0.0), axis=-1, keepdims=True)
                    centre = jnp.sum(jnp.where(mine, own["delta"][at, :], 0.0), axis=-1, keepdims=True)
                    scores = jnp.where(same, mm(only(queries, head), keys, NT), masked_score)
                    probability = jnp.exp(scores - log_sum)
                    prob_grad = mm(only(grads, head), values, NT)
                    score_low = (probability * (prob_grad - centre)).astype(BF16)
                    parts.append(mm(score_low, keys) * HD**-0.5)
                outs["query"][at, :] = jnp.where(lanes_of(0), parts[0], parts[1]).astype(BF16)

        late = step - first_key

        @pl.when(late == pairs)
        def _():
            for m in range(2):
                line.hop(m, 3)

        for half in range(2):

            @pl.when((late >= half * pairs) & (late < (half + 1) * pairs))
            def _():
                pair = late - half * pairs
                pieces = range(2 * half, 2 * half + 2)

                def span(part):
                    return pl.ds(pl.multiple_of(part * width + pair * lanes, lanes), lanes)

                these = pl.ds(2 * half * rows, 2 * rows)
                queries = held[these, span(0)]
                grads = mixed_back[2 * half : 2 * half + 2, :, span(0)].reshape(2 * rows, lanes)

                def line_of(row):
                    return jnp.concatenate([stats[k, pl.ds(row, 1), :] for k in pieces], axis=1)

                same = ins["segment_column"][...] == ins["segment_row"][:, these]
                keys = held[pl.ds(0, rows), span(1)] * eighth
                values = held[pl.ds(0, rows), span(2)]
                key_parts, value_parts = [], []
                for head in range(2):
                    scores = jnp.where(same, mm(only(keys, head), queries, NT), masked_score)
                    probability = jnp.exp(scores - line_of(2 * pair + head))
                    value_parts.append(mm(probability.astype(BF16), grads))
                    prob_grad = mm(only(values, head), grads, NT)
                    score_low = (probability * (prob_grad - line_of(16 + 2 * pair + head))).astype(BF16)
                    key_parts.append(mm(score_low, queries) * HD**-0.5)
                key = jnp.where(lanes_of(0), key_parts[0], key_parts[1])
                value = jnp.where(lanes_of(0), value_parts[0], value_parts[1])
                if half == 0:
                    hat[:, span(0)] = key
                    total[:, span(0)] = value
                else:
                    outs["key"][...] = (hat[:, span(0)] + key).astype(BF16)
                    outs["value"][...] = (total[:, span(0)] + value).astype(BF16)

        @at_step(step, steps - 1)
        def _():
            for m in range(2):
                line.finish(m)

        extra.closing(here, step, steps, ins, outs, own)

    return run(body, steps, ins, outs, scratch, collective, "encoder_middle" if encoder else "decoder_middle", 80)


def projection_back(coded, layer, slots, ins, extra, collective):
    rows, width = ins["query"].array.shape
    fine = width // slots // PARTS
    units = 3
    steps = 2 + units
    ins["stream"].spec = pl.BlockSpec((1, rows, width), lambda i: (0, 0, 0))
    outs = {"small": Item(shaped((8, width), F32)), "sums": Item(shaped((4, PARTS, units, fine, width)))}
    if coded:
        outs["unit_grad"] = Item(shaped((rows, CODE), F32))
        outs["decode_grad"] = Item(shaped((CODE, width), F32))
        ins["pieces"].spec = pl.BlockSpec((1, rows, CODE), lambda i: (0, 0, 0))
    else:
        outs["grad"] = Item(shaped((rows, width), F32))
    scratch = {"cores": Cores.scratch(units, (fine, width))}
    extra.declare(ins, outs, scratch)

    def body(here, step, ins, outs, own):
        table = ins["table"]
        cores = Cores(here, outs["sums"], own["cores"], 0)
        extra.events(here, step, steps, ins, outs, own)
        sources = (ins["query"], ins["key"], ins["value"])
        for n in range(units):

            @at_step(step, n)
            def _():
                cores.put(jnp.int32(n), mm(ins["normed"][...], sources[n][...], TN))

        for n in range(units):

            @at_step(step, n + 1)
            def _():
                cores.collect(jnp.int32(n))

        @at_step(step, units)
        def _():
            cores.finish(units)

        @at_step(step, units + 1)
        def _():
            query, key, value = sources
            weight = ins["weight"]
            grad = mm(query[...], weight[:, :width], NT)
            grad += mm(key[...], weight[:, width : 2 * width], NT)
            grad += mm(value[...], weight[:, 2 * width :], NT)
            hat, scale = norm_parts(ins["stream"][0].astype(F32))
            start = ins["middle"][...] + norm_back(grad, table[2 * layer : 2 * layer + 1, :], hat, scale)
            small = [columns(grad * hat), columns(grad), columns(query[...].astype(F32)), columns(value[...].astype(F32))]
            if coded:
                start_low = start.astype(BF16)
                outs["unit_grad"][...] = mm(start_low, table[43:61, :].astype(BF16), NT)
                outs["decode_grad"][...] = mm(ins["pieces"][0], start_low, TN)
                small.append(columns(start_low.astype(F32)))
            else:
                outs["grad"][...] = start
            small += [jnp.zeros_like(small[0])] * (8 - len(small))
            outs["small"][...] = jnp.concatenate(small)

        extra.closing(here, step, steps, ins, outs, own)

    return run(body, steps, ins, outs, scratch, collective, "projection_back", 12)


def last_kernel(here, step, ins, outs, own):
    stacks = [Stack(here, ins[f"total{n}"], own[f"stack{n}"]) for n in range(3)]
    rows = Sum(here, [ins["small"]], own["sum"])
    rows.begin()
    for stack in stacks:
        stack.start()
    for stage in range(3):
        rows.meet(stage)
    for n, stack in enumerate(stacks):
        stack.finish(outs["units"].at[pl.ds(n, 1)])
    rows.finish(outs["rows"])


def assemble_kernel(project0, project1, five, six, two, three, four, project, output, expand, shrink):
    encoder = [(five, n) for n in range(five.shape[0])] + [(six, n) for n in range(six.shape[0])]
    decoder = [(part, n) for part in (two, three, four) for n in range(part.shape[0])]
    fine, width = project0.shape[1:]
    for layer, units, triple in ((0, encoder, project0), (1, decoder, project1)):
        for n in range(3):
            project[layer, :, n * width : (n + 1) * width] = triple[n]
        for n in range(4):
            ref, at = units[n]
            shrink[layer, n * fine : (n + 1) * fine, :] = ref[at]
            ref, at = units[4 + n]
            expand[layer, :, n * width : (n + 1) * width] = ref[at]
        ref, at = units[8]
        output[layer] = ref[at]


class Nothing:
    def declare(self, ins, outs, scratch):
        pass

    def events(self, here, step, steps, ins, outs, own):
        pass

    def closing(self, here, step, steps, ins, outs, own):
        pass


class Beside(Nothing):
    def __init__(
        self, slots, gathers=None, gather_steps=(), squares=None, stacks=None, sums=None, lines=None, line_steps=(), spreads=None, spread_steps=(), hop=None
    ):
        self.hop = hop
        self.lines, self.line_steps, self.spreads, self.spread_steps = lines or {}, line_steps, spreads or {}, spread_steps
        self.slots, self.gathers, self.gather_steps = slots, gathers or {}, gather_steps
        self.squares, self.stacks, self.sums = squares or {}, stacks or {}, sums or {}

    def declare(self, ins, outs, scratch):
        if self.hop:
            array = self.hop[1]
            ins["hop"] = anywhere(array)
            outs["hopped"] = anywhere(shaped(array.shape))
            scratch["hop"] = Hop.scratch()
        for name, (array, layer) in self.gathers.items():
            block = (1,) + array.shape[1:]
            ins["shard_" + name] = Item(array, pl.BlockSpec(block, lambda i, layer=layer: (layer, 0, 0)))
            outs["gathered_" + name] = anywhere(shaped((self.slots, PARTS) + array.shape[1:]))
        if self.gathers:
            scratch["gather"] = Gather.scratch(len(self.gathers))
        for name, (item, absolute) in self.lines.items():
            ins["line_" + name] = item
            outs["lined_" + name] = anywhere(shaped((PARTS,) + item.spec.block_shape[1:]))
        if self.lines:
            scratch["lines"] = Line.scratch(len(self.lines)) + [DMA((len(self.lines),))]
        for name, array in self.spreads.items():
            ins["spread_" + name] = Item(array)
            outs["gathered_" + name] = anywhere(shaped((self.slots,) + array.shape))
        if self.spreads:
            scratch["spreads"] = Spread.scratch(len(self.spreads))
        for name, (sums, first, units, steps) in self.squares.items():
            loaded = sums is not None
            if loaded:
                tail = sums.shape[3:]
            else:
                tail = (scratch["sums"] if "sums" in scratch else outs["sums"].array).shape[3:]
            if loaded:
                ins["square_" + name] = anywhere(sums)
            outs["total_" + name] = Item(shaped((PARTS, units) + tail))
            scratch["square_" + name] = Square.scratch(units, tail, loaded)
        for name, (array, steps) in self.stacks.items():
            if isinstance(array, str):
                shape = outs["total_" + array].array.shape
            else:
                ins["stack_" + name] = Item(array)
                shape = array.shape
            outs["stacked_" + name] = Item(shaped(shape[1:], F32))
            scratch["stack_" + name] = Stack.scratch(shape[1], shape[2:])
        for name, (arrays, steps) in self.sums.items():
            for i, array in enumerate(arrays):
                if isinstance(array, str):
                    arrays = arrays[:i] + [outs[array].array] + arrays[i + 1 :]
                else:
                    ins[f"sum_{name}{i}"] = Item(array)
            width = min(a.shape[1] for a in arrays)
            rows = -(-sum(a.shape[0] * (a.shape[1] // width) for a in arrays) // 16) * 16
            outs["summed_" + name] = Item(shaped((rows, width), F32))
            scratch["sum_" + name] = Sum.scratch(rows, width)

    def listed(self, here, ins, outs, own):
        if self.hop:
            hop_task = Hop(here, self.hop[0], ins["hop"], outs["hopped"], own["hop"])
            yield self.hop[2], hop_task.start
            yield None, hop_task.finish
        if self.gathers:
            names = list(self.gathers)
            gather = Gather(here, [ins["shard_" + n].at[0] for n in names], [outs["gathered_" + n] for n in names], own["gather"])

            def each(*actions):
                def go():
                    for action, *more in actions:
                        for m in range(len(names)):
                            action(m, *more)

                return go

            start, one, two, three, turn, corner = self.gather_steps
            yield start, each((gather.start,))
            yield one, each((gather.hop, 1), (gather.turn, 0))
            yield two, each((gather.hop, 2), (gather.turn, 1))
            yield three, each((gather.hop, 3), (gather.turn, 2))
            yield turn, each((gather.turn, 3), (gather.siblings,))
            yield corner, each((gather.corner,))
            yield None, each((gather.finish,))
        if self.lines:
            line_names = list(self.lines)
            sources = [ins["line_" + n].at[0] for n in line_names]
            arrays = [outs["lined_" + n] for n in line_names]
            sems = own["lines"]
            line = Line(here, arrays, sems[:3], sources, [absolute for item, absolute in self.lines.values()])
            keeps = [
                pltpu.make_async_copy(sources[m], line.at(m, here.z, here.z), sems[3].at[m]) for m in range(len(line_names))
            ]

            def begin():
                for m in range(len(line_names)):
                    line.start(m)
                    keeps[m].start()

            def end():
                for m in range(len(line_names)):
                    line.finish(m)
                    keeps[m].wait()

            def hop(k):
                for m in range(len(line_names)):
                    line.hop(m, k)

            yield self.line_steps[0], begin
            for k in range(1, PARTS):
                yield self.line_steps[k], functools.partial(hop, k)
            yield None, end
        if self.spreads:
            spread_names = list(self.spreads)
            spread = Spread(here, [ins["spread_" + n] for n in spread_names], [outs["gathered_" + n] for n in spread_names], own["spreads"])
            for action, n in zip((spread.start, spread.turn, spread.corner, spread.finish), self.spread_steps):

                def go(action=action):
                    for m in range(len(spread_names)):
                        action(m)

                yield n, go
        for name, (sums, first, units, steps) in self.squares.items():
            scratch = own["square_" + name]
            span = pl.ds(first, units)
            if sums is None:
                held = own["sums"] if "sums" in own else outs["sums"]
                square = Square(here, held.at[:, :, span], scratch)
            else:
                square = Square(here, scratch[0], scratch[1:], ins["square_" + name].at[:, :, span])
                yield steps[0], square.load
            yield steps[1], square.start
            yield steps[2], square.sides
            yield steps[3], functools.partial(square.total, outs["total_" + name])
        for name, (array, steps) in self.stacks.items():
            held = outs["total_" + array] if isinstance(array, str) else ins["stack_" + name]
            stack = Stack(here, held, own["stack_" + name])
            yield steps[0], stack.start
            yield steps[1], functools.partial(stack.finish, outs["stacked_" + name])
        for name, (arrays, steps) in self.sums.items():
            sources = [outs[a] if isinstance(a, str) else ins[f"sum_{name}{i}"] for i, a in enumerate(arrays)]
            rows = Sum(here, sources, own["sum_" + name])
            yield steps[0], rows.begin
            for stage in range(3):
                yield steps[1 + stage], functools.partial(rows.meet, stage)
            yield steps[4], functools.partial(rows.finish, outs["summed_" + name])

    def grouped(self, here, ins, outs, own):
        groups = {}
        for n, action in self.listed(here, ins, outs, own):
            groups.setdefault(n, []).append(action)
        return groups

    def play(self, step, n, actions):
        def go():
            for action in actions:
                action()

        at_step(step, n)(go)

    def events(self, here, step, steps, ins, outs, own):
        for n, actions in sorted((n, a) for n, a in self.grouped(here, ins, outs, own).items() if n is not None):
            self.play(step, n, actions)

    def closing(self, here, step, steps, ins, outs, own):
        actions = self.grouped(here, ins, outs, own).get(None)
        if actions:
            self.play(step, steps - 1, actions)


FORWARD1_GATHER = (0, 3, 6, 9, None, None)
MIDDLE1_GATHER = (0, 5, 15, 21, 27, 31)
FORWARD0_SQUARE = (0, 1, 4, None)


def on_device(
    patches,
    segments,
    code_bits,
    norm_gain,
    norm_shift,
    project_weight,
    query_value_bias,
    output_weight,
    output_bias,
    expand_weight,
    expand_bias,
    shrink_weight,
    shrink_bias,
    encode_weight,
    decode_weight,
    decode_bias,
    cotangent,
):
    slots, parts = lax.axis_size("slot"), lax.axis_size("seq")
    fine, width = project_weight.shape[1], patches.shape[-1]
    if slots != 8 or parts != PARTS or fine % 8:
        return plain_device(
            patches,
            segments,
            code_bits,
            norm_gain,
            norm_shift,
            project_weight,
            query_value_bias,
            output_weight,
            output_bias,
            expand_weight,
            expand_bias,
            shrink_weight,
            shrink_bias,
            encode_weight,
            decode_weight,
            decode_bias,
            cotangent,
        )
    slot, z = lax.axis_index("slot"), lax.axis_index("seq")
    devices, rows, hidden = slots * parts, patches.shape[1], expand_weight.shape[-1]
    signs = ((2 * code_bits - 1).astype(F32) * CODE ** (-0.5)).astype(BF16)

    ins = {
        "gain": Item(norm_gain),
        "shift": Item(norm_shift),
        "query_value": Item(query_value_bias),
        "output_bias": Item(output_bias),
        "shrink_bias": Item(shrink_bias),
        "decode_bias": Item(decode_bias.reshape(1, fine)),
        "expand_bias": Item(expand_bias),
        "encode": Item(encode_weight),
        "decode": Item(decode_weight),
    }
    weights = {"project": project_weight, "output": output_weight, "expand": expand_weight, "shrink": shrink_weight}

    def shard(name, layer):
        array = weights[name]
        return Item(array, pl.BlockSpec((1,) + array.shape[1:], lambda i: (layer, 0, 0)))

    ins["signs"], ins["patches"] = Item(signs), Item(patches)
    ins["project"], ins["output"] = shard("project", 1), shard("output", 1)
    outs = {
        "table": anywhere(shaped((slots, parts, 64, fine), F32)),
        "project": anywhere(shaped((slots, parts) + project_weight.shape[1:])),
        "output": anywhere(shaped((slots, parts) + output_weight.shape[1:])),
        "signs": anywhere(shaped((parts, rows, CODE))),
        "patches": anywhere(shaped((parts, rows, width))),
    }
    names = ("expand", "shrink")
    scratch = {
        "table": pltpu.VMEM((64, fine), F32),
        "gather": Gather.scratch(3),
        "line": Line.scratch(1),
        "keep": DMA((1,)),
        "patches": Hop.scratch(),
    }
    first = run(first_kernel, 1, ins, outs, scratch, 0, "first_gather", 30)

    small = first["table"].reshape(devices, 64, fine)
    table = small.transpose(1, 0, 2).reshape(64, width)
    expand_shifts = small[:, 17:25].reshape(devices, 2, 4, fine).transpose(1, 0, 2, 3).reshape(2, 1, hidden)
    around = jnp.arange(parts) ^ z
    pieces = segments[0].reshape(parts, rows)[around]
    segment_row = pieces.reshape(1, parts * rows)
    segment_column = pieces[0].reshape(rows, 1)

    def flat(array):
        return array.reshape(-1, array.shape[-1])

    def piece(array, n):
        return Item(array, pl.BlockSpec((1, rows, width), lambda i: (n, 0, 0)))

    def forward(layer, pieces, weight, extra, collective):
        ins = {
            **pieces,
            "table": Item(table),
            "weight": Item(weight),
            "segment_row": Item(segment_row),
            "segment_column": Item(segment_column),
        }
        return forward_attention(layer == 1, layer, slots, ins, extra, collective)

    def middle(layer, stream, other, ahead, weights, extra, collective):
        ins = {
            "stream": Item(stream),
            "mixed": Item(ahead["mixed"]),
            "other": Item(other),
            "logs": Item(ahead["logs"]),
            "qkv": anywhere(ahead["qkv"]),
            "table": Item(table),
            "output": Item(weights["output"]),
            "expand": Item(weights["expand"]),
            "expand_shift": Item(expand_shifts[layer]),
            "shrink": Item(weights["shrink"]),
            "segment_row": Item(segment_row),
            "segment_column": Item(segment_column),
        }
        return middle_block(layer == 0, layer, slots, ins, extra, collective)

    def projection(layer, stream, ahead, between, weight, extra, collective, **more):
        ins = {
            "query": Item(between["query"]),
            "key": Item(between["key"]),
            "value": Item(between["value"]),
            "normed": Item(ahead["normed"]),
            "stream": Item(stream),
            "middle": Item(between["middle"]),
            "table": Item(table),
            "weight": Item(weight),
        }
        ins.update({k: Item(v) for k, v in more.items()})
        return projection_back(layer == 1, layer, slots, ins, extra, collective)

    decoder = {n: flat(first[n]) for n in ("project", "output")}
    beside = Beside(slots, {n: (weights[n], 1) for n in names}, FORWARD1_GATHER, hop=(2, first["patches"], 1))
    ahead1 = forward(1, {"pieces": Item(first["signs"])}, decoder["project"], beside, 1)
    decoder.update({n: flat(ahead1["gathered_" + n]) for n in names})

    beside = Beside(slots, {n: (weights[n], 0) for n in weights}, MIDDLE1_GATHER)
    stream1 = ahead1["stream"][None]
    between1 = middle(1, stream1, cotangent[0], ahead1, decoder, beside, 2)
    encoder = {n: flat(between1["gathered_" + n]) for n in weights}
    beside = Beside(slots, squares={"two": (between1["sums"], 0, 3, (0, 1, 3, None))}, hop=(3, ahead1["hopped"], 0))
    after1 = projection(1, stream1, ahead1, between1, decoder["project"], beside, 3, pieces=first["signs"])

    beside = Beside(
        slots,
        squares={"three": (between1["sums"], 3, 5, FORWARD0_SQUARE)},
        stacks={"two": (after1["total_two"], (0, 6))},
        sums={"one": ([after1["small"], between1["small"], between1["wide"], after1["decode_grad"]], (0, 1, 3, 6, None))},
    )
    pieces = [piece(patches, 0), piece(first["patches"], 1), piece(ahead1["hopped"], 2)]
    pieces += [piece(first["patches"], 3), piece(after1["hopped"], 3)]
    ahead0 = forward(0, {f"piece{n}": item for n, item in enumerate(pieces)}, encoder["project"], beside, 4)
    beside = Beside(
        slots,
        squares={
            "one": (after1["sums"], 0, 3, (0, 1, 4, 9)),
            "four": (between1["sums"], 8, 1, (0, 1, 4, 9)),
            "five": (None, 0, 4, (None, 18, 22, 28)),
            "six": (None, 4, 5, (None, 22, 30, None)),
        },
        stacks={
            "three": (ahead0["total_three"], (0, 9)),
            "one": ("one", (10, 18)),
            "five": ("five", (33, None)),
        },
        sums={"two": (["small", "wide", "code_grad"], (13, 15, 17, 20, 28))},
    )
    between0 = middle(0, patches, after1["unit_grad"], ahead0, encoder, beside, 5)
    beside = Beside(
        slots,
        squares={f"seven{n}": (None, n, 1, (None, n + 2, 4, None)) for n in range(3)},
        stacks={n: (between0["total_" + n], (0, None)) for n in ("six", "four")},
    )
    after0 = projection(0, patches, ahead0, between0, encoder["project"], beside, 6)

    ins = {f"total{n}": Item(after0[f"total_seven{n}"]) for n in range(3)}
    ins["small"] = Item(after0["small"])
    outs = {"units": Item(shaped((3, fine, width), F32)), "rows": Item(shaped((16, width), F32))}
    scratch = {f"stack{n}": Stack.scratch(1, (fine, width)) for n in range(3)}
    scratch["sum"] = Sum.scratch(16, width)
    last = run(last_kernel, 1, ins, outs, scratch, 7, "last_sums", 20)

    units = [last["units"], between0["stacked_one"], between0["stacked_five"], after0["stacked_six"]]
    units += [ahead0["stacked_two"], between0["stacked_three"], after0["stacked_four"]]
    project_grad, output_grad, expand_grad, shrink_grad = pl.pallas_call(
        assemble_kernel,
        out_shape=tuple(shaped(weights[n].shape, F32) for n in ("project", "output", "expand", "shrink")),
        compiler_params=pltpu.CompilerParams(vmem_limit_bytes=BIG),
        name="assemble",
    )(*units)

    device = slot * parts + z
    one, two = ahead0["summed_one"], between0["summed_two"]
    summed = jnp.concatenate([last["rows"][:8], one, two])
    mine = lax.dynamic_slice(summed, (0, device * fine), (summed.shape[0], fine))
    in0, in1, mid1 = mine[0:4], mine[8:13], mine[16:20]
    at = 8 + one.shape[0]
    mid0, decode_grad, code_grad = mine[at : at + 4], mine[28:46], mine[at + 12 : at + 30]
    wide = jnp.stack([two[8:12].reshape(hidden), one[16:20].reshape(hidden)])
    wide = lax.dynamic_slice(wide, (0, device * (hidden // devices)), (2, hidden // devices))
    return (
        between1["decoded"][None],
        after0["grad"][None],
        jnp.stack([jnp.stack([in0[0], mid0[0]]), jnp.stack([in1[0], mid1[0]])]),
        jnp.stack([jnp.stack([in0[1], mid0[1]]), jnp.stack([in1[1], mid1[1]])]),
        project_grad,
        jnp.stack([in0[2:4], in1[2:4]]),
        output_grad,
        jnp.stack([mid0[2], mid1[2]]),
        expand_grad,
        wide,
        shrink_grad,
        jnp.stack([mid0[3], mid1[3]]),
        code_grad.T,
        decode_grad,
        in1[4],
    )


def plain_norm(stream, gains, shifts):
    centre = stream - jnp.mean(stream, axis=-1, keepdims=True)
    spread = jnp.mean(centre * centre, axis=-1, keepdims=True)
    return centre * lax.rsqrt(spread + epsilon) * gains + shifts


def normalize(coded):
    return coded / jnp.sqrt(jnp.sum(coded * coded, axis=-1, keepdims=True) + epsilon)


def gelu_exact(hidden):
    return jax.nn.gelu(hidden, approximate=False)


def gather_weights(shards):
    return (
        lax.all_gather(shards[0], ("slot", "seq"), axis=2, tiled=True),
        lax.all_gather(shards[1], ("slot", "seq"), axis=2, tiled=True),
        lax.all_gather(shards[2], ("slot", "seq"), axis=1, tiled=True),
        lax.all_gather(shards[3], ("slot", "seq"), axis=2, tiled=True),
        lax.all_gather(shards[4], ("slot", "seq"), axis=1, tiled=True),
        lax.all_gather(shards[5], ("slot", "seq"), axis=1, tiled=True),
        lax.all_gather(shards[6], ("slot", "seq"), axis=1, tiled=True),
        lax.all_gather(shards[7], ("slot", "seq"), axis=1, tiled=True),
        lax.all_gather(shards[8], ("slot", "seq"), axis=1, tiled=True),
        lax.all_gather(shards[9], ("slot", "seq"), axis=1, tiled=True),
        lax.all_gather(shards[10], ("slot", "seq"), axis=0, tiled=True),
        lax.all_gather(shards[11], ("slot", "seq"), axis=1, tiled=True),
        lax.all_gather(shards[12], ("slot", "seq"), axis=0, tiled=True),
    )


def segment_mask(segments, offset, block_rows):
    return segments[:, None, offset : offset + block_rows, None] == segments[:, None, None, :]


def scaled_scores(queries, key_rows, same_item):
    scores = jnp.einsum("sqhd,skhd->shqk", queries, key_rows, preferred_element_type=jnp.float32)
    return jnp.where(same_item, scores * HD ** (-0.5), masked_score)


def forward_block(stream, layer, segments):
    (
        gains,
        shifts,
        project,
        query_value,
        output,
        output_shift,
        expand,
        expand_shift,
        shrink,
        shrink_shift,
    ) = layer
    slot_count, row_count, model_width = stream.shape
    seq_parts = lax.axis_size("seq")
    head_width = model_width // seq_parts
    normed = plain_norm(stream, gains[0].astype(jnp.float32), shifts[0].astype(jnp.float32)).astype(
        jnp.bfloat16
    )
    bias_row = jnp.concatenate(
        [query_value[0], jnp.zeros_like(query_value[0]), query_value[1]]
    ).astype(jnp.float32)
    projected = (jnp.dot(normed, project, preferred_element_type=jnp.float32) + bias_row).astype(
        jnp.bfloat16
    )
    split_heads = lax.all_to_all(
        projected.reshape(slot_count, row_count, 3, seq_parts, head_width),
        "seq",
        split_axis=3,
        concat_axis=1,
        tiled=True,
    )
    length = split_heads.shape[1]
    local_heads = head_width // HD
    queries = split_heads[:, :, 0, 0].reshape(slot_count, length, local_heads, HD)
    key_rows = split_heads[:, :, 1, 0].reshape(slot_count, length, local_heads, HD)
    values = split_heads[:, :, 2, 0].reshape(slot_count, length, local_heads, HD)
    block_rows = min(512, length)
    pieces = []
    log_parts = []
    for offset in range(0, length, block_rows):
        scores = scaled_scores(
            queries[:, offset : offset + block_rows],
            key_rows,
            segment_mask(segments, offset, block_rows),
        )
        row_top = jnp.max(scores, axis=-1, keepdims=True)
        raised = jnp.exp(scores - row_top)
        row_total = jnp.sum(raised, axis=-1, keepdims=True)
        probability = (raised / row_total).astype(jnp.bfloat16)
        pieces.append(
            jnp.einsum(
                "shqk,skhd->sqhd", probability, values, preferred_element_type=jnp.float32
            ).astype(jnp.bfloat16)
        )
        log_parts.append(row_top + jnp.log(row_total))
    log_sums = jnp.concatenate(log_parts, axis=2)
    attended = jnp.concatenate(pieces, axis=1).reshape(slot_count, length, 1, head_width)
    mixed_rows = lax.all_to_all(attended, "seq", split_axis=1, concat_axis=2, tiled=True).reshape(
        slot_count, row_count, model_width
    )
    middle = (
        stream
        + jnp.dot(mixed_rows, output, preferred_element_type=jnp.float32)
        + output_shift.astype(jnp.float32)
    )
    normed_mid = plain_norm(
        middle, gains[1].astype(jnp.float32), shifts[1].astype(jnp.float32)
    ).astype(jnp.bfloat16)
    hidden = jnp.dot(normed_mid, expand, preferred_element_type=jnp.float32) + expand_shift.astype(
        jnp.float32
    )
    active = gelu_exact(hidden).astype(jnp.bfloat16)
    result = (
        middle
        + jnp.dot(active, shrink, preferred_element_type=jnp.float32)
        + shrink_shift.astype(jnp.float32)
    )
    saved_values = (
        normed,
        queries,
        key_rows,
        values,
        log_sums,
        mixed_rows,
        middle,
        normed_mid,
        hidden,
        active,
    )
    return (result, saved_values)


def backward_block(grad_out, stream, saved_values, layer, segments):
    (
        gains,
        shifts,
        project,
        query_value,
        output,
        output_shift,
        expand,
        expand_shift,
        shrink,
        shrink_shift,
    ) = layer
    normed, queries, key_rows, values, log_sums, mixed_rows, middle, normed_mid, hidden, active = (
        saved_values
    )
    slot_count, row_count, model_width = stream.shape
    seq_parts = lax.axis_size("seq")
    head_width = model_width // seq_parts
    branch = grad_out.astype(jnp.bfloat16)
    shrink_shift_grad = jnp.sum(branch, axis=(0, 1), dtype=jnp.float32)
    shrink_grad = jnp.einsum("stf,sto->fo", active, branch, preferred_element_type=jnp.float32)
    active_grad = jnp.einsum("sto,fo->stf", branch, shrink, preferred_element_type=jnp.float32)
    unused, gelu_back = jax.vjp(gelu_exact, hidden)
    hidden_low = gelu_back(active_grad)[0].astype(jnp.bfloat16)
    expand_shift_grad = jnp.sum(hidden_low, axis=(0, 1), dtype=jnp.float32)
    expand_grad = jnp.einsum(
        "sti,stf->if", normed_mid, hidden_low, preferred_element_type=jnp.float32
    )
    normed_mid_grad = jnp.einsum(
        "stf,if->sti", hidden_low, expand, preferred_element_type=jnp.float32
    )
    unused, norm_back = jax.vjp(
        plain_norm, middle, gains[1].astype(jnp.float32), shifts[1].astype(jnp.float32)
    )
    middle_part, gain_mid_grad, shift_mid_grad = norm_back(normed_mid_grad)
    middle_grad = grad_out + middle_part
    branch_low = middle_grad.astype(jnp.bfloat16)
    output_shift_grad = jnp.sum(branch_low, axis=(0, 1), dtype=jnp.float32)
    output_grad = jnp.einsum(
        "sti,sto->io", mixed_rows, branch_low, preferred_element_type=jnp.float32
    )
    mixed_low = jnp.einsum(
        "sto,io->sti", branch_low, output, preferred_element_type=jnp.float32
    ).astype(jnp.bfloat16)
    head_grad = lax.all_to_all(
        mixed_low.reshape(slot_count, row_count, seq_parts, head_width),
        "seq",
        split_axis=2,
        concat_axis=1,
        tiled=True,
    )
    length = head_grad.shape[1]
    local_heads = head_width // HD
    head_grad = head_grad.reshape(slot_count, length, local_heads, HD)
    scale_factor = HD ** (-0.5)
    block_rows = min(512, length)
    key_grad = jnp.zeros((slot_count, length, local_heads, HD), jnp.float32)
    value_grad = jnp.zeros((slot_count, length, local_heads, HD), jnp.float32)
    query_parts = []
    for offset in range(0, length, block_rows):
        query_block = queries[:, offset : offset + block_rows]
        scores = scaled_scores(query_block, key_rows, segment_mask(segments, offset, block_rows))
        probability = jnp.exp(scores - log_sums[:, :, offset : offset + block_rows])
        out_grad = head_grad[:, offset : offset + block_rows]
        value_grad = value_grad + jnp.einsum(
            "shqk,sqhd->skhd",
            probability.astype(jnp.bfloat16),
            out_grad,
            preferred_element_type=jnp.float32,
        )
        prob_grad = jnp.einsum(
            "sqhd,skhd->shqk", out_grad, values, preferred_element_type=jnp.float32
        )
        centre = jnp.sum(probability * prob_grad, axis=-1, keepdims=True)
        score_low = (probability * (prob_grad - centre)).astype(jnp.bfloat16)
        query_parts.append(
            jnp.einsum("shqk,skhd->sqhd", score_low, key_rows, preferred_element_type=jnp.float32)
            * scale_factor
        )
        key_grad = (
            key_grad
            + jnp.einsum(
                "shqk,sqhd->skhd", score_low, query_block, preferred_element_type=jnp.float32
            )
            * scale_factor
        )
    query_grad = jnp.concatenate(query_parts, axis=1)
    joined = (
        jnp.stack([query_grad, key_grad, value_grad], axis=2)
        .astype(jnp.bfloat16)
        .reshape(slot_count, length, 3, 1, head_width)
    )
    project_low = lax.all_to_all(joined, "seq", split_axis=1, concat_axis=3, tiled=True).reshape(
        slot_count, row_count, 3 * model_width
    )
    project_shift = jnp.sum(project_low, axis=(0, 1), dtype=jnp.float32)
    query_value_grad = jnp.stack([project_shift[:model_width], project_shift[2 * model_width :]])
    project_grad = jnp.einsum(
        "sti,stj->ij", normed, project_low, preferred_element_type=jnp.float32
    )
    normed_grad = jnp.einsum(
        "stj,ij->sti", project_low, project, preferred_element_type=jnp.float32
    )
    unused, norm_back = jax.vjp(
        plain_norm, stream, gains[0].astype(jnp.float32), shifts[0].astype(jnp.float32)
    )
    stream_part, gain_in_grad, shift_in_grad = norm_back(normed_grad)
    input_part = middle_grad + stream_part
    grads = (
        jnp.stack([gain_in_grad, gain_mid_grad]),
        jnp.stack([shift_in_grad, shift_mid_grad]),
        project_grad,
        query_value_grad,
        output_grad,
        output_shift_grad,
        expand_grad,
        expand_shift_grad,
        shrink_grad,
        shrink_shift_grad,
    )
    return (input_part, grads)


def plain_device(
    patches,
    segments,
    code_bits,
    norm_gain,
    norm_shift,
    project_weight,
    query_value_bias,
    output_weight,
    output_bias,
    expand_weight,
    expand_bias,
    shrink_weight,
    shrink_bias,
    encode_weight,
    decode_weight,
    decode_bias,
    cotangent,
):
    shards = (
        norm_gain,
        norm_shift,
        project_weight,
        query_value_bias,
        output_weight,
        output_bias,
        expand_weight,
        expand_bias,
        shrink_weight,
        shrink_bias,
        encode_weight,
        decode_weight,
        decode_bias,
    )
    gathered = gather_weights(shards)
    stream_in = patches.astype(jnp.float32)
    encoded, unused = forward_block(
        stream_in, tuple((array[0] for array in gathered[:10])), segments
    )
    encoded_low = encoded.astype(jnp.bfloat16)
    coded = jnp.einsum("sti,ic->stc", encoded_low, gathered[10], preferred_element_type=jnp.float32)
    signs = ((2 * code_bits - 1).astype(jnp.float32) * CODE ** (-0.5)).astype(jnp.bfloat16)
    start = jnp.einsum(
        "stc,ci->sti", signs, gathered[11], preferred_element_type=jnp.float32
    ) + gathered[12].astype(jnp.float32)
    decoded, decoder_saved = forward_block(
        start, tuple((array[1] for array in gathered[:10])), segments
    )
    weights_back = gather_weights(shards)
    encoder = tuple((array[0] for array in weights_back[:10]))
    decoder = tuple((array[1] for array in weights_back[:10]))
    start_grad, decoder_grads = backward_block(
        cotangent.astype(jnp.float32), start, decoder_saved, decoder, segments
    )
    start_low = start_grad.astype(jnp.bfloat16)
    decode_bias_grad = jnp.sum(start_low, axis=(0, 1), dtype=jnp.float32)
    decode_grad = jnp.einsum("stc,sti->ci", signs, start_low, preferred_element_type=jnp.float32)
    unit_grad = jnp.einsum(
        "sti,ci->stc", start_low, weights_back[11], preferred_element_type=jnp.float32
    )
    unit_rows, unit_back = jax.vjp(normalize, coded)
    coded_low = unit_back(unit_grad)[0].astype(jnp.bfloat16)
    encode_grad = jnp.einsum(
        "sti,stc->ic", encoded_low, coded_low, preferred_element_type=jnp.float32
    )
    encoded_grad = jnp.einsum(
        "stc,ic->sti", coded_low, weights_back[10], preferred_element_type=jnp.float32
    )
    unused, encoder_saved = forward_block(stream_in, encoder, segments)
    input_grad, encoder_grads = backward_block(
        encoded_grad, stream_in, encoder_saved, encoder, segments
    )
    pairs = tuple(
        (jnp.stack([first, second]) for first, second in zip(encoder_grads, decoder_grads))
    )
    totals = (
        lax.psum_scatter(pairs[0], ("slot", "seq"), scatter_dimension=2, tiled=True),
        lax.psum_scatter(pairs[1], ("slot", "seq"), scatter_dimension=2, tiled=True),
        lax.psum_scatter(pairs[2], ("slot", "seq"), scatter_dimension=1, tiled=True),
        lax.psum_scatter(pairs[3], ("slot", "seq"), scatter_dimension=2, tiled=True),
        lax.psum_scatter(pairs[4], ("slot", "seq"), scatter_dimension=1, tiled=True),
        lax.psum_scatter(pairs[5], ("slot", "seq"), scatter_dimension=1, tiled=True),
        lax.psum_scatter(pairs[6], ("slot", "seq"), scatter_dimension=1, tiled=True),
        lax.psum_scatter(pairs[7], ("slot", "seq"), scatter_dimension=1, tiled=True),
        lax.psum_scatter(pairs[8], ("slot", "seq"), scatter_dimension=1, tiled=True),
        lax.psum_scatter(pairs[9], ("slot", "seq"), scatter_dimension=1, tiled=True),
        lax.psum_scatter(encode_grad, ("slot", "seq"), scatter_dimension=0, tiled=True),
        lax.psum_scatter(decode_grad, ("slot", "seq"), scatter_dimension=1, tiled=True),
        lax.psum_scatter(decode_bias_grad, ("slot", "seq"), scatter_dimension=0, tiled=True),
    )
    return (decoded.astype(jnp.bfloat16), input_grad) + tuple(totals)


def solution(mesh):
    in_specs = (
        P("slot", "seq", None),
        P("slot", None),
        P("slot", "seq", None),
        P(None, None, ("slot", "seq")),
        P(None, None, ("slot", "seq")),
        P(None, ("slot", "seq"), None),
        P(None, None, ("slot", "seq")),
        P(None, ("slot", "seq"), None),
        P(None, ("slot", "seq")),
        P(None, ("slot", "seq"), None),
        P(None, ("slot", "seq")),
        P(None, ("slot", "seq"), None),
        P(None, ("slot", "seq")),
        P(("slot", "seq"), None),
        P(None, ("slot", "seq")),
        P(("slot", "seq")),
        P("slot", "seq", None),
    )
    out_specs = (
        P("slot", "seq", None),
        P("slot", "seq", None),
        P(None, None, ("slot", "seq")),
        P(None, None, ("slot", "seq")),
        P(None, ("slot", "seq"), None),
        P(None, None, ("slot", "seq")),
        P(None, ("slot", "seq"), None),
        P(None, ("slot", "seq")),
        P(None, ("slot", "seq"), None),
        P(None, ("slot", "seq")),
        P(None, ("slot", "seq"), None),
        P(None, ("slot", "seq")),
        P(("slot", "seq"), None),
        P(None, ("slot", "seq")),
        P(("slot", "seq")),
    )
    return jax.shard_map(
        on_device, mesh=mesh, in_specs=in_specs, out_specs=out_specs, check_vma=False
    )
```
